32 devices in a mesh: dp: 8 (over z, core), ctx: 4 (over y, x).
Axes of the slice: x: 2, y: 2, z: 4, core: 2. Of those that a mesh axis runs over, the one named last changes fastest.
Arguments:
- hidden_in: bfloat16 [8192, 2048], P(('dp', 'ctx')), may hold values from -6 to 6
- segments: int32 [8192], P('dp'), may hold values from 0 to 4, as said below
- routes: int32 [8192, 6], P(('dp', 'ctx')), may hold values from 0 to 15, all different within a row; in each aligned block of 256 rows (0 to 255, 256 to 511, ...) at most 192 rows name the same one
- gates: float32 [8192, 6], P(('dp', 'ctx')), may hold values from 0.25 to 0.75
- cotangent: bfloat16 [8192, 2048], P(('dp', 'ctx')), may hold values from -6 to 6
- norm_attn: bfloat16 [2048], P(('dp', 'ctx')), may hold values from 0.25 to 1.75
- w_query: bfloat16 [2048, 3072], P(('dp', 'ctx')), may hold values from -0.125 to 0.125
- w_kv_down: bfloat16 [2048, 576], P(('dp', 'ctx')), may hold values from -0.125 to 0.125
- norm_latent: bfloat16 [512], P(('dp', 'ctx')), may hold values from 0.25 to 1.75
- w_kv_up: bfloat16 [512, 4096], P(('dp', 'ctx')), may hold values from -0.25 to 0.25
- w_out: bfloat16 [2048, 2048], P(('dp', 'ctx')), may hold values from -0.75 to 0.75
- norm_ffn: bfloat16 [2048], P(('dp', 'ctx')), may hold values from 0.25 to 1.75
- w_shared_in: bfloat16 [2048, 5632], P(('dp', 'ctx')), may hold values from -0.125 to 0.125
- w_shared_out: bfloat16 [2816, 2048], P(('dp', 'ctx')), may hold values from -0.109375 to 0.109375
- w_expert_in: bfloat16 [32, 2048, 1408], P(('dp', 'ctx')), may hold values from -0.125 to 0.125
- w_expert_out: bfloat16 [32, 704, 2048], P(('dp', 'ctx')), may hold values from -0.15625 to 0.15625
Outputs:
- mixed: bfloat16 [8192, 2048], P(('dp', 'ctx'))
- grad_in: float32 [8192, 2048], P(('dp', 'ctx'))
- grad_norm_attn: float32 [2048], P(('dp', 'ctx'))
- grad_w_query: float32 [2048, 3072], P(('dp', 'ctx'))
- grad_w_kv_down: float32 [2048, 576], P(('dp', 'ctx'))
- grad_norm_latent: float32 [512], P(('dp', 'ctx'))
- grad_w_kv_up: float32 [512, 4096], P(('dp', 'ctx'))
- grad_w_out: float32 [2048, 2048], P(('dp', 'ctx'))
- grad_norm_ffn: float32 [2048], P(('dp', 'ctx'))
- grad_w_shared_in: float32 [2048, 5632], P(('dp', 'ctx'))
- grad_w_shared_out: float32 [2816, 2048], P(('dp', 'ctx'))
- grad_w_expert_in: float32 [32, 2048, 1408], P(('dp', 'ctx'))
- grad_w_expert_out: float32 [32, 704, 2048], P(('dp', 'ctx'))
The draws below stay inside these ranges and needn't reach their ends.
Inputs may be any that keep to these rules, and one draw needn't show every extreme that they name: `routes`: in each aligned block of 256 rows (the rows of one device) no expert is named by more than 192 rows. `segments`: segment numbers never fall along a packed row of 1024 tokens; in every row one document begins within the first 256 positions and ends within the last 256.
All inputs are finite; a program needn't handle non-finite values.
Results may differ from the reference program's by a relative error of at most 0.018.
Values may be sent and summed in bfloat16 or wider, within the bound.
No kernel may reach another device: no remote copies, remote signals or barrier semaphores. Data moves between devices by JAX's collectives and lax.ppermute only.
A program may use at most 576 MiB of HBM per device.

```python
import math
from functools import partial
import jax
import jax.numpy as jnp
import numpy as np
from jax import lax

D = 2048
HEADS = 16
NOPE = 128
ROPE = 64
VDIM = 128
LATENT = 512
EXPERT_FF = 1408
SHARED_FF = 2816
TOP = 6
EXPERTS = 16
LEN = 1024
TOK_DEV = 256
TOKENS = 8192
CAP = 192
N_DP = 8
DEVICES = 32


def draw_segments(key, part):
    key = jax.random.fold_in(key, 11)
    row_count = TOKENS // LEN
    subkeys = jax.random.split(key, 4)
    long_start = jax.random.randint(subkeys[0], (row_count,), 1, TOK_DEV)
    first_cut = jax.random.randint(subkeys[1], (row_count,), 0, long_start)
    long_end = jax.random.randint(subkeys[2], (row_count,), LEN - TOK_DEV + 1, LEN)
    last_cut = jax.random.randint(subkeys[3], (row_count,), long_end + 1, LEN + 1)
    positions = jnp.arange(LEN, dtype=jnp.int32)[None, :]
    number = (positions >= first_cut[:, None]).astype(jnp.int32)
    number = number + (positions >= long_start[:, None]).astype(jnp.int32)
    number = number + (positions >= long_end[:, None]).astype(jnp.int32)
    number = number + (positions >= last_cut[:, None]).astype(jnp.int32)
    return number.reshape(-1)


def shard_levels(rng, shape, pieces, low, top_value):
    def one(position, shards_of):
        steps = jax.random.uniform(jax.random.fold_in(jax.random.fold_in(rng, 6), position), (shards_of,), jnp.float32, low / len(pieces), top_value / len(pieces))
        return jnp.repeat(jnp.exp(steps), shape[position] // shards_of).reshape((-1,) + (1,) * (len(shape) - position - 1))

    level = one(*pieces[0])
    for cut in pieces[1:]:
        level = level * one(*cut)
    return level


def deal_out(stream_key, own, number, rows, count, top, bound, skew):
    sequence = jax.random.permutation(stream_key, count)
    crowded, usual = shares(count, rows * top, bound, skew, True), shares(count, rows * top, bound, skew, False)
    places = jnp.arange(count)

    def named(lengths, offset_by):
        used = int((lengths > 0).sum())
        fixed = max(1, used // 4)
        passed = fixed + (places - fixed + offset_by * (used - fixed)) % max(1, count - fixed)
        return jnp.zeros((count,), jnp.int32).at[sequence[jnp.where(places < fixed, places, passed)]].set(jnp.asarray(lengths, jnp.int32))

    lengths = jnp.where(number % 4 == 0, named(crowded, number // 4), named(usual, number - number // 4 - 1))
    mixed = jax.random.permutation(jax.random.fold_in(own, 3), count)
    donor, receiver = mixed[0:count // 2 * 2:2], mixed[1:count // 2 * 2:2]
    slack = jnp.minimum(lengths[donor] - 1, bound - lengths[receiver]) // 2
    slack = jnp.where((donor == sequence[0]) | (receiver == sequence[0]) | (lengths[receiver] == 0), 0, jnp.maximum(slack, 0))
    passed = jax.random.randint(jax.random.fold_in(own, 4), (count // 2,), 0, 1 << 20) % (slack + 1)
    lengths = lengths.at[donor].add(-passed).at[receiver].add(passed)
    labels = jnp.searchsorted(jnp.cumsum(lengths), jnp.arange(rows * top), side="right").astype(jnp.int32)
    grid = labels.reshape(top, rows).T
    grid = grid[jax.random.permutation(jax.random.fold_in(own, 1), rows)]
    offset_by = jax.random.randint(jax.random.fold_in(own, 2), (rows, 1), 0, top)
    return jnp.take_along_axis(grid, (jnp.arange(top)[None, :] + offset_by) % top, axis=1)


def shares(amount, total, most, slope, full):
    weights = [(1 << 20) // math.isqrt(standing ** slope) + 1 for standing in range(1, amount + 1)]
    largest = most if full else min(most, max(-(-total // amount), total * weights[0] // sum(weights)))
    least = 1 if total - largest >= amount - 1 else 0
    counts, surplus = [largest] + [least] * (amount - 1), total - largest - least * (amount - 1)
    while surplus > 0:
        movable = [i for i in range(1, amount) if counts[i] < largest] or [i for i in range(1, amount) if counts[i] < most]
        mass, left = sum([weights[i] for i in movable]), surplus
        for i in movable:
            more = min(most - counts[i], max(1, left * weights[i] // mass), surplus)
            counts[i] = counts[i] + more
            surplus = surplus - more
    return np.array(counts)


def bell_draw(stream_key, extent, width, reach, cuts=(), held_as=jnp.bfloat16):
    values = jax.random.normal(stream_key, extent, jnp.float32) * width
    if len(cuts) > 0:
        values = shard_levels(stream_key, extent, cuts, -0.22, 0.18) * values
    return jnp.clip(values, min=-reach, max=reach).astype(held_as)


def setup_inputs(seed: int = 0) -> dict:
    streams_of = jax.random.split(jax.random.key(seed), 17)
    hidden_in = bell_draw(streams_of[0], (TOKENS, D), 1.0, 6.0, ((0, 32),))
    segments = draw_segments(jax.random.fold_in(streams_of[16], 71), 0)
    routes_keys = jax.random.split(jax.random.fold_in(streams_of[2], 1), TOKENS // TOK_DEV)
    routes_turns = jax.random.permutation(jax.random.fold_in(streams_of[2], 3), TOKENS // TOK_DEV)
    routes = jax.vmap(lambda own, number: deal_out(jax.random.fold_in(streams_of[2], 2), own, number, TOK_DEV, EXPERTS, TOP, CAP, 1))(routes_keys, routes_turns).reshape((TOKENS, TOP))
    gates = jnp.clip(0.25 + 0.5 * jax.random.uniform(streams_of[3], (TOKENS, TOP), jnp.float32) ** shard_levels(streams_of[3], (TOKENS, TOP), ((0, 32),), -0.2, 0.2), 0.25, 0.75)
    cotangent = bell_draw(streams_of[4], (TOKENS, D), 1.0, 6.0, ((0, 32),))
    norm_attn = jnp.clip(1.0 + 0.15 * jax.random.normal(streams_of[5], (D,), jnp.float32), 0.25, 1.75).astype(jnp.bfloat16)
    w_query = bell_draw(streams_of[6], (D, HEADS * (NOPE + ROPE)), D ** -0.5, 0.125, ((0, 32),))
    w_kv_down = bell_draw(streams_of[7], (D, LATENT + ROPE), D ** -0.5, 0.125, ((0, 32),))
    norm_latent = jnp.clip(1.0 + 0.15 * jax.random.normal(streams_of[8], (LATENT,), jnp.float32), 0.25, 1.75).astype(jnp.bfloat16)
    w_kv_up = bell_draw(streams_of[9], (LATENT, HEADS * (NOPE + VDIM)), LATENT ** -0.5, 0.25, ((0, 32),))
    w_out = bell_draw(streams_of[10], (HEADS * VDIM, D), (HEADS * VDIM * 32 // LEN) ** -0.5, 0.75, ((0, 32),))
    norm_ffn = jnp.clip(1.0 + 0.15 * jax.random.normal(streams_of[11], (D,), jnp.float32), 0.25, 1.75).astype(jnp.bfloat16)
    w_shared_in = bell_draw(streams_of[12], (D, 2 * SHARED_FF), D ** -0.5, 0.125, ((0, 32),))
    w_shared_out = bell_draw(streams_of[13], (SHARED_FF, D), SHARED_FF ** -0.5, 0.109375, ((0, 32),))
    w_expert_in = bell_draw(streams_of[14], (DEVICES, D, EXPERT_FF), D ** -0.5, 0.125, ((0, 32),))
    w_expert_out = bell_draw(streams_of[15], (DEVICES, EXPERT_FF // 2, D), EXPERT_FF ** -0.5, 0.15625, ((0, 32),))
    return {"hidden_in": hidden_in, "segments": segments, "routes": routes, "gates": gates, "cotangent": cotangent, "norm_attn": norm_attn, "w_query": w_query, "w_kv_down": w_kv_down, "norm_latent": norm_latent, "w_kv_up": w_kv_up, "w_out": w_out, "norm_ffn": norm_ffn, "w_shared_in": w_shared_in, "w_shared_out": w_shared_out, "w_expert_in": w_expert_in, "w_expert_out": w_expert_out}


epsilon = 1e-06

@jax.custom_vjp
def low(v):
    return lax.optimization_barrier(v.astype(jnp.bfloat16)).astype(jnp.float32)

@jax.custom_vjp
def low_back(v):
    return v

def low_keep(v):
    return (low(v), None)

def low_pass(kept, grad):
    return (grad,)

def back_keep(v):
    return (v, None)

def back_low(kept, grad):
    return (low(grad),)
low.defvjp(low_keep, low_pass)
low_back.defvjp(back_keep, back_low)

def product(left, right):
    return jnp.dot(left, right, precision=lax.Precision.HIGHEST, preferred_element_type=jnp.float32)

def rms_scale(operand, gain_vec):
    inverse = lax.rsqrt(lax.optimization_barrier(jnp.mean(operand * operand, axis=-1, keepdims=True)) + epsilon)
    return operand * inverse * gain_vec

def rope_tables(positions, rope_width):
    half_width = rope_width // 2
    frequency = jnp.exp(-math.log(10000.0) * jnp.arange(half_width).astype(jnp.float32) / half_width)
    angles = positions.astype(jnp.float32)[:, None] * frequency[None, :]
    return (jnp.cos(angles), jnp.sin(angles))

def rotate(operand, cosine, sine_part):
    half_width = operand.shape[-1] // 2
    first_half = operand[..., :half_width]
    second_half = operand[..., half_width:]
    return jnp.concatenate([first_half * cosine - second_half * sine_part, second_half * cosine + first_half * sine_part], axis=-1)

def swish(operand):
    return operand * jax.nn.sigmoid(operand)

def layer_row(params, row_item):
    row_input, row_segments, row_routes, row_gates = row_item
    norm_attn, w_query, w_kv_down, norm_latent, w_kv_up, w_out, norm_ffn, w_shared_in, w_shared_out, w_expert_in, w_expert_out = params
    highest = lax.Precision.HIGHEST
    scale = 1.0 / math.sqrt(NOPE + ROPE)
    half_ff = EXPERT_FF // 2
    positions = jnp.arange(LEN).astype(jnp.int32)
    cosine, sine_part = rope_tables(positions, ROPE)
    normed = low(rms_scale(row_input, norm_attn))
    query_raw = low_back(product(normed, w_query)).reshape(LEN, HEADS, NOPE + ROPE)
    query_nope = low(query_raw[..., :NOPE])
    query_rope = low(rotate(query_raw[..., NOPE:], cosine[:, None, :], sine_part[:, None, :]))
    compressed = low_back(product(normed, w_kv_down))
    latent = low(rms_scale(compressed[:, :LATENT], norm_latent))
    key_rope = low(rotate(compressed[:, LATENT:], cosine, sine_part))
    keyval = low(low_back(product(latent, w_kv_up))).reshape(LEN, HEADS, NOPE + VDIM)
    raw_scores = jnp.einsum('qhd,khd->hqk', query_nope, keyval[..., :NOPE], precision=highest)
    raw_scores = low_back(raw_scores + jnp.einsum('qhd,kd->hqk', query_rope, key_rope, precision=highest))
    allowed = (positions[None, :] <= positions[:, None]) & (row_segments[None, :] == row_segments[:, None])
    scores = jnp.where(allowed[None], raw_scores * scale, -1e+30)
    row_max = lax.optimization_barrier(jnp.max(scores, axis=-1, keepdims=True))
    exponent = jnp.exp(scores - row_max)
    probs = low(exponent / lax.optimization_barrier(jnp.sum(exponent, axis=-1, keepdims=True)))
    heads_out = low(low_back(jnp.einsum('hqk,khd->qhd', probs, keyval[..., NOPE:], precision=highest)))
    heads_out = heads_out.reshape(LEN, HEADS * VDIM)
    middle = row_input + low_back(product(heads_out, w_out))
    ffn_in = low(rms_scale(middle, norm_ffn))
    shared_pre = low_back(product(ffn_in, w_shared_in))
    shared_act = low(swish(shared_pre[:, :SHARED_FF]) * shared_pre[:, SHARED_FF:])
    shared_out = low_back(product(shared_act, w_shared_out))
    pairs_in = w_expert_in.reshape(EXPERTS, 2, D, EXPERT_FF)
    pairs_out = w_expert_out.reshape(EXPERTS, 2, half_ff, D)

    def one_expert(carried, expert_item):
        pair_in, pair_out, expert_index = expert_item
        weights = lax.optimization_barrier(jnp.sum(jnp.where(row_routes == expert_index, row_gates, 0.0), axis=-1))
        summed = jnp.zeros((LEN, D), jnp.float32)
        for half_index in range(2):
            source = low_back(ffn_in)
            pre_act = low_back(product(source, pair_in[half_index]))
            hidden = low(swish(pre_act[:, :half_ff]) * pre_act[:, half_ff:])
            summed = summed + low(product(hidden, pair_out[half_index]))
        return (carried + weights[:, None] * low_back(summed), None)
    routed, unused = lax.scan(jax.checkpoint(one_expert), jnp.zeros((LEN, D), jnp.float32), (pairs_in, pairs_out, jnp.arange(EXPERTS).astype(jnp.int32)))
    return middle + shared_out + routed

def reference(hidden_in, segments, routes, gates, cotangent, norm_attn, w_query, w_kv_down, norm_latent, w_kv_up, w_out, norm_ffn, w_shared_in, w_shared_out, w_expert_in, w_expert_out):
    params = (norm_attn.astype(jnp.float32), w_query.astype(jnp.float32), w_kv_down.astype(jnp.float32), norm_latent.astype(jnp.float32), w_kv_up.astype(jnp.float32), w_out.astype(jnp.float32), norm_ffn.astype(jnp.float32), w_shared_in.astype(jnp.float32), w_shared_out.astype(jnp.float32), w_expert_in.astype(jnp.float32), w_expert_out.astype(jnp.float32))
    row_inputs = hidden_in.astype(jnp.float32).reshape(N_DP, LEN, D)
    row_segments = segments.reshape(N_DP, LEN)
    row_routes = routes.reshape(N_DP, LEN, TOP)
    row_gates = gates.astype(jnp.float32).reshape(N_DP, LEN, TOP)

    def forward(inputs_all, weights_all):
        checkpointed = jax.checkpoint(partial(layer_row, weights_all))

        def row_step(carried, row_item):
            return (carried, checkpointed(row_item))
        unused, outputs = lax.scan(row_step, jnp.zeros((), jnp.float32), (inputs_all, row_segments, row_routes, row_gates))
        return outputs
    outputs, pull_back = jax.vjp(forward, row_inputs, params)
    grad_inputs, grad_params = pull_back(cotangent.astype(jnp.float32).reshape(N_DP, LEN, D))
    mixed = outputs.reshape(TOKENS, D).astype(jnp.bfloat16)
    return (mixed, grad_inputs.reshape(TOKENS, D), grad_params[0], grad_params[1], grad_params[2], grad_params[3], grad_params[4], grad_params[5], grad_params[6], grad_params[7], grad_params[8], grad_params[9], grad_params[10])
```

```python
import math

import jax
import jax.numpy as jnp
from jax import lax
from jax.experimental import pallas as pl
from jax.experimental.pallas import tpu as pltpu
from jax.sharding import PartitionSpec as P

D = 2048
HEADS = 16
NOPE = 128
ROPE = 64
VDIM = 128
LATENT = 512
EXPERT_FF = 1408
SHARED_FF = 2816
TOP = 6

BOTH = ("dp", "ctx")
epsilon = 1e-06
f32 = jnp.float32
bf16 = jnp.bfloat16


def matmul(left, right):
    return jnp.dot(left, right, preferred_element_type=f32)


def matmul_left_t(left, right):
    return lax.dot_general(left, right, (((0,), (0,)), ((), ())), preferred_element_type=f32)


def matmul_right_t(left, right):
    return lax.dot_general(left, right, (((1,), (1,)), ((), ())), preferred_element_type=f32)


def rope_tables(positions, rope_width):
    half_width = rope_width // 2
    frequency = jnp.exp(
        -math.log(10000.0) * jnp.arange(half_width).astype(f32) / half_width
    )
    angles = positions.astype(f32)[:, None] * frequency[None, :]
    return (jnp.cos(angles), jnp.sin(angles))


def rotate(operand, cosine, sine_part):
    half_width = operand.shape[-1] // 2
    first_half = operand[..., :half_width]
    second_half = operand[..., half_width:]
    return jnp.concatenate(
        [
            first_half * cosine - second_half * sine_part,
            second_half * cosine + first_half * sine_part,
        ],
        axis=-1,
    )


def unrotate(operand, cosine, sine_part):
    return rotate(operand, cosine, -sine_part)


def swish(operand):
    return operand * jax.nn.sigmoid(operand)


def swish_slope(operand):
    sigma = jax.nn.sigmoid(operand)
    return sigma * (1.0 + operand * (1.0 - sigma))


def rms_inverse(operand):
    return lax.rsqrt(jnp.mean(operand * operand, axis=-1, keepdims=True) + epsilon)


def rms_backward(operand, inverse, gain_vec, grad_out):
    scaled = grad_out * gain_vec
    grad_gain = jnp.sum(grad_out * operand * inverse, axis=0)
    grad_operand = inverse * scaled - operand * inverse * inverse * inverse * jnp.mean(
        scaled * operand, axis=-1, keepdims=True
    )
    return (grad_operand, grad_gain)


class Links:
    def __init__(self):
        self.dp = lax.axis_size("dp")
        self.ctx = lax.axis_size("ctx")
        self.size = {"z": self.dp // 2, "c": 2, "y": self.ctx // 2, "x": 2}
        dp, ctx = lax.axis_index("dp"), lax.axis_index("ctx")
        self.own = {"z": dp // 2, "c": dp % 2, "y": ctx // 2, "x": ctx % 2}

    def shift(self, value, axis, by):
        if axis in "zc":
            name, count = "dp", self.dp
        else:
            name, count = "ctx", self.ctx
        if axis in "zy":
            pairs = [(i, (i + 2 * by) % count) for i in range(count)]
        else:
            pairs = [(i, i ^ 1) for i in range(count)]
        return lax.ppermute(value, name, pairs)

    def shift_ctx(self, value, ky, kx):
        pairs = [
            (i, ((i // 2 - ky) % (self.ctx // 2)) * 2 + (i + kx) % 2) for i in range(self.ctx)
        ]
        return lax.ppermute(value, "ctx", pairs)

    def ring(self, block, axis):
        held = [block]
        for _ in range(self.size[axis] - 1):
            held.append(self.shift(held[-1], axis, 1))
        return held

    def gather(self, block, order):
        for axis in order:
            block = jnp.concatenate(self.ring(block, axis), axis=0)
        return block

    def reduce(self, parts, axis):
        total = parts[-1]
        for part in parts[-2::-1]:
            moved = self.shift(total, axis, -1)
            total = (moved.astype(f32) + part.astype(f32)).astype(bf16)
        return total

    def scatter_sum(self, block, order):
        for axis in order[::-1]:
            count = self.size[axis]
            rows = block.shape[0] // count
            block = self.reduce([block[k * rows : (k + 1) * rows] for k in range(count)], axis)
        return block

    def device_of(self, order):
        place = dict(self.own)
        depth = len(order)
        for i, axis in enumerate(order):
            shape = [1] * depth
            shape[depth - 1 - i] = self.size[axis]
            offsets = jnp.arange(self.size[axis], dtype=jnp.int32).reshape(shape)
            place[axis] = (self.own[axis] - offsets) % self.size[axis]
        number = ((place["z"] * 2 + place["c"]) * self.size["y"] + place["y"]) * 2 + place["x"]
        return number.reshape(-1)

    def place_of(self, order):
        count = self.dp * self.ctx
        number = jnp.arange(count, dtype=jnp.int32)
        coordinate = {
            "x": number % 2,
            "y": (number // 2) % self.size["y"],
            "c": (number // self.ctx) % 2,
            "z": number // (2 * self.ctx),
        }
        place = jnp.zeros_like(number)
        for axis in order[::-1]:
            steps = (self.own[axis] - coordinate[axis]) % self.size[axis]
            place = place * self.size[axis] + steps
        return place

    def ctx_relative(self):
        y = (self.own["y"] - jnp.arange(self.size["y"], dtype=jnp.int32)) % self.size["y"]
        x = (self.own["x"] - jnp.arange(2, dtype=jnp.int32)) % 2
        return (y[:, None] * 2 + x[None, :]).reshape(-1)

    def ctx_exchange(self, pieces):
        ny = self.size["y"]
        result = [pieces[0]] + [None] * (self.ctx - 1)
        for k in range(1, self.ctx):
            ky, kx = k // 2, k % 2
            result[((-ky) % ny) * 2 + kx] = self.shift_ctx(pieces[k], ky, kx)
        return result

    def ctx_gather(self, block):
        half = block.shape[0] // 2
        ny = self.size["y"]
        first = self.ring(block[:half], "x")
        first = self.ring(jnp.concatenate(first, axis=0), "y")
        second = self.ring(block[half:], "y")
        second = self.ring(jnp.concatenate(second, axis=0), "x")
        pieces = []
        for ky in range(ny):
            for kx in range(2):
                pieces.append(first[ky][kx * half : (kx + 1) * half])
                pieces.append(second[kx][ky * half : (ky + 1) * half])
        return jnp.concatenate(pieces, axis=0)


def after(value, *others):
    return lax.optimization_barrier((value,) + others)[0]


GROUP = 4


def ffn_kernel(half_ff, adds, devices_ref, x_ref, *refs):
    g_refs, (m_ref, w_in, w_out) = refs[:GROUP], refs[GROUP : GROUP + 3]
    refs = refs[GROUP + 3 :]
    if adds:
        add_out, add_grad = refs[:2]
    x_all, g_all, act, grad_pre, out, row_grad = refs[-6:]
    half_all = act.shape[1]
    count = x_ref.shape[0] // GROUP
    x_all[...] = x_ref[...]
    for i, g_ref in enumerate(g_refs):
        g_all[i * count : (i + 1) * count] = g_ref[0]
    pre = matmul(x_ref[...], w_in[...])
    gate, up = pre[:, :half_all], pre[:, half_all:]
    column = lax.broadcasted_iota(jnp.int32, (1, half_all), 1)
    weight = jnp.where(column < half_ff, m_ref[...], 1.0)
    sigma = jax.nn.sigmoid(gate)
    swished = gate * sigma
    act[...] = (swished * up * weight).astype(bf16)
    grad_act = matmul_right_t(g_all[...], w_out[...]) * weight
    slope = sigma * (1.0 + gate * (1.0 - sigma))
    grad_pre[:, :half_all] = (grad_act * up * slope).astype(bf16)
    grad_pre[:, half_all:] = (grad_act * swished).astype(bf16)
    out_part = matmul(act[...], w_out[...])
    grad_part = matmul_right_t(grad_pre[...], w_in[...])
    if adds:
        out_part = out_part + add_out[...].astype(f32)
        grad_part = grad_part + add_grad[...].astype(f32)
    out[...] = out_part.astype(bf16)
    row_grad[...] = grad_part.astype(bf16)


def ffn_chunk(x, g_blocks, m, w_in, w_out, half_ff, source, place, kept, start, tokens, adds):
    half_all = w_out.shape[0]
    count = x.shape[0] // source.shape[0]
    tile = GROUP * count
    steps = x.shape[0] // tile
    base = start // tile

    def rows(width, first=0):
        return pl.BlockSpec((tile, width), lambda i, _: (first + i, 0))

    def whole(value):
        return pl.BlockSpec(value.shape, lambda i, _: (0, 0), pipeline_mode=pl.Buffered(1))

    def g_spec(j):
        return pl.BlockSpec((1, count, D), lambda i, s: (s[GROUP * i + j], place, 0))

    operands = [source, x] + [g_blocks] * GROUP + [m, w_in, w_out]
    in_specs = [rows(D)] + [g_spec(j) for j in range(GROUP)]
    in_specs += [rows(1), whole(w_in), whole(w_out)]
    if adds is not None:
        operands += adds
        in_specs += [rows(D)] * 2
    aliases = {}
    if kept is not None:
        aliases = {len(operands) + i: i for i in range(4)}
        operands += kept
        in_specs += [pl.BlockSpec(memory_space=pl.ANY)] * 4
    widths = (D, D, half_all, 2 * half_all)
    out_shape = [jax.ShapeDtypeStruct((tokens, w), bf16) for w in widths]
    out_shape += [jax.ShapeDtypeStruct(x.shape, bf16)] * 2
    flops = 2 * x.shape[0] * D * 6 * half_all
    result = pl.pallas_call(
        lambda *refs: ffn_kernel(half_ff, adds is not None, *refs),
        grid_spec=pltpu.PrefetchScalarGridSpec(
            num_scalar_prefetch=1,
            grid=(steps,),
            in_specs=in_specs,
            out_specs=[rows(w, base) for w in widths] + [rows(D)] * 2,
        ),
        out_shape=out_shape,
        input_output_aliases=aliases,
        compiler_params=pltpu.CompilerParams(vmem_limit_bytes=60 * 2**20),
        cost_estimate=pl.CostEstimate(
            flops=flops, bytes_accessed=x.shape[0] * D * 16, transcendentals=0
        ),
        name="ffn_chunk",
    )(*operands)
    return result[:4], result[4], result[5]


def shards(
    hidden_in,
    segments,
    routes,
    gates,
    cotangent,
    norm_attn,
    w_query,
    w_kv_down,
    norm_latent,
    w_kv_up,
    w_out,
    norm_ffn,
    w_shared_in,
    w_shared_out,
    w_expert_in,
    w_expert_out,
):
    links = Links()
    tok = hidden_in.shape[0]
    row = segments.shape[0]
    ctx = links.ctx
    devices = links.dp * ctx
    me = lax.axis_index("dp") * ctx + lax.axis_index("ctx")
    half_ff = EXPERT_FF // 2
    half_sh = w_shared_out.shape[0]
    half_all = -(-(half_ff + half_sh) // 128) * 128
    heads = HEADS // ctx
    q_cols = heads * (NOPE + ROPE)
    v_cols = heads * VDIM
    kv_cols = heads * (NOPE + VDIM)
    dn_cols = (LATENT + ROPE) // ctx
    rows_d = w_query.shape[0]
    rows_l = w_kv_up.shape[0]
    up_fold = rows_l * kv_cols // rows_d
    up_parts = rows_d // rows_l
    scale = 1.0 / math.sqrt(NOPE + ROPE)
    rel_ctx = links.ctx_relative()
    ctx_number = jnp.arange(ctx, dtype=jnp.int32)
    ctx_place = ((links.own["y"] - ctx_number // 2) % links.size["y"]) * 2 + (
        links.own["x"] - ctx_number
    ) % 2

    def columns(value, k, width):
        return lax.dynamic_slice_in_dim(value, rel_ctx[k] * width, width, 1)

    hidden_row = links.ctx_gather(hidden_in)
    latent_gain = jnp.zeros((rows_d,), bf16).at[:rows_l].set(norm_latent)
    small = jnp.concatenate(
        [w_kv_down, norm_attn[:, None], norm_ffn[:, None], latent_gain[:, None]], axis=1
    )
    small = jnp.pad(small, ((0, 0), (0, -small.shape[1] % 128)))
    small_order = ("z", "x", "y", "c")
    small_all = links.gather(small, small_order).reshape(devices, rows_d, small.shape[1])
    small_all = small_all[links.place_of(small_order)]
    down_w = small_all[:, :, : LATENT + ROPE].reshape(D, LATENT + ROPE)
    gain_attn = small_all[:, :, LATENT + ROPE].reshape(D).astype(f32)
    gain_ffn = small_all[:, :, LATENT + ROPE + 1].reshape(D).astype(f32)
    gain_latent = small_all[:, :rows_l, LATENT + ROPE + 2].reshape(LATENT).astype(f32)

    pieces = []
    for k in range(ctx):
        folded = columns(w_kv_up, k, kv_cols).reshape(rows_l, up_parts, up_fold)
        folded = folded.transpose(1, 0, 2).reshape(rows_d, up_fold)
        pieces.append(jnp.concatenate([columns(w_query, k, q_cols), folded], axis=1))
    heads_w = jnp.concatenate(links.ctx_exchange(pieces), axis=0)
    heads_w = links.gather(heads_w, ("z", "c")).reshape(devices, rows_d, q_cols + up_fold)
    heads_place = links.place_of(("x", "y", "z", "c"))
    heads_w = heads_w[heads_place]
    query_w = heads_w[:, :, :q_cols].reshape(D, q_cols)
    up_w = heads_w[:, :, q_cols:].reshape(devices, up_parts, rows_l, up_fold)
    up_w = up_w.transpose(0, 2, 1, 3).reshape(LATENT, kv_cols)

    experts = devices // 2
    expert_number = jnp.arange(experts, dtype=jnp.int32)[:, None, None]
    gate_matrix = jnp.sum(
        jnp.where(routes.T[None] == expert_number, gates.T[None], 0.0), axis=1
    )
    m_all = lax.all_to_all(
        jnp.repeat(gate_matrix, 2, axis=0), BOTH, split_axis=0, concat_axis=0, tiled=True
    )
    out_w = lax.all_gather(after(w_out, heads_w, hidden_row), BOTH, axis=0, tiled=True)
    g_all = lax.all_gather(after(cotangent, out_w), BOTH, axis=0, tiled=True)
    g_blocks = g_all.reshape(devices, tok, D)

    inputs_row = hidden_row.astype(f32)
    inverse_row = rms_inverse(inputs_row)
    normed_row = (inputs_row * inverse_row * gain_attn).astype(bf16)
    positions = (rel_ctx[:, None] * tok + jnp.arange(tok, dtype=jnp.int32)[None, :]).reshape(-1)
    row_segments = segments.reshape(ctx, tok)[rel_ctx].reshape(-1)
    allowed = (positions[None, :] <= positions[:, None]) & (
        row_segments[None, :] == row_segments[:, None]
    )
    cosine, sine_part = rope_tables(positions, ROPE)
    query_raw = matmul(normed_row, query_w).reshape(row, heads, NOPE + ROPE)
    query = jnp.concatenate(
        [
            query_raw[..., :NOPE],
            rotate(query_raw[..., NOPE:], cosine[:, None, :], sine_part[:, None, :]),
        ],
        axis=-1,
    ).astype(bf16)
    query = query.transpose(1, 0, 2)
    compressed = matmul(normed_row, down_w)
    raw_latent = compressed[:, :LATENT]
    inverse_latent = rms_inverse(raw_latent)
    latent = (raw_latent * inverse_latent * gain_latent).astype(bf16)
    key_rope = rotate(compressed[:, LATENT:], cosine, sine_part).astype(bf16)
    keyval = matmul(latent, up_w).astype(bf16).reshape(row, heads, NOPE + VDIM)
    keyval = keyval.transpose(1, 0, 2)
    key = jnp.concatenate(
        [keyval[..., :NOPE], jnp.broadcast_to(key_rope[None], (heads, row, ROPE))], axis=-1
    )
    value = keyval[..., NOPE:]

    def masked_scores():
        raw = jnp.einsum("hqd,hkd->hqk", query, key, preferred_element_type=f32)
        return jnp.where(allowed[None], raw * scale, -1e30)

    scores = masked_scores()
    row_max = jnp.max(scores, axis=-1, keepdims=True)
    exponent = jnp.exp(scores - row_max)
    row_total = jnp.sum(exponent, axis=-1, keepdims=True)
    log_total = row_max + jnp.log(row_total)
    probs = (exponent / row_total).astype(bf16)
    heads_part = jnp.einsum("hqk,hkd->qhd", probs, value, preferred_element_type=f32)
    heads_part = heads_part.astype(bf16).reshape(ctx, tok, v_cols)
    returned = jnp.stack(links.ctx_exchange([heads_part[k] for k in range(ctx)]))
    heads_out = returned[ctx_place].transpose(1, 0, 2).reshape(tok, HEADS * VDIM)
    inputs = hidden_in.astype(f32)
    middle = inputs + matmul(heads_out, out_w)
    inverse_ffn = rms_inverse(middle)
    ffn_in = (middle * inverse_ffn * gain_ffn).astype(bf16)

    shared_pieces = jnp.concatenate(
        [
            w_shared_in[:, :SHARED_FF].reshape(rows_d, devices, half_sh),
            w_shared_in[:, SHARED_FF:].reshape(rows_d, devices, half_sh),
        ],
        axis=2,
    ).transpose(1, 0, 2)
    shared_w = lax.all_to_all(shared_pieces, BOTH, split_axis=0, concat_axis=0, tiled=True)
    shared_w = shared_w.reshape(D, 2 * half_sh)
    pad = half_all - half_ff - half_sh
    w_in = jnp.concatenate(
        [
            w_expert_in[0][:, :half_ff],
            jnp.pad(shared_w[:, :half_sh], ((0, 0), (0, pad))),
            w_expert_in[0][:, half_ff:],
            jnp.pad(shared_w[:, half_sh:], ((0, 0), (0, pad))),
        ],
        axis=1,
    )
    w_back = jnp.concatenate(
        [w_expert_out[0], jnp.pad(w_shared_out, ((0, pad), (0, 0)))], axis=0
    )

    most_rows = 3 * tok // 8
    paths = (
        (("y", "z", "x"), 0, most_rows),
        (("z", "x", "y"), most_rows, most_rows),
        (("x", "y", "z"), 2 * most_rows, tok - 2 * most_rows),
    )
    tokens = devices * tok
    x_own, x_sib = [], []
    for order, start, count in paths:
        x_own.append(links.gather(ffn_in[start : start + count], order))
    for x in x_own:
        x_sib.append(links.shift(x, "c", 1))
    region = [0] * 6
    for i in range(1, 6):
        region[i] = region[i - 1] + x_own[(i - 1) // 2].shape[0]
    kept = None
    moved, outs, row_grads = [None] * 3, [None] * 3, [None] * 3

    def ffn(i, side, kept, adds):
        order, start, count = paths[i]
        source = links.device_of(order + ("c",)).reshape(2, -1)[side]
        m = m_all[source][:, start : start + count].reshape(-1, 1)
        return ffn_chunk(
            (x_own, x_sib)[side][i],
            g_blocks,
            m,
            w_in,
            w_back,
            half_ff,
            source,
            start // count,
            kept,
            region[2 * i + side],
            tokens,
            adds,
        )

    for i, side in ((0, 1), (1, 1), (0, 0), (2, 1), (1, 0), (2, 0)):
        if side == 1:
            kept, out, grad = ffn(i, 1, kept, None)
            moved[i] = [links.shift(out, "c", -1), links.shift(grad, "c", -1)]
        else:
            kept, out, grad = ffn(i, 0, kept, moved[i])
            row_grads[i] = links.scatter_sum(grad, paths[i][0])
            outs[i] = links.scatter_sum(out, paths[i][0])
    ffn_out = jnp.concatenate(outs, axis=0).astype(f32)
    grad_ffn = jnp.concatenate(row_grads, axis=0).astype(f32)
    mixed = (middle + ffn_out).astype(bf16)
    x_all, g_kept, act_all, grad_pre_all = kept
    query_w_all = lax.all_gather(after(w_query, moved[2][0]), BOTH, axis=0, tiled=True)
    grad_w_in = matmul_left_t(x_all, grad_pre_all)
    grad_w_back = matmul_left_t(act_all, g_kept)
    grad_w_expert_in = jnp.concatenate(
        [grad_w_in[:, :half_ff], grad_w_in[:, half_all : half_all + half_ff]], axis=1
    )
    grad_w_expert_out = grad_w_back[:half_ff]
    grad_w_shared_out = grad_w_back[half_ff : half_ff + half_sh]
    grad_shared = jnp.concatenate(
        [
            grad_w_in[:, half_ff : half_ff + half_sh],
            grad_w_in[:, half_all + half_ff : half_all + half_ff + half_sh],
        ],
        axis=1,
    ).reshape(devices, rows_d, 2 * half_sh)
    grad_shared = lax.all_to_all(grad_shared, BOTH, split_axis=0, concat_axis=0, tiled=True)
    grad_shared = grad_shared.transpose(1, 0, 2)
    grad_w_shared_in = jnp.concatenate(
        [
            grad_shared[:, :, :half_sh].reshape(rows_d, SHARED_FF),
            grad_shared[:, :, half_sh:].reshape(rows_d, SHARED_FF),
        ],
        axis=1,
    )

    grad_out = cotangent.astype(f32)
    grad_middle_part, grad_norm_ffn = rms_backward(middle, inverse_ffn, gain_ffn, grad_ffn)
    grad_middle = grad_out + grad_middle_part
    grad_attended = grad_middle.astype(bf16)
    grad_heads_all = matmul_right_t(grad_attended, out_w).astype(bf16)
    pieces = [
        jnp.concatenate(
            [columns(grad_heads_all, k, v_cols), columns(grad_attended, k, D // ctx)], axis=1
        )
        for k in range(ctx)
    ]
    arrived = jnp.concatenate(links.ctx_exchange(pieces), axis=0)
    grad_heads = arrived[:, :v_cols].reshape(row, heads, VDIM).transpose(1, 0, 2)
    grad_attended_cols = arrived[:, v_cols:]
    heads_out_row = links.ctx_gather(heads_out)

    soft = jnp.exp(masked_scores() - log_total)
    grad_values = jnp.einsum(
        "hqk,hqd->hkd", soft.astype(bf16), grad_heads, preferred_element_type=f32
    )
    grad_probs = jnp.einsum("hqd,hkd->hqk", grad_heads, value, preferred_element_type=f32)
    row_delta = jnp.sum(soft * grad_probs, axis=-1, keepdims=True)
    grad_raw = (soft * (grad_probs - row_delta) * scale).astype(bf16)
    grad_query = jnp.einsum("hqk,hkd->qhd", grad_raw, key, preferred_element_type=f32)
    grad_key = jnp.einsum("hqk,hqd->khd", grad_raw, query, preferred_element_type=f32)
    grad_key_rope = jnp.sum(grad_key[..., NOPE:], axis=1)
    grad_keyval = jnp.concatenate(
        [grad_key[..., :NOPE], grad_values.transpose(1, 0, 2)], axis=-1
    )
    grad_keyval = grad_keyval.astype(bf16).reshape(row, kv_cols)
    grad_w_up = matmul_left_t(latent, grad_keyval)
    grad_latent = matmul_right_t(grad_keyval, up_w)
    grad_low = jnp.concatenate([grad_latent, grad_key_rope], axis=1).astype(bf16)
    grad_low = links.scatter_sum(grad_low, ("x", "y")).astype(f32)
    grad_query_raw = jnp.concatenate(
        [
            grad_query[..., :NOPE],
            unrotate(grad_query[..., NOPE:], cosine[:, None, :], sine_part[:, None, :]),
        ],
        axis=-1,
    )
    grad_query_raw = grad_query_raw.astype(bf16).reshape(ctx, tok, q_cols)
    query_back = jnp.stack(links.ctx_exchange([grad_query_raw[k] for k in range(ctx)]))
    query_back = query_back[ctx_place].transpose(1, 0, 2).reshape(tok, ctx * q_cols)
    grad_compressed_latent, grad_norm_latent = rms_backward(
        raw_latent[:tok], inverse_latent[:tok], gain_latent, grad_low[:, :LATENT]
    )
    grad_compressed = jnp.concatenate(
        [
            grad_compressed_latent,
            unrotate(grad_low[:, LATENT:], cosine[:tok], sine_part[:tok]),
        ],
        axis=1,
    ).astype(bf16)
    grad_normed = matmul_right_t(grad_compressed, down_w) + matmul_right_t(
        query_back, query_w_all
    )
    grad_input_part, grad_norm_attn = rms_backward(
        inputs, inverse_row[:tok], gain_attn, grad_normed
    )
    grad_in = grad_middle + grad_input_part

    z_rel = (links.own["z"] - jnp.arange(links.size["z"], dtype=jnp.int32)) % links.size["z"]
    c_rel = (links.own["c"] - jnp.arange(2, dtype=jnp.int32)) % 2
    dp_rel = (c_rel[:, None] + 2 * z_rel[None, :]).reshape(-1)

    def to_owners(value):
        count = value.shape[1]
        value = value.astype(bf16).reshape(links.dp, ctx * count, -1)[dp_rel]
        value = links.scatter_sum(value.reshape(devices * count, -1), ("z", "c"))
        value = value.reshape(ctx, count, -1)[rel_ctx]
        value = jnp.stack(links.ctx_exchange([value[k] for k in range(ctx)]))[ctx_place]
        return value.astype(f32)

    def joined(value):
        return value.transpose(1, 0, 2).reshape(value.shape[1], -1)

    grad_out_cols = matmul_left_t(heads_out_row, grad_attended_cols)
    grad_w_out = joined(to_owners(grad_out_cols.reshape(devices, rows_d, D // ctx)))
    grad_w_q = matmul_left_t(normed_row, grad_query_raw.reshape(row, q_cols))
    grad_w_up = grad_w_up.astype(bf16).reshape(devices, rows_l, up_parts, up_fold)
    grad_w_up = grad_w_up.transpose(0, 2, 1, 3).reshape(devices, rows_d, up_fold)
    heads_grads = to_owners(
        jnp.concatenate(
            [grad_w_q.astype(bf16).reshape(devices, rows_d, q_cols), grad_w_up], axis=2
        )
    )
    grad_w_query = joined(heads_grads[:, :, :q_cols])
    grad_w_kv_up = heads_grads[:, :, q_cols:].reshape(ctx, up_parts, rows_l, up_fold)
    grad_w_kv_up = grad_w_kv_up.transpose(2, 0, 1, 3).reshape(rows_l, ctx * kv_cols)

    compressed_cols = jnp.concatenate(
        links.ctx_exchange([columns(grad_compressed, k, dn_cols) for k in range(ctx)]), axis=0
    )
    grad_w_down = matmul_left_t(normed_row, compressed_cols).astype(bf16)
    vectors = jnp.stack(
        [
            jnp.pad(v.reshape(devices, -1), ((0, 0), (0, dn_cols - v.size // devices)))
            for v in (grad_norm_attn, grad_norm_ffn, grad_norm_latent)
        ],
        axis=1,
    )
    vectors = jnp.pad(vectors, ((0, 0), (0, 13), (0, 0))).astype(bf16)
    last_grads = to_owners(
        jnp.concatenate([grad_w_down.reshape(devices, rows_d, dn_cols), vectors], axis=1)
    )
    grad_w_kv_down = joined(last_grads[:, :rows_d])
    vector_sums = jnp.sum(last_grads[:, rows_d : rows_d + 3], axis=0)
    return (
        mixed,
        grad_in,
        vector_sums[0, :rows_d],
        grad_w_query,
        grad_w_kv_down,
        vector_sums[2, :rows_l],
        grad_w_kv_up,
        grad_w_out,
        vector_sums[1, :rows_d],
        grad_w_shared_in,
        grad_w_shared_out,
        grad_w_expert_in[None],
        grad_w_expert_out[None],
    )


def solution(mesh):
    rows = P(BOTH, None)
    vector = P(BOTH)
    experts = P(BOTH, None, None)
    return jax.shard_map(
        shards,
        mesh=mesh,
        in_specs=(
            rows,
            P("dp"),
            rows,
            rows,
            rows,
            vector,
            rows,
            rows,
            vector,
            rows,
            rows,
            vector,
            rows,
            rows,
            experts,
            experts,
        ),
        out_specs=(
            rows,
            rows,
            vector,
            rows,
            rows,
            vector,
            rows,
            rows,
            vector,
            rows,
            rows,
            experts,
            experts,
        ),
        check_vma=False,
    )
```

```python
import math

import jax
import jax.numpy as jnp
from jax import lax
from jax.experimental import pallas as pl
from jax.experimental.pallas import tpu as pltpu
from jax.sharding import PartitionSpec as P

D = 2048
HEADS = 16
NOPE = 128
ROPE = 64
VDIM = 128
LATENT = 512
EXPERT_FF = 1408
SHARED_FF = 2816
TOP = 6

BOTH = ("dp", "ctx")
epsilon = 1e-06
f32 = jnp.float32
bf16 = jnp.bfloat16


def matmul(left, right):
    return jnp.dot(left, right, preferred_element_type=f32)


def matmul_left_t(left, right):
    return lax.dot_general(left, right, (((0,), (0,)), ((), ())), preferred_element_type=f32)


def matmul_right_t(left, right):
    return lax.dot_general(left, right, (((1,), (1,)), ((), ())), preferred_element_type=f32)


def rope_tables(positions, rope_width):
    half_width = rope_width // 2
    frequency = jnp.exp(
        -math.log(10000.0) * jnp.arange(half_width).astype(f32) / half_width
    )
    angles = positions.astype(f32)[:, None] * frequency[None, :]
    return (jnp.cos(angles), jnp.sin(angles))


def rotate(operand, cosine, sine_part):
    half_width = operand.shape[-1] // 2
    first_half = operand[..., :half_width]
    second_half = operand[..., half_width:]
    return jnp.concatenate(
        [
            first_half * cosine - second_half * sine_part,
            second_half * cosine + first_half * sine_part,
        ],
        axis=-1,
    )


def unrotate(operand, cosine, sine_part):
    return rotate(operand, cosine, -sine_part)


def swish(operand):
    return operand * jax.nn.sigmoid(operand)


def swish_slope(operand):
    sigma = jax.nn.sigmoid(operand)
    return sigma * (1.0 + operand * (1.0 - sigma))


def rms_inverse(operand):
    return lax.rsqrt(jnp.mean(operand * operand, axis=-1, keepdims=True) + epsilon)


def rms_backward(operand, inverse, gain_vec, grad_out):
    scaled = grad_out * gain_vec
    grad_gain = jnp.sum(grad_out * operand * inverse, axis=0)
    grad_operand = inverse * scaled - operand * inverse * inverse * inverse * jnp.mean(
        scaled * operand, axis=-1, keepdims=True
    )
    return (grad_operand, grad_gain)


class Links:
    def __init__(self):
        self.dp = lax.axis_size("dp")
        self.ctx = lax.axis_size("ctx")
        self.size = {"z": self.dp // 2, "c": 2, "w": self.ctx // 4, "y": 2, "x": 2}
        dp, ctx = lax.axis_index("dp"), lax.axis_index("ctx")
        self.own = {
            "z": dp // 2,
            "c": dp % 2,
            "w": ctx // 4,
            "y": (ctx // 2) % 2,
            "x": ctx % 2,
        }

    def shift(self, value, axis, by=1):
        name, count = ("dp", self.dp) if axis in "zc" else ("ctx", self.ctx)
        if axis == "z":
            pairs = [(i, (i + 2 * by) % count) for i in range(count)]
        elif axis == "w":
            pairs = [(i, (i + 4 * by) % count) for i in range(count)]
        else:
            pairs = [(i, i ^ (2 if axis == "y" else 1)) for i in range(count)]
        return lax.ppermute(value, name, pairs)

    def shift_ctx(self, value, k):
        pairs = [
            (i, (i // 4 - k // 4) % self.size["w"] * 4 + (i ^ k) % 4) for i in range(self.ctx)
        ]
        return lax.ppermute(value, "ctx", pairs)

    def ring(self, block, axis):
        held = [block]
        for _ in range(self.size[axis] - 1):
            held.append(self.shift(held[-1], axis))
        return held

    def gather(self, block, order):
        for axis in order:
            block = joined_rows(self.ring(block, axis))
        return block

    def reduce(self, parts, axis):
        total = parts[-1]
        for part in parts[-2::-1]:
            total = plus(self.shift(total, axis, -1), part)
        return total

    def scatter_sum(self, block, order):
        for axis in order[::-1]:
            block = self.reduce(jnp.split(block, self.size[axis]), axis)
        return block

    def device_of(self, order):
        place = dict(self.own)
        depth = len(order)
        for i, axis in enumerate(order):
            shape = [1] * depth
            shape[depth - 1 - i] = self.size[axis]
            offsets = jnp.arange(self.size[axis], dtype=jnp.int32).reshape(shape)
            place[axis] = (self.own[axis] - offsets) % self.size[axis]
        number = (place["z"] * 2 + place["c"]) * self.ctx
        number = number + place["w"] * 4 + place["y"] * 2 + place["x"]
        return number.reshape(-1)

    def place_of(self, order):
        number = jnp.arange(self.dp * self.ctx, dtype=jnp.int32)
        coordinate = {
            "x": number % 2,
            "y": (number // 2) % 2,
            "w": (number // 4) % self.size["w"],
            "c": (number // self.ctx) % 2,
            "z": number // (2 * self.ctx),
        }
        place = jnp.zeros_like(number)
        for axis in order[::-1]:
            steps = (self.own[axis] - coordinate[axis]) % self.size[axis]
            place = place * self.size[axis] + steps
        return place

    def ctx_relative(self):
        return self.device_of(("x", "y", "w")) % self.ctx

    def ctx_place(self):
        number = jnp.arange(self.ctx, dtype=jnp.int32)
        w = (self.own["w"] - number // 4) % self.size["w"]
        return w * 4 + (lax.axis_index("ctx") ^ number) % 4

    def ctx_exchange(self, pieces):
        result = [pieces[0]] + [None] * (self.ctx - 1)
        for k in range(1, self.ctx):
            back = (-(k // 4)) % self.size["w"] * 4 + k % 4
            result[back] = self.shift_ctx(pieces[k], k)
        return result


def joined_rows(parts):
    return parts[0] if len(parts) == 1 else jnp.concatenate(parts, axis=0)


def plus(left, right):
    return (left.astype(f32) + right.astype(f32)).astype(bf16)


def tie(*values):
    return lax.optimization_barrier(values)


def after(value, *others):
    return lax.optimization_barrier((value,) + others)[0]


GROUP = 4


def ffn_kernel(half_ff, parts, part_steps, sources, x_ref, *refs):
    g_refs, (m_ref, w_in, w_out) = refs[:GROUP], refs[GROUP : GROUP + 3]
    refs = refs[GROUP + 3 :]
    if parts:
        moved, refs = refs[0], refs[1:]
    outs = refs[-max(2 * parts, 1) :]
    x_all, g_all, act, grad_pre = refs[-len(outs) - 4 : -len(outs)]
    half_all = act.shape[1]
    count = x_ref.shape[0] // GROUP
    x_all[...] = x_ref[...]
    for i, g_ref in enumerate(g_refs):
        g_all[i * count : (i + 1) * count] = g_ref[0]
    pre = matmul(x_ref[...], w_in[...])
    gate, up = pre[:, :half_all], pre[:, half_all:]
    column = lax.broadcasted_iota(jnp.int32, (1, half_all), 1)
    weight = jnp.where(column < half_ff, m_ref[...], 1.0)
    sigma = jax.nn.sigmoid(gate)
    swished = gate * sigma
    act[...] = (swished * up * weight).astype(bf16)
    grad_act = matmul_right_t(g_all[...], w_out[...]) * weight
    slope = sigma * (1.0 + gate * (1.0 - sigma))
    grad_pre[:, :half_all] = (grad_act * up * slope).astype(bf16)
    grad_pre[:, half_all:] = (grad_act * swished).astype(bf16)
    out_part = matmul(act[...], w_out[...])
    grad_part = matmul_right_t(grad_pre[...], w_in[...])
    if not parts:
        outs[0][:, :D] = out_part.astype(bf16)
        outs[0][:, D:] = grad_part.astype(bf16)
        return
    out_part = (out_part + moved[:, :D].astype(f32)).astype(bf16)
    grad_part = (grad_part + moved[:, D:].astype(f32)).astype(bf16)
    for k in range(parts):

        @pl.when(pl.program_id(0) // part_steps == k)
        def _():
            outs[2 * k][...] = out_part
            outs[2 * k + 1][...] = grad_part


def ffn_chunk(x, g_blocks, m, w_in, w_out, half_ff, sources, group, far, side, kept, moved, lean):
    half_all = w_out.shape[0]
    tokens = m.shape[0]
    count = tokens // sources.shape[0]
    tile = GROUP * count
    steps = x.shape[0] // tile
    parts = 4 if far == 2 else 2
    half = steps // parts
    per_slice = 4 * half
    base = 2 * group * per_slice + (2 * side + far % 2) * half

    def second(i):
        return (i // half) % 2

    def place(i):
        return base + i % half + second(i) * per_slice + i // (2 * half) * half

    def rows(width):
        return pl.BlockSpec((tile, width), lambda i, _: (i, 0))

    def kept_rows(width):
        return pl.BlockSpec((tile, width), lambda i, _: (i if lean else place(i), 0))

    def whole(value):
        return pl.BlockSpec(value.shape, lambda i, _: (0, 0), pipeline_mode=pl.Buffered(1))

    def g_spec(j):
        def index(i, s):
            return (s[GROUP * place(i) + j], 2 * group + second(i), 0)

        return pl.BlockSpec((1, count, D), index)

    operands = [sources, x] + [g_blocks] * GROUP + [m, w_in, w_out]
    in_specs = [rows(D)] + [g_spec(j) for j in range(GROUP)]
    in_specs += [pl.BlockSpec((tile, 1), lambda i, _: (place(i), 0)), whole(w_in), whole(w_out)]
    out_specs = [rows(2 * D)]
    out_shape = [jax.ShapeDtypeStruct((x.shape[0], 2 * D), bf16)]
    if moved is not None:
        operands.append(moved)
        in_specs.append(rows(2 * D))

        def part_spec(k):
            return pl.BlockSpec(
                (tile, D), lambda i, _: (jnp.clip(i - k * half, 0, half - 1), 0)
            )

        out_specs = [part_spec(k // 2) for k in range(2 * parts)]
        out_shape = [jax.ShapeDtypeStruct((half * tile, D), bf16)] * (2 * parts)
    aliases = {}
    if kept is not None:
        aliases = {len(operands) + i: i for i in range(4)}
        operands += kept
        in_specs += [pl.BlockSpec(memory_space=pl.ANY)] * 4
    widths = (D, D, half_all, 2 * half_all)
    kept_count = x.shape[0] if lean else tokens
    flops = 2 * x.shape[0] * D * 6 * half_all
    result = pl.pallas_call(
        lambda *refs: ffn_kernel(half_ff, 0 if moved is None else parts, half, *refs),
        grid_spec=pltpu.PrefetchScalarGridSpec(
            num_scalar_prefetch=1,
            grid=(steps,),
            in_specs=in_specs,
            out_specs=[kept_rows(w) for w in widths] + out_specs,
        ),
        out_shape=[jax.ShapeDtypeStruct((kept_count, w), bf16) for w in widths] + out_shape,
        input_output_aliases=aliases,
        compiler_params=pltpu.CompilerParams(vmem_limit_bytes=60 * 2**20),
        cost_estimate=pl.CostEstimate(
            flops=flops, bytes_accessed=x.shape[0] * D * 16, transcendentals=0
        ),
        name="ffn_chunk",
    )(*operands)
    return list(result[:4]), list(result[4:])


def shards(
    hidden_in,
    segments,
    routes,
    gates,
    cotangent,
    norm_attn,
    w_query,
    w_kv_down,
    norm_latent,
    w_kv_up,
    w_out,
    norm_ffn,
    w_shared_in,
    w_shared_out,
    w_expert_in,
    w_expert_out,
):
    links = Links()
    tok = hidden_in.shape[0]
    row = segments.shape[0]
    ctx = links.ctx
    devices = links.dp * ctx
    me = lax.axis_index("dp") * ctx + lax.axis_index("ctx")
    half_ff = EXPERT_FF // 2
    half_sh = w_shared_out.shape[0]
    half_all = -(-(half_ff + half_sh) // 128) * 128
    heads = HEADS // ctx
    q_cols = heads * (NOPE + ROPE)
    v_cols = heads * VDIM
    kv_cols = heads * (NOPE + VDIM)
    dn_cols = (LATENT + ROPE) // ctx
    rows_d = w_query.shape[0]
    rows_l = w_kv_up.shape[0]
    up_fold = rows_l * kv_cols // rows_d
    up_parts = rows_d // rows_l
    scale = 1.0 / math.sqrt(NOPE + ROPE)
    rel_ctx = links.ctx_relative()
    ctx_place = links.ctx_place()

    def columns(value, k, width):
        return lax.dynamic_slice_in_dim(value, rel_ctx[k] * width, width, 1)

    latent_gain = jnp.zeros((rows_d,), bf16).at[:rows_l].set(norm_latent)
    small = jnp.concatenate(
        [w_kv_down, norm_attn[:, None], norm_ffn[:, None], latent_gain[:, None]], axis=1
    )
    small = jnp.pad(small, ((0, 0), (0, -small.shape[1] % 128)))
    small_cols = small.shape[1]
    small = jnp.concatenate([small, w_out], axis=1)
    pieces = []
    for k in range(ctx):
        folded = columns(w_kv_up, k, kv_cols).reshape(rows_l, up_parts, up_fold)
        folded = folded.transpose(1, 0, 2).reshape(rows_d, up_fold)
        pieces.append(jnp.concatenate([columns(w_query, k, q_cols), folded], axis=1))
    hidden_parts = links.ctx_exchange([hidden_in] * ctx)
    step, *received = tie(links.shift(small, "z"), *links.ctx_exchange(pieces))
    heads_w = joined_rows(received)
    small_parts, heads_parts = [small, step], [heads_w]
    for i in range(links.size["z"] - 1):
        pair = [links.shift(heads_parts[-1], "z")]
        if i < links.size["z"] - 2:
            pair.append(links.shift(small_parts[-1], "z"))
        else:
            small_all = links.gather(joined_rows(small_parts), ("w",))
            small_all = small_all.reshape(-1, 2, rows_d // 2, small.shape[1])
            small_a = small_all[:, 0].reshape(-1, small.shape[1])
            small_b = small_all[:, 1].reshape(-1, small.shape[1])
            pair += [links.shift(small_a, "x"), links.shift(small_b, "y")]
        pair = list(tie(*pair))
        if i < links.size["z"] - 2:
            small_parts.append(pair[1])
        if i == 0:
            w_shared_in, _ = tie(w_shared_in, pair[0])
        if i == links.size["z"] - 3:
            pair[0], *hidden_parts = tie(pair[0], *hidden_parts)
            hidden_row = joined_rows(hidden_parts)
        heads_parts.append(pair[0])
    small_a, small_b = joined_rows([small_a, pair[1]]), joined_rows([small_b, pair[2]])
    heads_w = joined_rows(heads_parts)
    heads_c = links.shift(heads_w, "c")
    last_a, last_b = small_a[:, small_cols:], small_b[:, small_cols:]
    small_a, small_b = small_a[:, :small_cols], small_b[:, :small_cols]
    shared_pieces = jnp.concatenate(
        [
            w_shared_in[:, :SHARED_FF].reshape(rows_d, devices, half_sh),
            w_shared_in[:, SHARED_FF:].reshape(rows_d, devices, half_sh),
        ],
        axis=2,
    ).transpose(1, 0, 2)
    shared_w = lax.all_to_all(shared_pieces, BOTH, split_axis=0, concat_axis=0, tiled=True)
    far_a, far_b, shared_w = tie(links.shift(small_a, "y"), links.shift(small_b, "x"), shared_w)
    small_all = joined_rows([small_a, far_a, small_b, far_b])
    small_all = joined_rows([small_all, links.shift(small_all, "c")])
    heads_w = joined_rows([heads_w, heads_c]).reshape(devices, rows_d, q_cols + up_fold)
    blocks = devices // 2
    place_a = links.place_of(("z", "w", "x", "y", "c"))
    place_b = links.place_of(("z", "w", "y", "x", "c"))
    take_a = (place_a // blocks) * 2 * blocks + place_a % blocks
    take_b = (place_b // blocks) * 2 * blocks + blocks + place_b % blocks
    take = jnp.stack([take_a, take_b], axis=1).reshape(-1)
    small_all = small_all.reshape(2 * devices, rows_d // 2, small_cols)[take]
    small_all = small_all.reshape(devices, rows_d, small_cols)
    down_w = small_all[:, :, : LATENT + ROPE].reshape(D, LATENT + ROPE)
    gain_attn = small_all[:, :, LATENT + ROPE].reshape(D).astype(f32)
    gain_ffn = small_all[:, :, LATENT + ROPE + 1].reshape(D).astype(f32)
    gain_latent = small_all[:, :rows_l, LATENT + ROPE + 2].reshape(LATENT).astype(f32)

    heads_place = links.place_of(("x", "y", "w", "z", "c"))
    heads_w = heads_w[heads_place]
    query_w = heads_w[:, :, :q_cols].reshape(D, q_cols)
    up_w = heads_w[:, :, q_cols:].reshape(devices, up_parts, rows_l, up_fold)
    up_w = up_w.transpose(0, 2, 1, 3).reshape(LATENT, kv_cols)

    orders = (
        ("z", "w", "x", "y"),
        ("z", "w", "y", "x"),
        ("y", "z", "w", "x"),
        ("x", "z", "w", "y"),
    )
    slices = len(orders)
    count = tok // slices
    tokens = devices * tok
    source_list = [links.device_of(order + ("c",)) for order in orders]
    sources = jnp.concatenate(source_list)
    m_place = jnp.concatenate([d * slices + i for i, d in enumerate(source_list)])
    hidden_row, query_w, up_w, down_w = tie(hidden_row, query_w, up_w, down_w)
    g_all = lax.all_gather(after(cotangent, far_a), BOTH, axis=0, tiled=True)
    g_blocks = g_all.reshape(devices, tok, D)

    inputs_row = hidden_row.astype(f32)
    inverse_row = rms_inverse(inputs_row)
    normed_row = (inputs_row * inverse_row * gain_attn).astype(bf16)
    positions = (rel_ctx[:, None] * tok + jnp.arange(tok, dtype=jnp.int32)[None, :]).reshape(-1)
    row_segments = segments.reshape(ctx, tok)[rel_ctx].reshape(-1)
    allowed = (positions[None, :] <= positions[:, None]) & (
        row_segments[None, :] == row_segments[:, None]
    )
    cosine, sine_part = rope_tables(positions, ROPE)
    query_raw = matmul(normed_row, query_w).reshape(row, heads, NOPE + ROPE)
    query = jnp.concatenate(
        [
            query_raw[..., :NOPE],
            rotate(query_raw[..., NOPE:], cosine[:, None, :], sine_part[:, None, :]),
        ],
        axis=-1,
    ).astype(bf16)
    query = query.transpose(1, 0, 2)
    compressed = matmul(normed_row, down_w)
    raw_latent = compressed[:, :LATENT]
    inverse_latent = rms_inverse(raw_latent)
    latent = (raw_latent * inverse_latent * gain_latent).astype(bf16)
    key_rope = rotate(compressed[:, LATENT:], cosine, sine_part).astype(bf16)
    keyval = matmul(latent, up_w).astype(bf16).reshape(row, heads, NOPE + VDIM)
    last_a, last_b = tie(last_a, last_b, far_a)[:2]
    last_y, last_x, keyval = tie(links.shift(last_a, "y"), links.shift(last_b, "x"), keyval)
    out_w = joined_rows([last_a, last_y, last_b, last_x])
    out_w = joined_rows([out_w, links.shift(out_w, "c")])
    out_w = out_w.reshape(2 * devices, rows_d // 2, D)[take].reshape(D, D)
    keyval = keyval.transpose(1, 0, 2)
    key = jnp.concatenate(
        [keyval[..., :NOPE], jnp.broadcast_to(key_rope[None], (heads, row, ROPE))], axis=-1
    )
    value = keyval[..., NOPE:]

    def masked_scores():
        raw = jnp.einsum("hqd,hkd->hqk", query, key, preferred_element_type=f32)
        return jnp.where(allowed[None], raw * scale, -1e30)

    scores = masked_scores()
    row_max = jnp.max(scores, axis=-1, keepdims=True)
    exponent = jnp.exp(scores - row_max)
    row_total = jnp.sum(exponent, axis=-1, keepdims=True)
    log_total = row_max + jnp.log(row_total)
    probs = (exponent / row_total).astype(bf16)
    heads_part = jnp.einsum("hqk,hkd->qhd", probs, value, preferred_element_type=f32)
    heads_part = heads_part.astype(bf16).reshape(ctx, tok, v_cols)
    returned = jnp.stack(links.ctx_exchange([heads_part[k] for k in range(ctx)]))
    heads_out = returned[ctx_place].transpose(1, 0, 2).reshape(tok, HEADS * VDIM)
    inputs = hidden_in.astype(f32)
    middle = inputs + matmul(heads_out, out_w)
    inverse_ffn = rms_inverse(middle)
    ffn_in = (middle * inverse_ffn * gain_ffn).astype(bf16)

    cut = [ffn_in[i * count : (i + 1) * count] for i in range(slices)]

    def halved(parts):
        both = [jnp.split(part, 2) for part in parts]
        return [joined_rows([pair[i] for pair in both]) for i in range(2)]

    held = joined_rows(cut[:2])
    near_y, near_x, first, shared_w, w_expert_in, routes, gates = tie(
        links.shift(cut[2], "y"),
        links.shift(cut[3], "x"),
        links.shift(held, "z"),
        shared_w,
        w_expert_in,
        routes,
        gates,
    )
    experts = devices // 2
    expert_number = jnp.arange(experts, dtype=jnp.int32)[:, None, None]
    gate_matrix = jnp.sum(
        jnp.where(routes.T[None] == expert_number, gates.T[None], 0.0), axis=1
    )
    m_all = lax.all_to_all(
        jnp.repeat(gate_matrix, 2, axis=0), BOTH, split_axis=0, concat_axis=0, tiled=True
    )
    shared_w = shared_w.reshape(D, 2 * half_sh)
    pad = half_all - half_ff - half_sh
    w_in = jnp.concatenate(
        [
            w_expert_in[0][:, :half_ff],
            jnp.pad(shared_w[:, :half_sh], ((0, 0), (0, pad))),
            w_expert_in[0][:, half_ff:],
            jnp.pad(shared_w[:, half_sh:], ((0, 0), (0, pad))),
        ],
        axis=1,
    )
    w_back = jnp.concatenate(
        [w_expert_out[0], jnp.pad(w_shared_out, ((0, pad), (0, 0)))], axis=0
    )
    m = m_all.reshape(devices * slices, count)[m_place].reshape(tokens, 1)
    ring_a = [held, first]
    while len(ring_a) < links.size["z"]:
        ring_a.append(links.shift(ring_a[-1], "z"))
    held = links.gather(joined_rows(ring_a), ("w",)) if links.size["w"] > 1 else None
    slice_0, slice_1 = halved(jnp.split(held, ctx // 4 * links.size["z"]) if held is not None else ring_a)
    held = joined_rows([cut[2], near_y, cut[3], near_x])
    held, slice_0, slice_1, w_in, w_back, m = tie(held, slice_0, slice_1, w_in, w_back, m)
    ring_b = [held]
    moved_0, moved_1, step = tie(
        links.shift(slice_0, "x"), links.shift(slice_1, "y"), links.shift(held, "z")
    )
    ring_b.append(step)
    near_a = [joined_rows([slice_0, moved_0]), joined_rows([slice_1, moved_1])]
    far_a = [links.shift(near_a[0], "y"), links.shift(near_a[1], "x")]
    near_a_rows = joined_rows(near_a)
    near_a_sib = links.shift(near_a_rows, "c")

    lean = devices > 32
    kept = None
    done, moved = {}, {}

    def ffn(rows, name, side):
        kept_now, parts = ffn_chunk(
            rows,
            g_blocks,
            m,
            w_in,
            w_back,
            half_ff,
            sources,
            "ab".index(name[0]),
            ("n", "f", "").index(name[1:]),
            side,
            None if lean else kept,
            moved.get(name) if side == 0 else None,
            lean,
        )
        if side == 1:
            moved[name] = links.shift(parts[0], "c", -1)
        done[name, side] = parts
        if lean:
            sums = [
                matmul_left_t(kept_now[0], kept_now[3]),
                matmul_left_t(kept_now[2], kept_now[1]),
            ]
            return sums if kept is None else [a + b for a, b in zip(kept, sums)]
        return kept_now

    near_a_sib, step = tie(near_a_sib, links.shift(ring_b[-1], "z"))
    ring_b.append(step)
    step = links.shift(ring_b[-1], "z")
    kept = ffn(near_a_sib, "an", 1)
    step, *far_a = tie(step, *far_a, done["an", 1][0])[:3]
    far_a_rows = joined_rows(far_a)
    far_a_sib = links.shift(far_a_rows, "c")
    ring_b.append(step)
    far_a_sib, ring_b[-1] = tie(far_a_sib, ring_b[-1])
    while len(ring_b) < links.size["z"]:
        ring_b.append(links.shift(ring_b[-1], "z"))
    held = links.gather(joined_rows(ring_b), ("w",)) if links.size["w"] > 1 else None
    near_b = halved(jnp.split(held, ctx // 4 * links.size["z"]) if held is not None else ring_b)
    far_b = [links.shift(near_b[0], "x"), links.shift(near_b[1], "y")]
    kept = ffn(far_a_sib, "af", 1)
    kept = ffn(near_a_rows, "an", 0)
    far_a_rows, *far_b = tie(far_a_rows, *far_b, done["an", 0][0])[:3]
    rows_b = joined_rows([*near_b, *far_b])
    sib_b = links.shift(rows_b, "c")
    kept = ffn(far_a_rows, "af", 0)

    def add_far(moved_rows, near):
        return [plus(m_rows, n_rows) for m_rows, n_rows in zip(moved_rows, near)]

    def split_far(rows):
        pairs = [jnp.split(r, 2) for r in rows]
        return [p[0] for p in pairs], [p[1] for p in pairs]

    def z_parts(rows):
        if links.size["w"] > 1:
            rows = [links.scatter_sum(r, ("w",)) for r in rows]
        return [joined_rows(p) for p in zip(*[jnp.split(r, links.size["z"]) for r in rows])]

    def last_b(total):
        n0, f0, n1, f1 = jnp.split(total, 4)
        return plus(links.shift(f0, "y", -1), n0), plus(links.shift(f1, "x", -1), n1)

    far = done["af", 0][1::2]
    a_far = [links.shift(far[0], "y", -1), links.shift(far[1], "x", -1)]
    query_w_all = lax.all_gather(after(w_query, sib_b), BOTH, axis=0, tiled=True)
    kept = ffn(sib_b, "b", 1)
    a_far = tie(*a_far, done["b", 1][0])[:2]
    a_near = add_far(a_far, done["an", 0][1::2])
    rows_b, heads_out, *a_near = tie(rows_b, heads_out, *a_near)
    a_near, far = split_far(a_near)
    a_far = [links.shift(far[0], "x", -1), links.shift(far[1], "y", -1)]
    heads_half = [heads_out[: tok // 2], heads_out[tok // 2 :]]
    heads_far = [links.shift(heads_half[0], "x"), links.shift(heads_half[1], "y")]
    kept = ffn(rows_b, "b", 0)
    *a_far, heads_far[0], heads_far[1] = tie(*a_far, *heads_far, done["b", 0][0])[:4]
    done["bn", 0], done["bf", 0] = done["b", 0][:4], done["b", 0][4:]
    heads_half = [joined_rows(p) for p in zip(heads_half, heads_far)]
    far = done["bf", 0][1::2]
    b_far = [links.shift(far[0], "x", -1), links.shift(far[1], "y", -1)]
    a_parts = z_parts(add_far(a_far, a_near))
    heads_far = [links.shift(heads_half[0], "y"), links.shift(heads_half[1], "x")]
    a_sum = links.shift(a_parts[-1], "z", -1)
    out_far = [done["af", 0][0], done["af", 0][2]]
    out_far_b = [done["bf", 0][0], done["bf", 0][2]]
    if lean:
        grad_w_in, grad_w_back = kept
        a_sum = plus(a_sum, a_parts[-2])
        for part in a_parts[-3::-1]:
            a_sum = plus(links.shift(a_sum, "z", -1), part)
        out_far = [links.shift(p, axis, -1) for p, axis in zip(out_far, "yx")]
        out_far_b = [links.shift(p, axis, -1) for p, axis in zip(out_far_b, "xy")]
        b_parts = z_parts(add_far(b_far, done["bn", 0][1::2]))
        b_sum = b_parts[-1]
        for part in b_parts[-2:0:-1]:
            b_sum = plus(links.shift(b_sum, "z", -1), part)
    else:
        x_all, g_kept, act_all, grad_pre_all = kept
        grad_w_top = matmul_left_t(x_all[:, : D // 2], grad_pre_all)
        *b_far, a_sum, heads_far[0], heads_far[1], _ = tie(*b_far, a_sum, *heads_far, grad_w_top)
        b_parts = z_parts(add_far(b_far, done["bn", 0][1::2]))
        a_sum = plus(a_sum, a_parts[-2])
        x_all, a_sum, out_far[0], out_far[1], *b_parts = tie(x_all, a_sum, *out_far, *b_parts)
        out_far = [links.shift(p, axis, -1) for p, axis in zip(out_far, "yx")]
        a_next = links.shift(a_sum, "z", -1)
        b_next = links.shift(b_parts[-1], "z", -1)
        grad_w_end = matmul_left_t(x_all[:, D // 2 :], grad_pre_all)
        a_next, b_next, _ = tie(a_next, b_next, grad_w_end)
        for part in a_parts[-3:0:-1]:
            a_sum = plus(a_next, part)
            a_next = links.shift(a_sum, "z", -1)
        b_sum = plus(b_next, b_parts[-2])
        act_all, a_sum, b_sum = tie(act_all, a_sum, b_sum)
        b_next = links.shift(b_sum, "z", -1)
        out_far_b = [links.shift(p, axis, -1) for p, axis in zip(out_far_b, "xy")]
        grad_w_back = matmul_left_t(act_all, g_kept)
        a_next, b_next, *out_far, _ = tie(a_next, b_next, *out_far, grad_w_back)
        a_sum = plus(a_next, a_parts[0])
        b_sum = plus(b_next, b_parts[-3])
        for part in b_parts[-4:0:-1]:
            b_sum = plus(links.shift(b_sum, "z", -1), part)
        grad_w_top, grad_w_end, grad_w_back, b_sum = tie(
            grad_w_top, grad_w_end, grad_w_back, b_sum
        )
    out_near, out_far = split_far(add_far(out_far, [done["an", 0][0], done["an", 0][2]]))
    out_far = [links.shift(p, axis, -1) for p, axis in zip(out_far, "xy")]
    out_near_b = add_far(out_far_b, [done["bn", 0][0], done["bn", 0][2]])
    b_sum = plus(links.shift(b_sum, "z", -1), b_parts[0])
    grad_ffn = joined_rows([a_sum, *last_b(b_sum)])
    out_far[0], out_far[1], out_near_b[0], out_near_b[1], grad_ffn = tie(
        *out_far, *out_near_b, grad_ffn
    )
    grad_ffn = grad_ffn.astype(f32)

    def output_steps():
        parts = [
            joined_rows(p)
            for p in zip(z_parts(add_far(out_far, out_near)), z_parts(out_near_b))
        ]
        total = parts[-1]
        for part in parts[-2::-1]:
            moved_total = links.shift(total, "z", -1)
            yield [moved_total]
            total = plus(moved_total, part)
        rows = total.shape[0] // 3
        yield [joined_rows([total[:rows], *last_b(total[rows:])])]

    out_steps = output_steps()
    out_now = next(out_steps)
    def pick(value, start, count):
        return jnp.concatenate(
            [value[:, start : start + count], value[:, half_all + start : half_all + start + count]],
            axis=1,
        )

    blocks_in = [grad_w_in] if lean else [grad_w_top, grad_w_end]
    grad_w_expert_in = joined_rows([pick(v, 0, half_ff) for v in blocks_in])
    grad_w_expert_out = grad_w_back[:half_ff]
    grad_w_shared_out = grad_w_back[half_ff : half_ff + half_sh]
    grad_shared = joined_rows([pick(v, half_ff, half_sh) for v in blocks_in])
    grad_shared = grad_shared.reshape(devices, rows_d, 2 * half_sh)
    grad_out = cotangent.astype(f32)
    grad_middle_part, grad_norm_ffn = rms_backward(middle, inverse_ffn, gain_ffn, grad_ffn)
    grad_middle = grad_out + grad_middle_part
    grad_attended = grad_middle.astype(bf16)
    grad_heads_all = matmul_right_t(grad_attended, out_w).astype(bf16)
    pieces = [
        jnp.concatenate(
            [columns(grad_heads_all, k, v_cols), columns(grad_attended, k, D // ctx)], axis=1
        )
        for k in range(ctx)
    ]
    arrived = jnp.concatenate(links.ctx_exchange(pieces), axis=0)
    arrived, grad_shared, *out_now = tie(arrived, grad_shared, *out_now)
    grad_shared = lax.all_to_all(grad_shared, BOTH, split_axis=0, concat_axis=0, tiled=True)
    grad_shared = grad_shared.transpose(1, 0, 2)
    grad_w_shared_in = jnp.concatenate(
        [
            grad_shared[:, :, :half_sh].reshape(rows_d, SHARED_FF),
            grad_shared[:, :, half_sh:].reshape(rows_d, SHARED_FF),
        ],
        axis=1,
    )
    out_now = next(out_steps)
    grad_heads = arrived[:, :v_cols].reshape(row, heads, VDIM).transpose(1, 0, 2)
    grad_attended_cols = arrived[:, v_cols:]
    quarter = tok // 2
    parts = [heads_half[0][:quarter], heads_half[1][:quarter]]
    parts += [heads_half[0][quarter:], heads_far[1][:quarter]]
    parts += [heads_far[0][:quarter], heads_half[1][quarter:]]
    parts += [heads_far[0][quarter:], heads_far[1][quarter:]]
    heads_out_row = joined_rows(parts)
    if links.size["w"] > 1:
        heads_out_row = links.gather(heads_out_row, ("w",))

    soft = jnp.exp(masked_scores() - log_total)
    grad_values = jnp.einsum(
        "hqk,hqd->hkd", soft.astype(bf16), grad_heads, preferred_element_type=f32
    )
    grad_probs = jnp.einsum("hqd,hkd->hqk", grad_heads, value, preferred_element_type=f32)
    row_delta = jnp.sum(soft * grad_probs, axis=-1, keepdims=True)
    grad_raw = (soft * (grad_probs - row_delta) * scale).astype(bf16)
    grad_raw, grad_values, *out_now = tie(grad_raw, grad_values, *out_now)
    out_now = next(out_steps)
    grad_query = jnp.einsum("hqk,hkd->qhd", grad_raw, key, preferred_element_type=f32)
    grad_key = jnp.einsum("hqk,hqd->khd", grad_raw, query, preferred_element_type=f32)
    grad_key_rope = jnp.sum(grad_key[..., NOPE:], axis=1)
    grad_keyval = jnp.concatenate(
        [grad_key[..., :NOPE], grad_values.transpose(1, 0, 2)], axis=-1
    )
    grad_keyval = grad_keyval.astype(bf16).reshape(row, kv_cols)
    grad_keyval, *out_now = tie(grad_keyval, *out_now)
    mixed = (middle + list(out_steps)[-1][0].astype(f32)).astype(bf16)
    grad_w_up = matmul_left_t(latent, grad_keyval)
    grad_latent = matmul_right_t(grad_keyval, up_w)
    grad_low = jnp.concatenate([grad_latent, grad_key_rope], axis=1).astype(bf16)
    grad_low = links.scatter_sum(grad_low, ("x", "y", "w")).astype(f32)
    grad_query_raw = jnp.concatenate(
        [
            grad_query[..., :NOPE],
            unrotate(grad_query[..., NOPE:], cosine[:, None, :], sine_part[:, None, :]),
        ],
        axis=-1,
    )
    grad_query_raw = grad_query_raw.astype(bf16).reshape(ctx, tok, q_cols)
    query_back = jnp.stack(links.ctx_exchange([grad_query_raw[k] for k in range(ctx)]))
    query_back = query_back[ctx_place].transpose(1, 0, 2).reshape(tok, ctx * q_cols)
    grad_compressed_latent, grad_norm_latent = rms_backward(
        raw_latent[:tok], inverse_latent[:tok], gain_latent, grad_low[:, :LATENT]
    )
    grad_compressed = jnp.concatenate(
        [
            grad_compressed_latent,
            unrotate(grad_low[:, LATENT:], cosine[:tok], sine_part[:tok]),
        ],
        axis=1,
    ).astype(bf16)
    grad_normed = matmul_right_t(grad_compressed, down_w) + matmul_right_t(
        query_back, query_w_all
    )
    grad_input_part, grad_norm_attn = rms_backward(
        inputs, inverse_row[:tok], gain_attn, grad_normed
    )
    grad_in = grad_middle + grad_input_part

    def to_owners(value):
        count, size = value.shape[1], links.size["z"]
        value = value.astype(bf16).reshape(size, 2, ctx * count, -1)

        def core(c):
            return lax.dynamic_index_in_dim(value, c, 1, keepdims=False)

        total = plus(links.shift(core(1 - links.own["c"]), "c"), core(links.own["c"]))

        def part(k):
            return lax.dynamic_index_in_dim(
                total, (links.own["z"] - k) % size, 0, keepdims=False
            )

        summed = part(size - 1)
        for k in range(size - 2, -1, -1):
            summed = plus(links.shift(summed, "z", -1), part(k))
        summed = summed.reshape(ctx, count, -1)
        pieces = [
            lax.dynamic_index_in_dim(summed, rel_ctx[k], 0, keepdims=False) for k in range(ctx)
        ]
        return jnp.stack(links.ctx_exchange(pieces))[ctx_place].astype(f32)

    def joined(value):
        return value.transpose(1, 0, 2).reshape(value.shape[1], -1)

    grad_out_cols = matmul_left_t(heads_out_row, grad_attended_cols)
    grad_w_out = joined(to_owners(grad_out_cols.reshape(devices, rows_d, D // ctx)))
    grad_w_q = matmul_left_t(normed_row, grad_query_raw.reshape(row, q_cols))
    grad_w_up = grad_w_up.astype(bf16).reshape(devices, rows_l, up_parts, up_fold)
    grad_w_up = grad_w_up.transpose(0, 2, 1, 3).reshape(devices, rows_d, up_fold)
    heads_grads = to_owners(
        jnp.concatenate(
            [grad_w_q.astype(bf16).reshape(devices, rows_d, q_cols), grad_w_up], axis=2
        )
    )
    grad_w_query = joined(heads_grads[:, :, :q_cols])
    grad_w_kv_up = heads_grads[:, :, q_cols:].reshape(ctx, up_parts, rows_l, up_fold)
    grad_w_kv_up = grad_w_kv_up.transpose(2, 0, 1, 3).reshape(rows_l, ctx * kv_cols)

    compressed_cols = jnp.concatenate(
        links.ctx_exchange([columns(grad_compressed, k, dn_cols) for k in range(ctx)]), axis=0
    )
    grad_w_down = matmul_left_t(normed_row, compressed_cols).astype(bf16)
    vectors = jnp.stack(
        [
            jnp.pad(v.reshape(devices, -1), ((0, 0), (0, dn_cols - v.size // devices)))
            for v in (grad_norm_attn, grad_norm_ffn, grad_norm_latent)
        ],
        axis=1,
    )
    vectors = jnp.pad(vectors, ((0, 0), (0, 13), (0, 0))).astype(bf16)
    last_grads = to_owners(
        jnp.concatenate([grad_w_down.reshape(devices, rows_d, dn_cols), vectors], axis=1)
    )
    grad_w_kv_down = joined(last_grads[:, :rows_d])
    vector_sums = jnp.sum(last_grads[:, rows_d : rows_d + 3], axis=0)
    return (
        mixed,
        grad_in,
        vector_sums[0, :rows_d],
        grad_w_query,
        grad_w_kv_down,
        vector_sums[2, :rows_l],
        grad_w_kv_up,
        grad_w_out,
        vector_sums[1, :rows_d],
        grad_w_shared_in,
        grad_w_shared_out,
        grad_w_expert_in[None],
        grad_w_expert_out[None],
    )


def solution(mesh):
    rows = P(BOTH, None)
    vector = P(BOTH)
    experts = P(BOTH, None, None)
    return jax.shard_map(
        shards,
        mesh=mesh,
        in_specs=(
            rows,
            P("dp"),
            rows,
            rows,
            rows,
            vector,
            rows,
            rows,
            vector,
            rows,
            rows,
            vector,
            rows,
            rows,
            experts,
            experts,
        ),
        out_specs=(
            rows,
            rows,
            vector,
            rows,
            rows,
            vector,
            rows,
            rows,
            vector,
            rows,
            rows,
            experts,
            experts,
        ),
        check_vma=False,
    )
```

```python
import math

import jax
import jax.numpy as jnp
from jax import lax
from jax.experimental import pallas as pl
from jax.experimental.pallas import tpu as pltpu
from jax.sharding import PartitionSpec as P

D = 2048
HEADS = 16
NOPE = 128
ROPE = 64
VDIM = 128
LATENT = 512
EXPERT_FF = 1408
SHARED_FF = 2816
TOP = 6

BOTH = ("dp", "ctx")
epsilon = 1e-06
f32 = jnp.float32
bf16 = jnp.bfloat16


def matmul(left, right):
    return jnp.dot(left, right, preferred_element_type=f32)


def matmul_left_t(left, right):
    return lax.dot_general(left, right, (((0,), (0,)), ((), ())), preferred_element_type=f32)


def matmul_right_t(left, right):
    return lax.dot_general(left, right, (((1,), (1,)), ((), ())), preferred_element_type=f32)


def rope_tables(positions, rope_width):
    half_width = rope_width // 2
    frequency = jnp.exp(
        -math.log(10000.0) * jnp.arange(half_width).astype(f32) / half_width
    )
    angles = positions.astype(f32)[:, None] * frequency[None, :]
    return (jnp.cos(angles), jnp.sin(angles))


def rotate(operand, cosine, sine_part):
    half_width = operand.shape[-1] // 2
    first_half = operand[..., :half_width]
    second_half = operand[..., half_width:]
    return jnp.concatenate(
        [
            first_half * cosine - second_half * sine_part,
            second_half * cosine + first_half * sine_part,
        ],
        axis=-1,
    )


def unrotate(operand, cosine, sine_part):
    return rotate(operand, cosine, -sine_part)


def swish(operand):
    return operand * jax.nn.sigmoid(operand)


def swish_slope(operand):
    sigma = jax.nn.sigmoid(operand)
    return sigma * (1.0 + operand * (1.0 - sigma))


def rms_inverse(operand):
    return lax.rsqrt(jnp.mean(operand * operand, axis=-1, keepdims=True) + epsilon)


def rms_backward(operand, inverse, gain_vec, grad_out):
    scaled = grad_out * gain_vec
    grad_gain = jnp.sum(grad_out * operand * inverse, axis=0)
    grad_operand = inverse * scaled - operand * inverse * inverse * inverse * jnp.mean(
        scaled * operand, axis=-1, keepdims=True
    )
    return (grad_operand, grad_gain)


class Links:
    def __init__(self):
        self.dp = lax.axis_size("dp")
        self.ctx = lax.axis_size("ctx")
        self.size = {"z": self.dp // 2, "c": 2, "w": self.ctx // 4, "y": 2, "x": 2}
        dp = lax.axis_index("dp").astype(jnp.uint32)
        self.place = ctx = lax.axis_index("ctx").astype(jnp.uint32)
        self.own = {
            "z": dp >> 1,
            "c": dp & 1,
            "w": ctx >> 2,
            "y": (ctx >> 1) & 1,
            "x": ctx & 1,
        }

    def minus(self, axis, steps):
        return (self.own[axis] - steps) & (self.size[axis] - 1)

    def ctx_at(self, k):
        return self.minus("w", jnp.uint32(k // 4)) * 4 + ((self.place ^ jnp.uint32(k)) & 3)

    def shift(self, value, axis, by=1):
        name, count = ("dp", self.dp) if axis in "zc" else ("ctx", self.ctx)
        if axis == "z":
            pairs = [(i, (i + 2 * by) % count) for i in range(count)]
        elif axis == "w":
            pairs = [(i, (i + 4 * by) % count) for i in range(count)]
        else:
            pairs = [(i, i ^ (2 if axis == "y" else 1)) for i in range(count)]
        return lax.ppermute(value, name, pairs)

    def shift_ctx(self, value, k):
        pairs = [
            (i, (i // 4 - k // 4) % self.size["w"] * 4 + (i ^ k) % 4) for i in range(self.ctx)
        ]
        return lax.ppermute(value, "ctx", pairs)

    def ring(self, block, axis):
        held = [block]
        for _ in range(self.size[axis] - 1):
            held.append(self.shift(held[-1], axis))
        return held

    def gather(self, block, order):
        for axis in order:
            block = joined_rows(self.ring(block, axis))
        return block

    def reduce(self, parts, axis):
        total = parts[-1]
        for part in parts[-2::-1]:
            total = plus(self.shift(total, axis, -1), part)
        return total

    def scatter_sum(self, block, order):
        for axis in order[::-1]:
            block = self.reduce(jnp.split(block, self.size[axis]), axis)
        return block

    def device_of(self, order):
        place = dict(self.own)
        depth = len(order)
        for i, axis in enumerate(order):
            shape = [1] * depth
            shape[depth - 1 - i] = self.size[axis]
            place[axis] = self.minus(
                axis, jnp.arange(self.size[axis], dtype=jnp.uint32).reshape(shape)
            )
        number = (place["z"] * 2 + place["c"]) * self.ctx
        number = number + place["w"] * 4 + place["y"] * 2 + place["x"]
        return number.reshape(-1)

    def place_of(self, order):
        number = jnp.arange(self.dp * self.ctx, dtype=jnp.uint32)
        coordinate = {
            "x": number & 1,
            "y": (number >> 1) & 1,
            "w": (number >> 2) & (self.size["w"] - 1),
            "c": (number // self.ctx) & 1,
            "z": number // (2 * self.ctx),
        }
        place = jnp.zeros_like(number)
        for axis in order[::-1]:
            place = place * self.size[axis] + self.minus(axis, coordinate[axis])
        return place

    def ctx_place(self):
        number = jnp.arange(self.ctx, dtype=jnp.uint32)
        return self.minus("w", number >> 2) * 4 + ((self.place ^ number) & 3)

    def ctx_exchange(self, pieces):
        result = [pieces[0]] + [None] * (self.ctx - 1)
        for k in range(1, self.ctx):
            back = (-(k // 4)) % self.size["w"] * 4 + k % 4
            result[back] = self.shift_ctx(pieces[k], k)
        return result


def joined_rows(parts):
    return parts[0] if len(parts) == 1 else jnp.concatenate(parts, axis=0)


def plus(left, right):
    return (left.astype(f32) + right.astype(f32)).astype(bf16)


def tie(*values):
    return lax.optimization_barrier(values)


def after(value, *others):
    return lax.optimization_barrier((value,) + others)[0]


GROUP = 4


def ffn_kernel(half_ff, parts, part_steps, sources, x_ref, *refs):
    g_refs, (m_ref, w_in, w_out) = refs[:GROUP], refs[GROUP : GROUP + 3]
    refs = refs[GROUP + 3 :]
    if parts:
        moved, refs = refs[0], refs[1:]
    outs = refs[-max(2 * parts, 1) :]
    x_all, g_all, act, grad_pre = refs[-len(outs) - 4 : -len(outs)]
    half_all = act.shape[1]
    count = x_ref.shape[0] // GROUP
    x_all[...] = x_ref[...]
    for i, g_ref in enumerate(g_refs):
        g_all[i * count : (i + 1) * count] = g_ref[0]
    pre = matmul(x_ref[...], w_in[...])
    gate, up = pre[:, :half_all], pre[:, half_all:]
    column = lax.broadcasted_iota(jnp.int32, (1, half_all), 1)
    weight = jnp.where(column < half_ff, m_ref[...], 1.0)
    sigma = jax.nn.sigmoid(gate)
    swished = gate * sigma
    act[...] = (swished * up * weight).astype(bf16)
    grad_act = matmul_right_t(g_all[...], w_out[...]) * weight
    slope = sigma * (1.0 + gate * (1.0 - sigma))
    grad_pre[:, :half_all] = (grad_act * up * slope).astype(bf16)
    grad_pre[:, half_all:] = (grad_act * swished).astype(bf16)
    out_part = matmul(act[...], w_out[...])
    grad_part = matmul_right_t(grad_pre[...], w_in[...])
    if not parts:
        outs[0][:, :D] = out_part.astype(bf16)
        outs[0][:, D:] = grad_part.astype(bf16)
        return
    out_part = (out_part + moved[:, :D].astype(f32)).astype(bf16)
    grad_part = (grad_part + moved[:, D:].astype(f32)).astype(bf16)
    for k in range(parts):

        @pl.when(pl.program_id(0) // part_steps == k)
        def _():
            outs[2 * k][...] = out_part
            outs[2 * k + 1][...] = grad_part


def ffn_chunk(x, g_blocks, m, w_in, w_out, half_ff, sources, group, far, side, kept, moved, lean):
    half_all = w_out.shape[0]
    tokens = m.shape[0]
    count = tokens // sources.shape[0]
    tile = GROUP * count
    steps = x.shape[0] // tile
    parts = 4 if far == 2 else 2
    half = steps // parts
    per_slice = 4 * half
    base = 2 * group * per_slice + (2 * side + far % 2) * half

    def second(i):
        return (i // half) % 2

    def place(i):
        return base + i % half + second(i) * per_slice + i // (2 * half) * half

    def rows(width):
        return pl.BlockSpec((tile, width), lambda i, _: (i, 0))

    def kept_rows(width):
        return pl.BlockSpec((tile, width), lambda i, _: (i if lean else place(i), 0))

    def whole(value):
        return pl.BlockSpec(value.shape, lambda i, _: (0, 0), pipeline_mode=pl.Buffered(1))

    def g_spec(j):
        def index(i, s):
            return (s[GROUP * place(i) + j], 2 * group + second(i), 0)

        return pl.BlockSpec((1, count, D), index)

    operands = [sources, x] + [g_blocks] * GROUP + [m, w_in, w_out]
    in_specs = [rows(D)] + [g_spec(j) for j in range(GROUP)]
    in_specs += [pl.BlockSpec((tile, 1), lambda i, _: (place(i), 0)), whole(w_in), whole(w_out)]
    out_specs = [rows(2 * D)]
    out_shape = [jax.ShapeDtypeStruct((x.shape[0], 2 * D), bf16)]
    if moved is not None:
        operands.append(moved)
        in_specs.append(rows(2 * D))

        def part_spec(k):
            return pl.BlockSpec(
                (tile, D), lambda i, _: (jnp.clip(i - k * half, 0, half - 1), 0)
            )

        out_specs = [part_spec(k // 2) for k in range(2 * parts)]
        out_shape = [jax.ShapeDtypeStruct((half * tile, D), bf16)] * (2 * parts)
    aliases = {}
    if kept is not None:
        aliases = {len(operands) + i: i for i in range(4)}
        operands += kept
        in_specs += [pl.BlockSpec(memory_space=pl.ANY)] * 4
    widths = (D, D, half_all, 2 * half_all)
    kept_count = x.shape[0] if lean else tokens
    flops = 2 * x.shape[0] * D * 6 * half_all
    result = pl.pallas_call(
        lambda *refs: ffn_kernel(half_ff, 0 if moved is None else parts, half, *refs),
        grid_spec=pltpu.PrefetchScalarGridSpec(
            num_scalar_prefetch=1,
            grid=(steps,),
            in_specs=in_specs,
            out_specs=[kept_rows(w) for w in widths] + out_specs,
        ),
        out_shape=[jax.ShapeDtypeStruct((kept_count, w), bf16) for w in widths] + out_shape,
        input_output_aliases=aliases,
        compiler_params=pltpu.CompilerParams(vmem_limit_bytes=60 * 2**20),
        cost_estimate=pl.CostEstimate(
            flops=flops, bytes_accessed=x.shape[0] * D * 16, transcendentals=0
        ),
        name="ffn_chunk",
    )(*operands)
    return list(result[:4]), list(result[4:])


def shards(
    hidden_in,
    segments,
    routes,
    gates,
    cotangent,
    norm_attn,
    w_query,
    w_kv_down,
    norm_latent,
    w_kv_up,
    w_out,
    norm_ffn,
    w_shared_in,
    w_shared_out,
    w_expert_in,
    w_expert_out,
):
    links = Links()
    tok = hidden_in.shape[0]
    row = segments.shape[0]
    ctx = links.ctx
    devices = links.dp * ctx
    half_ff = EXPERT_FF // 2
    half_sh = w_shared_out.shape[0]
    half_all = -(-(half_ff + half_sh) // 128) * 128
    heads = HEADS // ctx
    q_cols = heads * (NOPE + ROPE)
    v_cols = heads * VDIM
    kv_cols = heads * (NOPE + VDIM)
    dn_cols = (LATENT + ROPE) // ctx
    rows_d = w_query.shape[0]
    rows_l = w_kv_up.shape[0]
    up_fold = rows_l * kv_cols // rows_d
    up_parts = rows_d // rows_l
    scale = 1.0 / math.sqrt(NOPE + ROPE)
    rel_ctx = [links.ctx_at(k) for k in range(ctx)]
    ctx_place = links.ctx_place()

    def columns(value, k, width):
        return lax.dynamic_slice_in_dim(value, rel_ctx[k] * width, width, 1)

    latent_gain = jnp.zeros((rows_d,), bf16).at[:rows_l].set(norm_latent)
    small = jnp.concatenate(
        [w_kv_down, norm_attn[:, None], norm_ffn[:, None], latent_gain[:, None]], axis=1
    )
    small = jnp.pad(small, ((0, 0), (0, -small.shape[1] % 128)))
    small_cols = small.shape[1]
    small = jnp.concatenate([small, w_out], axis=1)
    pieces = []
    for k in range(ctx):
        folded = columns(w_kv_up, k, kv_cols).reshape(rows_l, up_parts, up_fold)
        folded = folded.transpose(1, 0, 2).reshape(rows_d, up_fold)
        pieces.append(jnp.concatenate([columns(w_query, k, q_cols), folded], axis=1))
    hidden_parts = links.ctx_exchange([hidden_in] * ctx)
    step, *received = tie(links.shift(small, "z"), *links.ctx_exchange(pieces))
    heads_w = joined_rows(received)
    small_parts, heads_parts = [small, step], [heads_w]
    for i in range(links.size["z"] - 1):
        pair = [links.shift(heads_parts[-1], "z")]
        if i < links.size["z"] - 2:
            pair.append(links.shift(small_parts[-1], "z"))
        else:
            small_all = links.gather(joined_rows(small_parts), ("w",))
            small_all = small_all.reshape(-1, 2, rows_d // 2, small.shape[1])
            small_a = small_all[:, 0].reshape(-1, small.shape[1])
            small_b = small_all[:, 1].reshape(-1, small.shape[1])
            pair += [links.shift(small_a, "x"), links.shift(small_b, "y")]
        pair = list(tie(*pair))
        if i < links.size["z"] - 2:
            small_parts.append(pair[1])
        if i == 0:
            w_shared_in, _ = tie(w_shared_in, pair[0])
        if i == links.size["z"] - 3:
            pair[0], *hidden_parts = tie(pair[0], *hidden_parts)
            hidden_row = joined_rows(hidden_parts)
        heads_parts.append(pair[0])
    small_a, small_b = joined_rows([small_a, pair[1]]), joined_rows([small_b, pair[2]])
    heads_w = joined_rows(heads_parts)
    heads_c = links.shift(heads_w, "c")
    last_a, last_b = small_a[:, small_cols:], small_b[:, small_cols:]
    small_a, small_b = small_a[:, :small_cols], small_b[:, :small_cols]
    shared_pieces = jnp.concatenate(
        [
            w_shared_in[:, :SHARED_FF].reshape(rows_d, devices, half_sh),
            w_shared_in[:, SHARED_FF:].reshape(rows_d, devices, half_sh),
        ],
        axis=2,
    ).transpose(1, 0, 2)
    shared_w = lax.all_to_all(shared_pieces, BOTH, split_axis=0, concat_axis=0, tiled=True)
    far_a, far_b, shared_w = tie(links.shift(small_a, "y"), links.shift(small_b, "x"), shared_w)
    small_all = joined_rows([small_a, far_a, small_b, far_b])
    small_all = joined_rows([small_all, links.shift(small_all, "c")])
    heads_w = joined_rows([heads_w, heads_c]).reshape(devices, rows_d, q_cols + up_fold)
    blocks = devices // 2
    place_a = links.place_of(("z", "w", "x", "y", "c"))
    place_b = links.place_of(("z", "w", "y", "x", "c"))
    take_a = (place_a // blocks) * 2 * blocks + place_a % blocks
    take_b = (place_b // blocks) * 2 * blocks + blocks + place_b % blocks
    take = jnp.stack([take_a, take_b], axis=1).reshape(-1)
    small_all = small_all.reshape(2 * devices, rows_d // 2, small_cols)[take]
    small_all = small_all.reshape(devices, rows_d, small_cols)
    down_w = small_all[:, :, : LATENT + ROPE].reshape(D, LATENT + ROPE)
    gain_attn = small_all[:, :, LATENT + ROPE].reshape(D).astype(f32)
    gain_ffn = small_all[:, :, LATENT + ROPE + 1].reshape(D).astype(f32)
    gain_latent = small_all[:, :rows_l, LATENT + ROPE + 2].reshape(LATENT).astype(f32)

    heads_place = links.place_of(("x", "y", "w", "z", "c"))
    heads_w = heads_w[heads_place]
    query_w = heads_w[:, :, :q_cols].reshape(D, q_cols)
    up_w = heads_w[:, :, q_cols:].reshape(devices, up_parts, rows_l, up_fold)
    up_w = up_w.transpose(0, 2, 1, 3).reshape(LATENT, kv_cols)

    orders = (
        ("z", "w", "x", "y"),
        ("z", "w", "y", "x"),
        ("y", "z", "w", "x"),
        ("x", "z", "w", "y"),
    )
    slices = len(orders)
    count = tok // slices
    tokens = devices * tok
    source_list = [links.device_of(order + ("c",)) for order in orders]
    sources = jnp.concatenate(source_list).astype(jnp.int32)
    m_place = jnp.concatenate([d * slices + i for i, d in enumerate(source_list)])
    hidden_row, query_w, up_w, down_w = tie(hidden_row, query_w, up_w, down_w)
    g_all = lax.all_gather(after(cotangent, far_a), BOTH, axis=0, tiled=True)
    g_blocks = g_all.reshape(devices, tok, D)

    inputs_row = hidden_row.astype(f32)
    inverse_row = rms_inverse(inputs_row)
    normed_row = (inputs_row * inverse_row * gain_attn).astype(bf16)
    rel_numbers = jnp.stack(rel_ctx)
    positions = rel_numbers.astype(jnp.int32)[:, None] * tok
    positions = (positions + jnp.arange(tok, dtype=jnp.int32)[None, :]).reshape(-1)
    row_segments = segments.reshape(ctx, tok)[rel_numbers].reshape(-1)
    allowed = (positions[None, :] <= positions[:, None]) & (
        row_segments[None, :] == row_segments[:, None]
    )
    cosine, sine_part = rope_tables(positions, ROPE)
    query_raw = matmul(normed_row, query_w).reshape(row, heads, NOPE + ROPE)
    query = jnp.concatenate(
        [
            query_raw[..., :NOPE],
            rotate(query_raw[..., NOPE:], cosine[:, None, :], sine_part[:, None, :]),
        ],
        axis=-1,
    ).astype(bf16)
    query = query.transpose(1, 0, 2)
    compressed = matmul(normed_row, down_w)
    raw_latent = compressed[:, :LATENT]
    inverse_latent = rms_inverse(raw_latent)
    latent = (raw_latent * inverse_latent * gain_latent).astype(bf16)
    key_rope = rotate(compressed[:, LATENT:], cosine, sine_part).astype(bf16)
    keyval = matmul(latent, up_w).astype(bf16).reshape(row, heads, NOPE + VDIM)
    last_a, last_b = tie(last_a, last_b, far_a)[:2]
    last_y, last_x, keyval = tie(links.shift(last_a, "y"), links.shift(last_b, "x"), keyval)
    out_w = joined_rows([last_a, last_y, last_b, last_x])
    out_w = joined_rows([out_w, links.shift(out_w, "c")])
    out_w = out_w.reshape(2 * devices, rows_d // 2, D)[take].reshape(D, D)
    keyval = keyval.transpose(1, 0, 2)
    key = jnp.concatenate(
        [keyval[..., :NOPE], jnp.broadcast_to(key_rope[None], (heads, row, ROPE))], axis=-1
    )
    value = keyval[..., NOPE:]

    def masked_scores():
        raw = jnp.einsum("hqd,hkd->hqk", query, key, preferred_element_type=f32)
        return jnp.where(allowed[None], raw * scale, -1e30)

    scores = masked_scores()
    row_max = jnp.max(scores, axis=-1, keepdims=True)
    exponent = jnp.exp(scores - row_max)
    row_total = jnp.sum(exponent, axis=-1, keepdims=True)
    log_total = row_max + jnp.log(row_total)
    probs = (exponent / row_total).astype(bf16)
    heads_part = jnp.einsum("hqk,hkd->qhd", probs, value, preferred_element_type=f32)
    heads_part = heads_part.astype(bf16).reshape(ctx, tok, v_cols)
    returned = jnp.stack(links.ctx_exchange([heads_part[k] for k in range(ctx)]))
    heads_out = returned[ctx_place].transpose(1, 0, 2).reshape(tok, HEADS * VDIM)
    inputs = hidden_in.astype(f32)
    middle = inputs + matmul(heads_out, out_w)
    inverse_ffn = rms_inverse(middle)
    ffn_in = (middle * inverse_ffn * gain_ffn).astype(bf16)

    cut = [ffn_in[i * count : (i + 1) * count] for i in range(slices)]

    def halved(parts):
        both = [jnp.split(part, 2) for part in parts]
        return [joined_rows([pair[i] for pair in both]) for i in range(2)]

    held = joined_rows(cut[:2])
    heads_half = [heads_out[: tok // 2], heads_out[tok // 2 :]]
    near_y, near_x, first, shared_w, w_expert_in, routes, gates = tie(
        links.shift(cut[2], "y"),
        links.shift(cut[3], "x"),
        links.shift(held, "z"),
        shared_w,
        w_expert_in,
        routes,
        gates,
    )
    experts = devices // 2
    expert_number = jnp.arange(experts, dtype=jnp.int32)[:, None, None]
    gate_matrix = jnp.sum(
        jnp.where(routes.T[None] == expert_number, gates.T[None], 0.0), axis=1
    )
    m_all = lax.all_to_all(
        jnp.repeat(gate_matrix, 2, axis=0), BOTH, split_axis=0, concat_axis=0, tiled=True
    )
    shared_w = shared_w.reshape(D, 2 * half_sh)
    pad = half_all - half_ff - half_sh
    w_in = jnp.concatenate(
        [
            w_expert_in[0][:, :half_ff],
            jnp.pad(shared_w[:, :half_sh], ((0, 0), (0, pad))),
            w_expert_in[0][:, half_ff:],
            jnp.pad(shared_w[:, half_sh:], ((0, 0), (0, pad))),
        ],
        axis=1,
    )
    w_back = jnp.concatenate(
        [w_expert_out[0], jnp.pad(w_shared_out, ((0, pad), (0, 0)))], axis=0
    )
    m = m_all.reshape(devices * slices, count)[m_place].reshape(tokens, 1)
    ring_a = [held, first]
    heads_far = [links.shift(heads_half[0], "x"), links.shift(heads_half[1], "y")]
    while len(ring_a) < links.size["z"]:
        step, *heads_far = tie(links.shift(ring_a[-1], "z"), *heads_far)
        if len(ring_a) == 2:
            heads_half = [joined_rows(p) for p in zip(heads_half, heads_far)]
            heads_far = [links.shift(heads_half[0], "y"), links.shift(heads_half[1], "x")]
        ring_a.append(step)
    held = links.gather(joined_rows(ring_a), ("w",)) if links.size["w"] > 1 else None
    slice_0, slice_1 = halved(jnp.split(held, ctx // 4 * links.size["z"]) if held is not None else ring_a)
    held = joined_rows([cut[2], near_y, cut[3], near_x])
    held, slice_0, slice_1, w_in, w_back, m = tie(held, slice_0, slice_1, w_in, w_back, m)
    ring_b = [held]
    moved_0, moved_1, step = tie(
        links.shift(slice_0, "x"), links.shift(slice_1, "y"), links.shift(held, "z")
    )
    ring_b.append(step)
    near_a = [joined_rows([slice_0, moved_0]), joined_rows([slice_1, moved_1])]
    far_a = [links.shift(near_a[0], "y"), links.shift(near_a[1], "x")]
    near_a_rows = joined_rows(near_a)
    near_a_sib = links.shift(near_a_rows, "c")

    lean = devices > 32
    kept = None
    done, moved = {}, {}

    def ffn(rows, name, side):
        kept_now, parts = ffn_chunk(
            rows,
            g_blocks,
            m,
            w_in,
            w_back,
            half_ff,
            sources,
            "ab".index(name[0]),
            ("n", "f", "").index(name[1:]),
            side,
            None if lean else kept,
            moved.get(name) if side == 0 else None,
            lean,
        )
        if side == 1:
            moved[name] = links.shift(parts[0], "c", -1)
        done[name, side] = parts
        if lean:
            sums = [
                matmul_left_t(kept_now[0], kept_now[3]),
                matmul_left_t(kept_now[2], kept_now[1]),
            ]
            return sums if kept is None else [a + b for a, b in zip(kept, sums)]
        return kept_now

    near_a_sib, step = tie(near_a_sib, links.shift(ring_b[-1], "z"))
    ring_b.append(step)
    step = links.shift(ring_b[-1], "z")
    kept = ffn(near_a_sib, "an", 1)
    step, *far_a = tie(step, *far_a, done["an", 1][0])[:3]
    far_a_rows = joined_rows(far_a)
    far_a_sib = links.shift(far_a_rows, "c")
    ring_b.append(step)
    far_a_sib, ring_b[-1] = tie(far_a_sib, ring_b[-1])
    while len(ring_b) < links.size["z"]:
        ring_b.append(links.shift(ring_b[-1], "z"))
    held = links.gather(joined_rows(ring_b), ("w",)) if links.size["w"] > 1 else None
    near_b = halved(jnp.split(held, ctx // 4 * links.size["z"]) if held is not None else ring_b)
    far_b = [links.shift(near_b[0], "x"), links.shift(near_b[1], "y")]
    kept = ffn(far_a_sib, "af", 1)
    kept = ffn(far_a_rows, "af", 0)
    near_a_rows, *far_b = tie(near_a_rows, *far_b, done["af", 0][0])[:3]
    rows_b = joined_rows([*near_b, *far_b])
    sib_b = links.shift(rows_b, "c")

    def add_far(moved_rows, near):
        return [plus(m_rows, n_rows) for m_rows, n_rows in zip(moved_rows, near)]

    def split_far(rows):
        pairs = [jnp.split(r, 2) for r in rows]
        return [p[0] for p in pairs], [p[1] for p in pairs]

    def z_parts(rows):
        if links.size["w"] > 1:
            rows = [links.scatter_sum(r, ("w",)) for r in rows]
        return [joined_rows(p) for p in zip(*[jnp.split(r, links.size["z"]) for r in rows])]

    def last_b(total):
        n0, f0, n1, f1 = jnp.split(total, 4)
        return plus(links.shift(f0, "y", -1), n0), plus(links.shift(f1, "x", -1), n1)

    far = done["af", 0][1::2]
    a_far = [links.shift(far[0], "y", -1), links.shift(far[1], "x", -1)]
    kept = ffn(near_a_rows, "an", 0)
    a_far = tie(*a_far, done["an", 0][0])[:2]
    a_near = add_far(a_far, done["an", 0][1::2])
    sib_b, *a_near = tie(sib_b, *a_near)
    a_near, far = split_far(a_near)
    a_far = [links.shift(far[0], "x", -1), links.shift(far[1], "y", -1)]
    query_w_all = lax.all_gather(after(w_query, sib_b), BOTH, axis=0, tiled=True)
    kept = ffn(sib_b, "b", 1)
    a_far = tie(*a_far, done["b", 1][0])[:2]
    a_parts = z_parts(add_far(a_far, a_near))
    rows_b, *a_parts = tie(rows_b, *a_parts)
    a_sum = links.shift(a_parts[-1], "z", -1)
    kept = ffn(rows_b, "b", 0)
    a_sum = after(a_sum, done["b", 0][0])
    done["bn", 0], done["bf", 0] = done["b", 0][:4], done["b", 0][4:]
    far = done["bf", 0][1::2]
    b_far = [links.shift(far[0], "x", -1), links.shift(far[1], "y", -1)]
    out_far = [done["af", 0][0], done["af", 0][2]]
    out_far_b = [done["bf", 0][0], done["bf", 0][2]]

    def send_outputs(far_rows, far_rows_b):
        near_rows, far_rows = split_far(add_far(far_rows, [done["an", 0][0], done["an", 0][2]]))
        return near_rows, [
            links.shift(joined_rows(pair), axis, -1)
            for pair, axis in zip(zip(far_rows, far_rows_b), "xy")
        ]

    if lean:
        grad_w_in, grad_w_back = kept
        a_sum = plus(a_sum, a_parts[-2])
        for part in a_parts[-3::-1]:
            a_sum = plus(links.shift(a_sum, "z", -1), part)
        out_far = [links.shift(p, axis, -1) for p, axis in zip(out_far, "yx")]
        out_near, out_sent = send_outputs(out_far, out_far_b)
        b_parts = z_parts(add_far(b_far, done["bn", 0][1::2]))
        b_sum = b_parts[-1]
        for part in b_parts[-2:0:-1]:
            b_sum = plus(links.shift(b_sum, "z", -1), part)
    else:
        x_all, g_kept, act_all, grad_pre_all = kept
        a_sum = plus(a_sum, a_parts[-2])
        x_all, a_sum = tie(x_all, a_sum)
        a_next = links.shift(a_sum, "z", -1)
        grad_w_top = matmul_left_t(x_all[:, : D // 2], grad_pre_all)
        *b_far, a_next, _ = tie(*b_far, a_next, grad_w_top)
        b_parts = z_parts(add_far(b_far, done["bn", 0][1::2]))
        a_sum = plus(a_next, a_parts[-3])
        x_all, a_sum, out_far[0], out_far[1], *b_parts = tie(x_all, a_sum, *out_far, *b_parts)
        out_far = [links.shift(p, axis, -1) for p, axis in zip(out_far, "yx")]
        a_next = links.shift(a_sum, "z", -1)
        b_next = links.shift(b_parts[-1], "z", -1)
        grad_w_end = matmul_left_t(x_all[:, D // 2 :], grad_pre_all)
        a_next, b_next, _ = tie(a_next, b_next, grad_w_end)
        a_sum = plus(a_next, a_parts[-4])
        b_sum = plus(b_next, b_parts[-2])
        act_all, a_sum, b_sum, *out_all = tie(act_all, a_sum, b_sum, *out_far, *out_far_b)
        out_near, out_sent = send_outputs(out_all[:2], out_all[2:])
        b_next = links.shift(b_sum, "z", -1)
        grad_w_back = matmul_left_t(act_all, g_kept)
        b_next, _ = tie(b_next, grad_w_back)
        b_sum = plus(b_next, b_parts[-3])
        for part in b_parts[-4:0:-1]:
            b_sum = plus(links.shift(b_sum, "z", -1), part)
        grad_w_top, grad_w_end, grad_w_back, b_sum = tie(
            grad_w_top, grad_w_end, grad_w_back, b_sum
        )
    b_sum = plus(links.shift(b_sum, "z", -1), b_parts[0])
    grad_ffn = joined_rows([a_sum, *last_b(b_sum)])
    out_sent[0], out_sent[1], grad_ffn = tie(*out_sent, grad_ffn)
    out_split = out_near[0].shape[0]
    out_far = [p[:out_split] for p in out_sent]
    out_near_b = add_far(
        [p[out_split:] for p in out_sent], [done["bn", 0][0], done["bn", 0][2]]
    )
    grad_ffn = grad_ffn.astype(f32)

    def output_steps():
        parts = [
            joined_rows(p)
            for p in zip(z_parts(add_far(out_far, out_near)), z_parts(out_near_b))
        ]
        total = parts[-1]
        for part in parts[-2::-1]:
            moved_total = links.shift(total, "z", -1)
            yield [moved_total]
            total = plus(moved_total, part)
        rows = total.shape[0] // 3
        yield [joined_rows([total[:rows], *last_b(total[rows:])])]

    out_steps = output_steps()
    out_now = next(out_steps)
    def pick(value, start, count):
        return jnp.concatenate(
            [value[:, start : start + count], value[:, half_all + start : half_all + start + count]],
            axis=1,
        )

    blocks_in = [grad_w_in] if lean else [grad_w_top, grad_w_end]
    grad_w_expert_in = joined_rows([pick(v, 0, half_ff) for v in blocks_in])
    grad_w_expert_out = grad_w_back[:half_ff]
    grad_w_shared_out = grad_w_back[half_ff : half_ff + half_sh]
    grad_shared = joined_rows([pick(v, half_ff, half_sh) for v in blocks_in])
    grad_shared = grad_shared.reshape(devices, rows_d, 2 * half_sh)
    def owner_steps(value, direct):
        count, size = value.shape[1], links.size["z"]
        value = value.reshape(size, 2, ctx * count, -1)

        def core(c):
            return lax.dynamic_index_in_dim(value, c, 1, keepdims=False)

        moved_core = links.shift(core(links.own["c"] ^ 1), "c")
        (moved_core,) = yield [moved_core]
        total = plus(moved_core, core(links.own["c"]))
        parts = [
            lax.dynamic_index_in_dim(total, links.minus("z", jnp.uint32(k)), 0, keepdims=False)
            for k in range(size)
        ]
        if direct:
            back = [links.shift(parts[k], "z", -k) for k in range(1, size)]
            back = yield back
            summed = sum([p.astype(f32) for p in back], parts[0].astype(f32)).astype(bf16)
        else:
            summed = parts[-1]
            for part in parts[-2::-1]:
                moved_sum = links.shift(summed, "z", -1)
                (moved_sum,) = yield [moved_sum]
                summed = plus(moved_sum, part)
        summed = summed.reshape(ctx, count, -1)
        pieces = [
            lax.dynamic_index_in_dim(summed, rel_ctx[k], 0, keepdims=False) for k in range(ctx)
        ]
        pieces = links.ctx_exchange(pieces)
        received = yield pieces[1:]
        yield jnp.stack([pieces[0], *received])[ctx_place].astype(f32)

    grad_out = cotangent.astype(f32)
    grad_middle_part, grad_norm_ffn = rms_backward(middle, inverse_ffn, gain_ffn, grad_ffn)
    grad_middle = grad_out + grad_middle_part
    grad_attended = grad_middle.astype(bf16)
    grad_heads_all = matmul_right_t(grad_attended, out_w).astype(bf16)
    pieces = [
        jnp.concatenate(
            [columns(grad_heads_all, k, v_cols), columns(grad_attended, k, D // ctx)], axis=1
        )
        for k in range(ctx)
    ]
    arrived = jnp.concatenate(links.ctx_exchange(pieces), axis=0)
    arrived, grad_shared, *out_now = tie(arrived, grad_shared, *out_now)
    grad_shared = lax.all_to_all(grad_shared, BOTH, split_axis=0, concat_axis=0, tiled=True)
    grad_shared = grad_shared.transpose(1, 0, 2)
    grad_w_shared_in = jnp.concatenate(
        [
            grad_shared[:, :, :half_sh].reshape(rows_d, SHARED_FF),
            grad_shared[:, :, half_sh:].reshape(rows_d, SHARED_FF),
        ],
        axis=1,
    )
    out_now = next(out_steps)
    grad_heads = arrived[:, :v_cols].reshape(row, heads, VDIM).transpose(1, 0, 2)
    grad_attended_cols = arrived[:, v_cols:]
    quarter = tok // 2
    parts = [heads_half[0][:quarter], heads_half[1][:quarter]]
    parts += [heads_half[0][quarter:], heads_far[1][:quarter]]
    parts += [heads_far[0][:quarter], heads_half[1][quarter:]]
    parts += [heads_far[0][quarter:], heads_far[1][quarter:]]
    heads_out_row = joined_rows(parts)
    if links.size["w"] > 1:
        heads_out_row = links.gather(heads_out_row, ("w",))

    soft = jnp.exp(masked_scores() - log_total)
    grad_values = jnp.einsum(
        "hqk,hqd->hkd", soft.astype(bf16), grad_heads, preferred_element_type=f32
    )
    grad_probs = jnp.einsum("hqd,hkd->hqk", grad_heads, value, preferred_element_type=f32)
    row_delta = jnp.sum(soft * grad_probs, axis=-1, keepdims=True)
    grad_raw = (soft * (grad_probs - row_delta) * scale).astype(bf16)
    grad_raw, grad_values, *out_now = tie(grad_raw, grad_values, *out_now)
    out_now = next(out_steps)
    grad_query = jnp.einsum("hqk,hkd->qhd", grad_raw, key, preferred_element_type=f32)
    grad_key = jnp.einsum("hqk,hqd->khd", grad_raw, query, preferred_element_type=f32)
    grad_key_rope = jnp.sum(grad_key[..., NOPE:], axis=1)
    grad_keyval = jnp.concatenate(
        [grad_key[..., :NOPE], grad_values.transpose(1, 0, 2)], axis=-1
    )
    grad_keyval = grad_keyval.astype(bf16).reshape(row, kv_cols)
    grad_w_up = matmul_left_t(latent, grad_keyval)
    grad_latent = matmul_right_t(grad_keyval, up_w)
    grad_low = jnp.concatenate([grad_latent, grad_key_rope], axis=1).astype(bf16)
    grad_query_raw = jnp.concatenate(
        [
            grad_query[..., :NOPE],
            unrotate(grad_query[..., NOPE:], cosine[:, None, :], sine_part[:, None, :]),
        ],
        axis=-1,
    )
    grad_query_raw = grad_query_raw.astype(bf16).reshape(ctx, tok, q_cols)
    query_back = links.ctx_exchange([grad_query_raw[k] for k in range(ctx)])
    grad_low, *query_back = tie(grad_low, *query_back)
    query_back = jnp.stack(query_back)
    grad_out_cols = matmul_left_t(heads_out_row, grad_attended_cols)
    grad_w_q = matmul_left_t(normed_row, grad_query_raw.reshape(row, q_cols))
    grad_w_up = grad_w_up.astype(bf16).reshape(devices, rows_l, up_parts, up_fold)
    grad_w_up = grad_w_up.transpose(0, 2, 1, 3).reshape(devices, rows_d, up_fold)
    heads_owned = owner_steps(
        jnp.concatenate(
            [
                grad_w_q.astype(bf16).reshape(devices, rows_d, q_cols),
                grad_w_up,
                grad_out_cols.astype(bf16).reshape(devices, rows_d, D // ctx),
            ],
            axis=2,
        ),
        False,
    )
    heads_moved = next(heads_owned)
    low_parts = links.ctx_exchange(list(grad_low.reshape(ctx, tok, -1)))
    *low_parts, out_now[0], heads_moved[0] = tie(*low_parts, *out_now, *heads_moved)
    heads_moved = heads_owned.send(heads_moved)
    grad_low = sum(p.astype(f32) for p in low_parts)
    mixed = (middle + list(out_steps)[-1][0].astype(f32)).astype(bf16)
    query_back = query_back[ctx_place].transpose(1, 0, 2).reshape(tok, ctx * q_cols)
    grad_compressed_latent, grad_norm_latent = rms_backward(
        raw_latent[:tok], inverse_latent[:tok], gain_latent, grad_low[:, :LATENT]
    )
    grad_compressed = jnp.concatenate(
        [
            grad_compressed_latent,
            unrotate(grad_low[:, LATENT:], cosine[:tok], sine_part[:tok]),
        ],
        axis=1,
    ).astype(bf16)
    grad_normed = matmul_right_t(grad_compressed, down_w) + matmul_right_t(
        query_back, query_w_all
    )
    grad_normed, heads_moved[0] = tie(grad_normed, *heads_moved)
    heads_moved = heads_owned.send(heads_moved)
    grad_input_part, grad_norm_attn = rms_backward(
        inputs, inverse_row[:tok], gain_attn, grad_normed
    )
    grad_in = grad_middle + grad_input_part

    def joined(value):
        return value.transpose(1, 0, 2).reshape(value.shape[1], -1)

    compressed_cols = jnp.concatenate(
        links.ctx_exchange([columns(grad_compressed, k, dn_cols) for k in range(ctx)]), axis=0
    )
    grad_w_down = matmul_left_t(normed_row, compressed_cols).astype(bf16)
    vectors = jnp.stack(
        [
            jnp.pad(v.reshape(devices, -1), ((0, 0), (0, dn_cols - v.size // devices)))
            for v in (grad_norm_attn, grad_norm_ffn, grad_norm_latent)
        ],
        axis=1,
    )
    vectors = jnp.pad(vectors, ((0, 0), (0, 13), (0, 0))).astype(bf16)
    last_owned = owner_steps(
        jnp.concatenate([grad_w_down.reshape(devices, rows_d, dn_cols), vectors], axis=1), True
    )
    last_moved = next(last_owned)
    last_moved[0], heads_moved[0] = tie(*last_moved, *heads_moved)
    heads_moved = heads_owned.send(heads_moved)
    last_moved = last_owned.send(last_moved)

    def finish(steps, received):
        for received in iter(lambda: steps.send(received), None):
            if not isinstance(received, list):
                return received

    heads_grads = finish(heads_owned, heads_moved)
    last_grads = finish(last_owned, last_moved)
    grad_w_query = joined(heads_grads[:, :, :q_cols])
    grad_w_out = joined(heads_grads[:, :, q_cols + up_fold :])
    grad_w_kv_up = heads_grads[:, :, q_cols : q_cols + up_fold]
    grad_w_kv_up = grad_w_kv_up.reshape(ctx, up_parts, rows_l, up_fold)
    grad_w_kv_up = grad_w_kv_up.transpose(2, 0, 1, 3).reshape(rows_l, ctx * kv_cols)
    grad_w_kv_down = joined(last_grads[:, :rows_d])
    vector_sums = jnp.sum(last_grads[:, rows_d : rows_d + 3], axis=0)
    return (
        mixed,
        grad_in,
        vector_sums[0, :rows_d],
        grad_w_query,
        grad_w_kv_down,
        vector_sums[2, :rows_l],
        grad_w_kv_up,
        grad_w_out,
        vector_sums[1, :rows_d],
        grad_w_shared_in,
        grad_w_shared_out,
        grad_w_expert_in[None],
        grad_w_expert_out[None],
    )


def solution(mesh):
    rows = P(BOTH, None)
    vector = P(BOTH)
    experts = P(BOTH, None, None)
    return jax.shard_map(
        shards,
        mesh=mesh,
        in_specs=(
            rows,
            P("dp"),
            rows,
            rows,
            rows,
            vector,
            rows,
            rows,
            vector,
            rows,
            rows,
            vector,
            rows,
            rows,
            experts,
            experts,
        ),
        out_specs=(
            rows,
            rows,
            vector,
            rows,
            rows,
            vector,
            rows,
            rows,
            vector,
            rows,
            rows,
            experts,
            experts,
        ),
        check_vma=False,
    )
```

```python
import math

import jax
import jax.numpy as jnp
from jax import lax
from jax.experimental import pallas as pl
from jax.experimental.pallas import tpu as pltpu
from jax.sharding import PartitionSpec as P

D = 2048
HEADS = 16
NOPE = 128
ROPE = 64
VDIM = 128
LATENT = 512
EXPERT_FF = 1408
SHARED_FF = 2816
TOP = 6

BOTH = ("dp", "ctx")
epsilon = 1e-06
f32 = jnp.float32
bf16 = jnp.bfloat16


def matmul(left, right):
    return jnp.dot(left, right, preferred_element_type=f32)


def matmul_left_t(left, right):
    return lax.dot_general(left, right, (((0,), (0,)), ((), ())), preferred_element_type=f32)


def matmul_right_t(left, right):
    return lax.dot_general(left, right, (((1,), (1,)), ((), ())), preferred_element_type=f32)


def rope_tables(positions, rope_width):
    half_width = rope_width // 2
    frequency = jnp.exp(
        -math.log(10000.0) * jnp.arange(half_width).astype(f32) / half_width
    )
    angles = positions.astype(f32)[:, None] * frequency[None, :]
    return (jnp.cos(angles), jnp.sin(angles))


def rotate(operand, cosine, sine_part):
    half_width = operand.shape[-1] // 2
    first_half = operand[..., :half_width]
    second_half = operand[..., half_width:]
    return jnp.concatenate(
        [
            first_half * cosine - second_half * sine_part,
            second_half * cosine + first_half * sine_part,
        ],
        axis=-1,
    )


def unrotate(operand, cosine, sine_part):
    return rotate(operand, cosine, -sine_part)


def swish(operand):
    return operand * jax.nn.sigmoid(operand)


def swish_slope(operand):
    sigma = jax.nn.sigmoid(operand)
    return sigma * (1.0 + operand * (1.0 - sigma))


def rms_inverse(operand):
    return lax.rsqrt(jnp.mean(operand * operand, axis=-1, keepdims=True) + epsilon)


def rms_backward(operand, inverse, gain_vec, grad_out):
    scaled = grad_out * gain_vec
    grad_gain = jnp.sum(grad_out * operand * inverse, axis=0)
    grad_operand = inverse * scaled - operand * inverse * inverse * inverse * jnp.mean(
        scaled * operand, axis=-1, keepdims=True
    )
    return (grad_operand, grad_gain)


class Links:
    def __init__(self):
        self.dp = lax.axis_size("dp")
        self.ctx = lax.axis_size("ctx")
        self.size = {"z": self.dp // 2, "c": 2, "w": self.ctx // 4, "y": 2, "x": 2}
        dp = lax.axis_index("dp").astype(jnp.uint32)
        self.place = ctx = lax.axis_index("ctx").astype(jnp.uint32)
        self.own = {
            "z": dp >> 1,
            "c": dp & 1,
            "w": ctx >> 2,
            "y": (ctx >> 1) & 1,
            "x": ctx & 1,
        }

    def minus(self, axis, steps):
        return (self.own[axis] - steps) & (self.size[axis] - 1)

    def ctx_at(self, k):
        return self.minus("w", jnp.uint32(k // 4)) * 4 + ((self.place ^ jnp.uint32(k)) & 3)

    def shift(self, value, axis, by=1):
        name, count = ("dp", self.dp) if axis in "zc" else ("ctx", self.ctx)
        if axis == "z":
            pairs = [(i, (i + 2 * by) % count) for i in range(count)]
        elif axis == "w":
            pairs = [(i, (i + 4 * by) % count) for i in range(count)]
        else:
            pairs = [(i, i ^ (2 if axis == "y" else 1)) for i in range(count)]
        return lax.ppermute(value, name, pairs)

    def shift_ctx(self, value, k):
        pairs = [
            (i, (i // 4 - k // 4) % self.size["w"] * 4 + (i ^ k) % 4) for i in range(self.ctx)
        ]
        return lax.ppermute(value, "ctx", pairs)

    def ring(self, block, axis):
        held = [block]
        for _ in range(self.size[axis] - 1):
            held.append(self.shift(held[-1], axis))
        return held

    def gather(self, block, order):
        for axis in order:
            block = joined_rows(self.ring(block, axis))
        return block

    def reduce(self, parts, axis):
        total = parts[-1]
        for part in parts[-2::-1]:
            total = plus(self.shift(total, axis, -1), part)
        return total

    def scatter_sum(self, block, order):
        for axis in order[::-1]:
            block = self.reduce(jnp.split(block, self.size[axis]), axis)
        return block

    def device_of(self, order):
        place = dict(self.own)
        depth = len(order)
        for i, axis in enumerate(order):
            shape = [1] * depth
            shape[depth - 1 - i] = self.size[axis]
            place[axis] = self.minus(
                axis, jnp.arange(self.size[axis], dtype=jnp.uint32).reshape(shape)
            )
        number = (place["z"] * 2 + place["c"]) * self.ctx
        number = number + place["w"] * 4 + place["y"] * 2 + place["x"]
        return number.reshape(-1)

    def place_of(self, order):
        number = jnp.arange(self.dp * self.ctx, dtype=jnp.uint32)
        coordinate = {
            "x": number & 1,
            "y": (number >> 1) & 1,
            "w": (number >> 2) & (self.size["w"] - 1),
            "c": (number // self.ctx) & 1,
            "z": number // (2 * self.ctx),
        }
        place = jnp.zeros_like(number)
        for axis in order[::-1]:
            place = place * self.size[axis] + self.minus(axis, coordinate[axis])
        return place

    def ctx_place(self):
        number = jnp.arange(self.ctx, dtype=jnp.uint32)
        return self.minus("w", number >> 2) * 4 + ((self.place ^ number) & 3)

    def ctx_exchange(self, pieces):
        result = [pieces[0]] + [None] * (self.ctx - 1)
        for k in range(1, self.ctx):
            back = (-(k // 4)) % self.size["w"] * 4 + k % 4
            result[back] = self.shift_ctx(pieces[k], k)
        return result


def joined_rows(parts):
    return parts[0] if len(parts) == 1 else jnp.concatenate(parts, axis=0)


def plus(left, right):
    return (left.astype(f32) + right.astype(f32)).astype(bf16)


def tie(*values):
    return lax.optimization_barrier(values)


def after(value, *others):
    return lax.optimization_barrier((value,) + others)[0]


GROUP = 4


def ffn_kernel(half_ff, parts, part_steps, sources, x_ref, *refs):
    g_refs, (m_ref, w_in, w_out) = refs[:GROUP], refs[GROUP : GROUP + 3]
    refs = refs[GROUP + 3 :]
    if parts:
        moved, refs = refs[0], refs[1:]
    outs = refs[-max(2 * parts, 1) :]
    x_all, g_all, act, grad_pre = refs[-len(outs) - 4 : -len(outs)]
    half_all = act.shape[1]
    count = x_ref.shape[0] // GROUP
    x_all[...] = x_ref[...]
    for i, g_ref in enumerate(g_refs):
        g_all[i * count : (i + 1) * count] = g_ref[0]
    pre = matmul(x_ref[...], w_in[...])
    gate, up = pre[:, :half_all], pre[:, half_all:]
    column = lax.broadcasted_iota(jnp.int32, (1, half_all), 1)
    weight = jnp.where(column < half_ff, m_ref[...], 1.0)
    sigma = jax.nn.sigmoid(gate)
    swished = gate * sigma
    act[...] = (swished * up * weight).astype(bf16)
    grad_act = matmul_right_t(g_all[...], w_out[...]) * weight
    slope = sigma * (1.0 + gate * (1.0 - sigma))
    grad_pre[:, :half_all] = (grad_act * up * slope).astype(bf16)
    grad_pre[:, half_all:] = (grad_act * swished).astype(bf16)
    out_part = matmul(act[...], w_out[...])
    grad_part = matmul_right_t(grad_pre[...], w_in[...])
    if not parts:
        outs[0][:, :D] = out_part.astype(bf16)
        outs[0][:, D:] = grad_part.astype(bf16)
        return
    out_part = (out_part + moved[:, :D].astype(f32)).astype(bf16)
    grad_part = (grad_part + moved[:, D:].astype(f32)).astype(bf16)
    for k in range(parts):

        @pl.when(pl.program_id(0) // part_steps == k)
        def _():
            outs[2 * k][...] = out_part
            outs[2 * k + 1][...] = grad_part


def ffn_chunk(x, g_blocks, m, w_in, w_out, half_ff, sources, group, far, side, kept, moved, lean):
    half_all = w_out.shape[0]
    tokens = m.shape[0]
    count = tokens // sources.shape[0]
    tile = GROUP * count
    steps = x.shape[0] // tile
    parts = 4 if far == 2 else 2
    half = steps // parts
    per_slice = 4 * half
    base = 2 * group * per_slice + (2 * side + far % 2) * half

    def second(i):
        return (i // half) % 2

    def place(i):
        return base + i % half + second(i) * per_slice + i // (2 * half) * half

    def rows(width):
        return pl.BlockSpec((tile, width), lambda i, _: (i, 0))

    def kept_rows(width):
        return pl.BlockSpec((tile, width), lambda i, _: (i if lean else place(i), 0))

    def whole(value):
        return pl.BlockSpec(value.shape, lambda i, _: (0, 0), pipeline_mode=pl.Buffered(1))

    def g_spec(j):
        def index(i, s):
            return (s[GROUP * place(i) + j], 2 * group + second(i), 0)

        return pl.BlockSpec((1, count, D), index)

    operands = [sources, x] + [g_blocks] * GROUP + [m, w_in, w_out]
    in_specs = [rows(D)] + [g_spec(j) for j in range(GROUP)]
    in_specs += [pl.BlockSpec((tile, 1), lambda i, _: (place(i), 0)), whole(w_in), whole(w_out)]
    out_specs = [rows(2 * D)]
    out_shape = [jax.ShapeDtypeStruct((x.shape[0], 2 * D), bf16)]
    if moved is not None:
        operands.append(moved)
        in_specs.append(rows(2 * D))

        def part_spec(k):
            return pl.BlockSpec(
                (tile, D), lambda i, _: (jnp.clip(i - k * half, 0, half - 1), 0)
            )

        out_specs = [part_spec(k // 2) for k in range(2 * parts)]
        out_shape = [jax.ShapeDtypeStruct((half * tile, D), bf16)] * (2 * parts)
    aliases = {}
    if kept is not None:
        aliases = {len(operands) + i: i for i in range(4)}
        operands += kept
        in_specs += [pl.BlockSpec(memory_space=pl.ANY)] * 4
    widths = (D, D, half_all, 2 * half_all)
    kept_count = x.shape[0] if lean else tokens
    flops = 2 * x.shape[0] * D * 6 * half_all
    result = pl.pallas_call(
        lambda *refs: ffn_kernel(half_ff, 0 if moved is None else parts, half, *refs),
        grid_spec=pltpu.PrefetchScalarGridSpec(
            num_scalar_prefetch=1,
            grid=(steps,),
            in_specs=in_specs,
            out_specs=[kept_rows(w) for w in widths] + out_specs,
        ),
        out_shape=[jax.ShapeDtypeStruct((kept_count, w), bf16) for w in widths] + out_shape,
        input_output_aliases=aliases,
        compiler_params=pltpu.CompilerParams(vmem_limit_bytes=60 * 2**20),
        cost_estimate=pl.CostEstimate(
            flops=flops, bytes_accessed=x.shape[0] * D * 16, transcendentals=0
        ),
        name="ffn_chunk",
    )(*operands)
    return list(result[:4]), list(result[4:])


def shards(
    hidden_in,
    segments,
    routes,
    gates,
    cotangent,
    norm_attn,
    w_query,
    w_kv_down,
    norm_latent,
    w_kv_up,
    w_out,
    norm_ffn,
    w_shared_in,
    w_shared_out,
    w_expert_in,
    w_expert_out,
):
    links = Links()
    tok = hidden_in.shape[0]
    row = segments.shape[0]
    ctx = links.ctx
    devices = links.dp * ctx
    half_ff = EXPERT_FF // 2
    half_sh = w_shared_out.shape[0]
    half_all = -(-(half_ff + half_sh) // 128) * 128
    heads = HEADS // ctx
    q_cols = heads * (NOPE + ROPE)
    v_cols = heads * VDIM
    kv_cols = heads * (NOPE + VDIM)
    dn_cols = (LATENT + ROPE) // ctx
    rows_d = w_query.shape[0]
    rows_l = w_kv_up.shape[0]
    up_fold = rows_l * kv_cols // rows_d
    up_parts = rows_d // rows_l
    scale = 1.0 / math.sqrt(NOPE + ROPE)
    rel_ctx = [links.ctx_at(k) for k in range(ctx)]
    ctx_place = links.ctx_place()

    def columns(value, k, width):
        return lax.dynamic_slice_in_dim(value, rel_ctx[k] * width, width, 1)

    latent_gain = jnp.zeros((rows_d,), bf16).at[:rows_l].set(norm_latent)
    small = jnp.concatenate(
        [w_kv_down, norm_attn[:, None], norm_ffn[:, None], latent_gain[:, None]], axis=1
    )
    small = jnp.pad(small, ((0, 0), (0, -small.shape[1] % 128)))
    small_cols = small.shape[1]
    small = jnp.concatenate([small, w_out], axis=1)
    pieces = []
    for k in range(ctx):
        folded = columns(w_kv_up, k, kv_cols).reshape(rows_l, up_parts, up_fold)
        folded = folded.transpose(1, 0, 2).reshape(rows_d, up_fold)
        pieces.append(jnp.concatenate([columns(w_query, k, q_cols), folded], axis=1))
    hidden_parts = links.ctx_exchange([hidden_in] * ctx)
    step, *received = tie(links.shift(small, "z"), *links.ctx_exchange(pieces))
    heads_w = joined_rows(received)
    small_parts, heads_parts = [small, step], [heads_w]
    for i in range(links.size["z"] - 1):
        pair = [links.shift(heads_parts[-1], "z")]
        if i < links.size["z"] - 2:
            pair.append(links.shift(small_parts[-1], "z"))
        else:
            small_all = links.gather(joined_rows(small_parts), ("w",))
            small_all = small_all.reshape(-1, 2, rows_d // 2, small.shape[1])
            small_a = small_all[:, 0].reshape(-1, small.shape[1])
            small_b = small_all[:, 1].reshape(-1, small.shape[1])
            pair += [links.shift(small_a, "x"), links.shift(small_b, "y")]
        pair = list(tie(*pair))
        if i < links.size["z"] - 2:
            small_parts.append(pair[1])
        if i == 0:
            w_shared_in, _ = tie(w_shared_in, pair[0])
        if i == links.size["z"] - 3:
            pair[0], *hidden_parts = tie(pair[0], *hidden_parts)
            hidden_row = joined_rows(hidden_parts)
        heads_parts.append(pair[0])
    small_a, small_b = joined_rows([small_a, pair[1]]), joined_rows([small_b, pair[2]])
    heads_w = joined_rows(heads_parts)
    heads_c = links.shift(heads_w, "c")
    last_a, last_b = small_a[:, small_cols:], small_b[:, small_cols:]
    small_a, small_b = small_a[:, :small_cols], small_b[:, :small_cols]
    shared_pieces = jnp.concatenate(
        [
            w_shared_in[:, :SHARED_FF].reshape(rows_d, devices, half_sh),
            w_shared_in[:, SHARED_FF:].reshape(rows_d, devices, half_sh),
        ],
        axis=2,
    ).transpose(1, 0, 2)
    shared_w = lax.all_to_all(shared_pieces, BOTH, split_axis=0, concat_axis=0, tiled=True)
    far_a, far_b, shared_w = tie(links.shift(small_a, "y"), links.shift(small_b, "x"), shared_w)
    small_all = joined_rows([small_a, far_a, small_b, far_b])
    small_all = joined_rows([small_all, links.shift(small_all, "c")])
    heads_w = joined_rows([heads_w, heads_c]).reshape(devices, rows_d, q_cols + up_fold)
    blocks = devices // 2
    place_a = links.place_of(("z", "w", "x", "y", "c"))
    place_b = links.place_of(("z", "w", "y", "x", "c"))
    take_a = (place_a // blocks) * 2 * blocks + place_a % blocks
    take_b = (place_b // blocks) * 2 * blocks + blocks + place_b % blocks
    take = jnp.stack([take_a, take_b], axis=1).reshape(-1)
    small_all = small_all.reshape(2 * devices, rows_d // 2, small_cols)[take]
    small_all = small_all.reshape(devices, rows_d, small_cols)
    down_w = small_all[:, :, : LATENT + ROPE].reshape(D, LATENT + ROPE)
    gain_attn = small_all[:, :, LATENT + ROPE].reshape(D).astype(f32)
    gain_ffn = small_all[:, :, LATENT + ROPE + 1].reshape(D).astype(f32)
    gain_latent = small_all[:, :rows_l, LATENT + ROPE + 2].reshape(LATENT).astype(f32)

    heads_place = links.place_of(("x", "y", "w", "z", "c"))
    heads_w = heads_w[heads_place]
    query_w = heads_w[:, :, :q_cols].reshape(D, q_cols)
    up_w = heads_w[:, :, q_cols:].reshape(devices, up_parts, rows_l, up_fold)
    up_w = up_w.transpose(0, 2, 1, 3).reshape(LATENT, kv_cols)

    orders = (
        ("z", "w", "x", "y"),
        ("z", "w", "y", "x"),
        ("y", "z", "w", "x"),
        ("x", "z", "w", "y"),
    )
    slices = len(orders)
    count = tok // slices
    tokens = devices * tok
    source_list = [links.device_of(order + ("c",)) for order in orders]
    sources = jnp.concatenate(source_list).astype(jnp.int32)
    m_place = jnp.concatenate([d * slices + i for i, d in enumerate(source_list)])
    hidden_row, query_w, up_w, down_w = tie(hidden_row, query_w, up_w, down_w)
    g_all = lax.all_gather(after(cotangent, far_a), BOTH, axis=0, tiled=True)
    g_blocks = g_all.reshape(devices, tok, D)

    inputs_row = hidden_row.astype(f32)
    inverse_row = rms_inverse(inputs_row)
    normed_row = (inputs_row * inverse_row * gain_attn).astype(bf16)
    rel_numbers = jnp.stack(rel_ctx)
    positions = rel_numbers.astype(jnp.int32)[:, None] * tok
    positions = (positions + jnp.arange(tok, dtype=jnp.int32)[None, :]).reshape(-1)
    row_segments = segments.reshape(ctx, tok)[rel_numbers].reshape(-1)
    allowed = (positions[None, :] <= positions[:, None]) & (
        row_segments[None, :] == row_segments[:, None]
    )
    cosine, sine_part = rope_tables(positions, ROPE)
    query_raw = matmul(normed_row, query_w).reshape(row, heads, NOPE + ROPE)
    query = jnp.concatenate(
        [
            query_raw[..., :NOPE],
            rotate(query_raw[..., NOPE:], cosine[:, None, :], sine_part[:, None, :]),
        ],
        axis=-1,
    ).astype(bf16)
    query = query.transpose(1, 0, 2)
    compressed = matmul(normed_row, down_w)
    raw_latent = compressed[:, :LATENT]
    inverse_latent = rms_inverse(raw_latent)
    latent = (raw_latent * inverse_latent * gain_latent).astype(bf16)
    key_rope = rotate(compressed[:, LATENT:], cosine, sine_part).astype(bf16)
    keyval = matmul(latent, up_w).astype(bf16).reshape(row, heads, NOPE + VDIM)
    last_a, last_b = tie(last_a, last_b, far_a)[:2]
    last_y, last_x, keyval = tie(links.shift(last_a, "y"), links.shift(last_b, "x"), keyval)
    out_w = joined_rows([last_a, last_y, last_b, last_x])
    out_w = joined_rows([out_w, links.shift(out_w, "c")])
    out_w = out_w.reshape(2 * devices, rows_d // 2, D)[take].reshape(D, D)
    keyval = keyval.transpose(1, 0, 2)
    key = jnp.concatenate(
        [keyval[..., :NOPE], jnp.broadcast_to(key_rope[None], (heads, row, ROPE))], axis=-1
    )
    value = keyval[..., NOPE:]

    def masked_scores():
        raw = jnp.einsum("hqd,hkd->hqk", query, key, preferred_element_type=f32)
        return jnp.where(allowed[None], raw * scale, -1e30)

    scores = masked_scores()
    row_max = jnp.max(scores, axis=-1, keepdims=True)
    exponent = jnp.exp(scores - row_max)
    row_total = jnp.sum(exponent, axis=-1, keepdims=True)
    log_total = row_max + jnp.log(row_total)
    probs = (exponent / row_total).astype(bf16)
    heads_part = jnp.einsum("hqk,hkd->qhd", probs, value, preferred_element_type=f32)
    heads_part = heads_part.astype(bf16).reshape(ctx, tok, v_cols)
    returned = jnp.stack(links.ctx_exchange([heads_part[k] for k in range(ctx)]))
    heads_out = returned[ctx_place].transpose(1, 0, 2).reshape(tok, HEADS * VDIM)
    inputs = hidden_in.astype(f32)
    middle = inputs + matmul(heads_out, out_w)
    inverse_ffn = rms_inverse(middle)
    ffn_in = (middle * inverse_ffn * gain_ffn).astype(bf16)

    cut = [ffn_in[i * count : (i + 1) * count] for i in range(slices)]

    def halved(parts):
        both = [jnp.split(part, 2) for part in parts]
        return [joined_rows([pair[i] for pair in both]) for i in range(2)]

    held = joined_rows(cut[:2])
    heads_half = [heads_out[: tok // 2], heads_out[tok // 2 :]]
    near_y, near_x, first, shared_w, w_expert_in, routes, gates = tie(
        links.shift(cut[2], "y"),
        links.shift(cut[3], "x"),
        links.shift(held, "z"),
        shared_w,
        w_expert_in,
        routes,
        gates,
    )
    experts = devices // 2
    expert_number = jnp.arange(experts, dtype=jnp.int32)[:, None, None]
    gate_matrix = jnp.sum(
        jnp.where(routes.T[None] == expert_number, gates.T[None], 0.0), axis=1
    )
    m_all = lax.all_to_all(
        jnp.repeat(gate_matrix, 2, axis=0), BOTH, split_axis=0, concat_axis=0, tiled=True
    )
    shared_w = shared_w.reshape(D, 2 * half_sh)
    pad = half_all - half_ff - half_sh
    w_in = jnp.concatenate(
        [
            w_expert_in[0][:, :half_ff],
            jnp.pad(shared_w[:, :half_sh], ((0, 0), (0, pad))),
            w_expert_in[0][:, half_ff:],
            jnp.pad(shared_w[:, half_sh:], ((0, 0), (0, pad))),
        ],
        axis=1,
    )
    w_back = jnp.concatenate(
        [w_expert_out[0], jnp.pad(w_shared_out, ((0, pad), (0, 0)))], axis=0
    )
    m = m_all.reshape(devices * slices, count)[m_place].reshape(tokens, 1)
    ring_a = [held, first]
    heads_far = [links.shift(heads_half[0], "x"), links.shift(heads_half[1], "y")]
    while len(ring_a) < links.size["z"]:
        step, *heads_far = tie(links.shift(ring_a[-1], "z"), *heads_far)
        if len(ring_a) == 2:
            heads_half = [joined_rows(p) for p in zip(heads_half, heads_far)]
            heads_far = [links.shift(heads_half[0], "y"), links.shift(heads_half[1], "x")]
        ring_a.append(step)
    held = links.gather(joined_rows(ring_a), ("w",)) if links.size["w"] > 1 else None
    slice_0, slice_1 = halved(jnp.split(held, ctx // 4 * links.size["z"]) if held is not None else ring_a)
    held = joined_rows([cut[2], near_y, cut[3], near_x])
    held, slice_0, slice_1, w_in, w_back, m = tie(held, slice_0, slice_1, w_in, w_back, m)
    ring_b = [held]
    moved_0, moved_1, step = tie(
        links.shift(slice_0, "x"), links.shift(slice_1, "y"), links.shift(held, "z")
    )
    ring_b.append(step)
    near_a = [joined_rows([slice_0, moved_0]), joined_rows([slice_1, moved_1])]
    far_a = [links.shift(near_a[0], "y"), links.shift(near_a[1], "x")]
    near_a_rows = joined_rows(near_a)
    near_a_sib = links.shift(near_a_rows, "c")

    lean = devices > 32
    kept = None
    done, moved = {}, {}

    def ffn(rows, name, side):
        kept_now, parts = ffn_chunk(
            rows,
            g_blocks,
            m,
            w_in,
            w_back,
            half_ff,
            sources,
            "ab".index(name[0]),
            ("n", "f", "").index(name[1:]),
            side,
            None if lean else kept,
            moved.get(name) if side == 0 else None,
            lean,
        )
        if side == 1:
            moved[name] = links.shift(parts[0], "c", -1)
        done[name, side] = parts
        if lean:
            sums = [
                matmul_left_t(kept_now[0], kept_now[3]),
                matmul_left_t(kept_now[2], kept_now[1]),
            ]
            return sums if kept is None else [a + b for a, b in zip(kept, sums)]
        return kept_now

    near_a_sib, step = tie(near_a_sib, links.shift(ring_b[-1], "z"))
    ring_b.append(step)
    step = links.shift(ring_b[-1], "z")
    kept = ffn(near_a_sib, "an", 1)
    step, *far_a = tie(step, *far_a, done["an", 1][0])[:3]
    far_a_rows = joined_rows(far_a)
    far_a_sib = links.shift(far_a_rows, "c")
    ring_b.append(step)
    far_a_sib, ring_b[-1] = tie(far_a_sib, ring_b[-1])
    while len(ring_b) < links.size["z"]:
        ring_b.append(links.shift(ring_b[-1], "z"))
    held = links.gather(joined_rows(ring_b), ("w",)) if links.size["w"] > 1 else None
    near_b = halved(jnp.split(held, ctx // 4 * links.size["z"]) if held is not None else ring_b)
    far_b = [links.shift(near_b[0], "x"), links.shift(near_b[1], "y")]
    kept = ffn(far_a_sib, "af", 1)
    kept = ffn(far_a_rows, "af", 0)
    near_a_rows, *far_b = tie(near_a_rows, *far_b, done["af", 0][0])[:3]
    rows_b = joined_rows([*near_b, *far_b])
    sib_b = links.shift(rows_b, "c")

    def add_far(moved_rows, near):
        return [plus(m_rows, n_rows) for m_rows, n_rows in zip(moved_rows, near)]

    def split_far(rows):
        pairs = [jnp.split(r, 2) for r in rows]
        return [p[0] for p in pairs], [p[1] for p in pairs]

    def z_parts(rows):
        if links.size["w"] > 1:
            rows = [links.scatter_sum(r, ("w",)) for r in rows]
        return [joined_rows(p) for p in zip(*[jnp.split(r, links.size["z"]) for r in rows])]

    def last_b(total):
        n0, f0, n1, f1 = jnp.split(total, 4)
        return plus(links.shift(f0, "y", -1), n0), plus(links.shift(f1, "x", -1), n1)

    far = done["af", 0][1::2]
    a_far = [links.shift(far[0], "y", -1), links.shift(far[1], "x", -1)]
    kept = ffn(near_a_rows, "an", 0)
    a_far = tie(*a_far, done["an", 0][0])[:2]
    a_near = add_far(a_far, done["an", 0][1::2])
    sib_b, *a_near = tie(sib_b, *a_near)
    a_near, far = split_far(a_near)
    a_far = [links.shift(far[0], "x", -1), links.shift(far[1], "y", -1)]
    query_w_all = lax.all_gather(after(w_query, sib_b), BOTH, axis=0, tiled=True)
    kept = ffn(sib_b, "b", 1)
    kept = ffn(rows_b, "b", 0)
    a_far = tie(*a_far, done["b", 0][0])[:2]
    a_parts = z_parts(add_far(a_far, a_near))
    a_sum = links.shift(a_parts[-1], "z", -1)
    done["bn", 0], done["bf", 0] = done["b", 0][:4], done["b", 0][4:]
    far = done["bf", 0][1::2]
    b_far = [links.shift(far[0], "x", -1), links.shift(far[1], "y", -1)]
    out_far = [done["af", 0][0], done["af", 0][2]]
    out_far_b = [done["bf", 0][0], done["bf", 0][2]]

    def send_outputs(far_rows, far_rows_b):
        near_rows, far_rows = split_far(add_far(far_rows, [done["an", 0][0], done["an", 0][2]]))
        return near_rows, [
            links.shift(joined_rows(pair), axis, -1)
            for pair, axis in zip(zip(far_rows, far_rows_b), "xy")
        ]

    if lean:
        grad_w_in, grad_w_back = kept
        a_sum = plus(a_sum, a_parts[-2])
        for part in a_parts[-3::-1]:
            a_sum = plus(links.shift(a_sum, "z", -1), part)
        out_far = [links.shift(p, axis, -1) for p, axis in zip(out_far, "yx")]
        out_near, out_sent = send_outputs(out_far, out_far_b)
        b_parts = z_parts(add_far(b_far, done["bn", 0][1::2]))
        b_sum = b_parts[-1]
        for part in b_parts[-2:0:-1]:
            b_sum = plus(links.shift(b_sum, "z", -1), part)
    else:
        x_all, g_kept, act_all, grad_pre_all = kept
        grad_w_top = matmul_left_t(x_all[:, : D // 2], grad_pre_all)
        *b_far, a_sum, _ = tie(*b_far, a_sum, grad_w_top)
        b_parts = z_parts(add_far(b_far, done["bn", 0][1::2]))
        a_sum = plus(a_sum, a_parts[-2])
        x_all, a_sum, out_far[0], out_far[1], *b_parts = tie(x_all, a_sum, *out_far, *b_parts)
        out_far = [links.shift(p, axis, -1) for p, axis in zip(out_far, "yx")]
        a_next = links.shift(a_sum, "z", -1)
        b_next = links.shift(b_parts[-1], "z", -1)
        grad_w_end = matmul_left_t(x_all[:, D // 2 :], grad_pre_all)
        a_next, b_next, _ = tie(a_next, b_next, grad_w_end)
        a_sum = plus(a_next, a_parts[-3])
        b_sum = plus(b_next, b_parts[-2])
        act_all, a_sum, b_sum, *out_all = tie(act_all, a_sum, b_sum, *out_far, *out_far_b)
        out_near, out_sent = send_outputs(out_all[:2], out_all[2:])
        b_next = links.shift(b_sum, "z", -1)
        a_next = links.shift(a_sum, "z", -1)
        grad_w_back = matmul_left_t(act_all, g_kept)
        a_next, b_next, _ = tie(a_next, b_next, grad_w_back)
        a_sum = plus(a_next, a_parts[-4])
        b_sum = plus(b_next, b_parts[-3])
        for part in b_parts[-4:0:-1]:
            b_sum = plus(links.shift(b_sum, "z", -1), part)
        grad_w_top, grad_w_end, grad_w_back, b_sum = tie(
            grad_w_top, grad_w_end, grad_w_back, b_sum
        )
    b_sum = plus(links.shift(b_sum, "z", -1), b_parts[0])
    grad_ffn = joined_rows([a_sum, *last_b(b_sum)])
    out_sent[0], out_sent[1], grad_ffn = tie(*out_sent, grad_ffn)
    out_split = out_near[0].shape[0]
    out_far = [p[:out_split] for p in out_sent]
    out_near_b = add_far(
        [p[out_split:] for p in out_sent], [done["bn", 0][0], done["bn", 0][2]]
    )
    grad_ffn = grad_ffn.astype(f32)

    def output_steps():
        parts = [
            joined_rows(p)
            for p in zip(z_parts(add_far(out_far, out_near)), z_parts(out_near_b))
        ]
        total = parts[-1]
        for part in parts[-2::-1]:
            moved_total = links.shift(total, "z", -1)
            yield [moved_total]
            total = plus(moved_total, part)
        rows = total.shape[0] // 3
        yield [joined_rows([total[:rows], *last_b(total[rows:])])]

    out_steps = output_steps()
    out_now = next(out_steps)
    def pick(value, start, count):
        return jnp.concatenate(
            [value[:, start : start + count], value[:, half_all + start : half_all + start + count]],
            axis=1,
        )

    blocks_in = [grad_w_in] if lean else [grad_w_top, grad_w_end]
    grad_w_expert_in = joined_rows([pick(v, 0, half_ff) for v in blocks_in])
    grad_w_expert_out = grad_w_back[:half_ff]
    grad_w_shared_out = grad_w_back[half_ff : half_ff + half_sh]
    grad_shared = joined_rows([pick(v, half_ff, half_sh) for v in blocks_in])
    grad_shared = grad_shared.reshape(devices, rows_d, 2 * half_sh)
    def owner_steps(value, direct):
        count, size = value.shape[1], links.size["z"]
        value = value.reshape(size, 2, ctx * count, -1)

        def core(c):
            return lax.dynamic_index_in_dim(value, c, 1, keepdims=False)

        moved_core = links.shift(core(links.own["c"] ^ 1), "c")
        (moved_core,) = yield [moved_core]
        total = plus(moved_core, core(links.own["c"]))
        parts = [
            lax.dynamic_index_in_dim(total, links.minus("z", jnp.uint32(k)), 0, keepdims=False)
            for k in range(size)
        ]
        if direct:
            back = [links.shift(parts[k], "z", -k) for k in range(1, size)]
            back = yield back
            summed = sum([p.astype(f32) for p in back], parts[0].astype(f32)).astype(bf16)
        else:
            summed = parts[-1]
            for part in parts[-2::-1]:
                moved_sum = links.shift(summed, "z", -1)
                (moved_sum,) = yield [moved_sum]
                summed = plus(moved_sum, part)
        summed = summed.reshape(ctx, count, -1)
        pieces = [
            lax.dynamic_index_in_dim(summed, rel_ctx[k], 0, keepdims=False) for k in range(ctx)
        ]
        pieces = links.ctx_exchange(pieces)
        received = yield pieces[1:]
        yield jnp.stack([pieces[0], *received])[ctx_place].astype(f32)

    grad_out = cotangent.astype(f32)
    grad_middle_part, grad_norm_ffn = rms_backward(middle, inverse_ffn, gain_ffn, grad_ffn)
    grad_middle = grad_out + grad_middle_part
    grad_attended = grad_middle.astype(bf16)
    grad_heads_all = matmul_right_t(grad_attended, out_w).astype(bf16)
    pieces = [
        jnp.concatenate(
            [columns(grad_heads_all, k, v_cols), columns(grad_attended, k, D // ctx)], axis=1
        )
        for k in range(ctx)
    ]
    arrived = jnp.concatenate(links.ctx_exchange(pieces), axis=0)
    arrived, grad_shared, *out_now = tie(arrived, grad_shared, *out_now)
    grad_shared = lax.all_to_all(grad_shared, BOTH, split_axis=0, concat_axis=0, tiled=True)
    grad_shared = grad_shared.transpose(1, 0, 2)
    grad_w_shared_in = jnp.concatenate(
        [
            grad_shared[:, :, :half_sh].reshape(rows_d, SHARED_FF),
            grad_shared[:, :, half_sh:].reshape(rows_d, SHARED_FF),
        ],
        axis=1,
    )
    out_now = next(out_steps)
    grad_heads = arrived[:, :v_cols].reshape(row, heads, VDIM).transpose(1, 0, 2)
    grad_attended_cols = arrived[:, v_cols:]
    quarter = tok // 2
    parts = [heads_half[0][:quarter], heads_half[1][:quarter]]
    parts += [heads_half[0][quarter:], heads_far[1][:quarter]]
    parts += [heads_far[0][:quarter], heads_half[1][quarter:]]
    parts += [heads_far[0][quarter:], heads_far[1][quarter:]]
    heads_out_row = joined_rows(parts)
    if links.size["w"] > 1:
        heads_out_row = links.gather(heads_out_row, ("w",))

    soft = jnp.exp(masked_scores() - log_total)
    grad_values = jnp.einsum(
        "hqk,hqd->hkd", soft.astype(bf16), grad_heads, preferred_element_type=f32
    )
    grad_probs = jnp.einsum("hqd,hkd->hqk", grad_heads, value, preferred_element_type=f32)
    row_delta = jnp.sum(soft * grad_probs, axis=-1, keepdims=True)
    grad_raw = (soft * (grad_probs - row_delta) * scale).astype(bf16)
    grad_raw, grad_values, *out_now = tie(grad_raw, grad_values, *out_now)
    out_now = next(out_steps)
    grad_query = jnp.einsum("hqk,hkd->qhd", grad_raw, key, preferred_element_type=f32)
    grad_key = jnp.einsum("hqk,hqd->khd", grad_raw, query, preferred_element_type=f32)
    grad_key_rope = jnp.sum(grad_key[..., NOPE:], axis=1)
    grad_keyval = jnp.concatenate(
        [grad_key[..., :NOPE], grad_values.transpose(1, 0, 2)], axis=-1
    )
    grad_keyval = grad_keyval.astype(bf16).reshape(row, kv_cols)
    grad_w_up = matmul_left_t(latent, grad_keyval)
    grad_latent = matmul_right_t(grad_keyval, up_w)
    grad_low = jnp.concatenate([grad_latent, grad_key_rope], axis=1).astype(bf16)
    grad_query_raw = jnp.concatenate(
        [
            grad_query[..., :NOPE],
            unrotate(grad_query[..., NOPE:], cosine[:, None, :], sine_part[:, None, :]),
        ],
        axis=-1,
    )
    grad_query_raw = grad_query_raw.astype(bf16).reshape(ctx, tok, q_cols)
    query_back = links.ctx_exchange([grad_query_raw[k] for k in range(ctx)])
    grad_low, *query_back = tie(grad_low, *query_back)
    query_back = jnp.stack(query_back)
    grad_out_cols = matmul_left_t(heads_out_row, grad_attended_cols)
    grad_w_q = matmul_left_t(normed_row, grad_query_raw.reshape(row, q_cols))
    grad_w_up = grad_w_up.astype(bf16).reshape(devices, rows_l, up_parts, up_fold)
    grad_w_up = grad_w_up.transpose(0, 2, 1, 3).reshape(devices, rows_d, up_fold)
    heads_owned = owner_steps(
        jnp.concatenate(
            [
                grad_w_q.astype(bf16).reshape(devices, rows_d, q_cols),
                grad_w_up,
                grad_out_cols.astype(bf16).reshape(devices, rows_d, D // ctx),
            ],
            axis=2,
        ),
        False,
    )
    heads_moved = next(heads_owned)
    low_parts = links.ctx_exchange(list(grad_low.reshape(ctx, tok, -1)))
    *low_parts, out_now[0], heads_moved[0] = tie(*low_parts, *out_now, *heads_moved)
    heads_moved = heads_owned.send(heads_moved)
    grad_low = sum(p.astype(f32) for p in low_parts)
    mixed = (middle + list(out_steps)[-1][0].astype(f32)).astype(bf16)
    query_back = query_back[ctx_place].transpose(1, 0, 2).reshape(tok, ctx * q_cols)
    grad_compressed_latent, grad_norm_latent = rms_backward(
        raw_latent[:tok], inverse_latent[:tok], gain_latent, grad_low[:, :LATENT]
    )
    grad_compressed = jnp.concatenate(
        [
            grad_compressed_latent,
            unrotate(grad_low[:, LATENT:], cosine[:tok], sine_part[:tok]),
        ],
        axis=1,
    ).astype(bf16)
    grad_normed = matmul_right_t(grad_compressed, down_w) + matmul_right_t(
        query_back, query_w_all
    )
    grad_normed, heads_moved[0] = tie(grad_normed, *heads_moved)
    heads_moved = heads_owned.send(heads_moved)
    grad_input_part, grad_norm_attn = rms_backward(
        inputs, inverse_row[:tok], gain_attn, grad_normed
    )
    grad_in = grad_middle + grad_input_part

    def joined(value):
        return value.transpose(1, 0, 2).reshape(value.shape[1], -1)

    compressed_cols = jnp.concatenate(
        links.ctx_exchange([columns(grad_compressed, k, dn_cols) for k in range(ctx)]), axis=0
    )
    grad_w_down = matmul_left_t(normed_row, compressed_cols).astype(bf16)
    vectors = jnp.stack(
        [
            jnp.pad(v.reshape(devices, -1), ((0, 0), (0, dn_cols - v.size // devices)))
            for v in (grad_norm_attn, grad_norm_ffn, grad_norm_latent)
        ],
        axis=1,
    )
    vectors = jnp.pad(vectors, ((0, 0), (0, 13), (0, 0))).astype(bf16)
    last_owned = owner_steps(
        jnp.concatenate([grad_w_down.reshape(devices, rows_d, dn_cols), vectors], axis=1), True
    )
    last_moved = next(last_owned)
    last_moved[0], heads_moved[0] = tie(*last_moved, *heads_moved)
    heads_moved = heads_owned.send(heads_moved)
    last_moved = last_owned.send(last_moved)

    def finish(steps, received):
        for received in iter(lambda: steps.send(received), None):
            if not isinstance(received, list):
                return received

    heads_grads = finish(heads_owned, heads_moved)
    last_grads = finish(last_owned, last_moved)
    grad_w_query = joined(heads_grads[:, :, :q_cols])
    grad_w_out = joined(heads_grads[:, :, q_cols + up_fold :])
    grad_w_kv_up = heads_grads[:, :, q_cols : q_cols + up_fold]
    grad_w_kv_up = grad_w_kv_up.reshape(ctx, up_parts, rows_l, up_fold)
    grad_w_kv_up = grad_w_kv_up.transpose(2, 0, 1, 3).reshape(rows_l, ctx * kv_cols)
    grad_w_kv_down = joined(last_grads[:, :rows_d])
    vector_sums = jnp.sum(last_grads[:, rows_d : rows_d + 3], axis=0)
    return (
        mixed,
        grad_in,
        vector_sums[0, :rows_d],
        grad_w_query,
        grad_w_kv_down,
        vector_sums[2, :rows_l],
        grad_w_kv_up,
        grad_w_out,
        vector_sums[1, :rows_d],
        grad_w_shared_in,
        grad_w_shared_out,
        grad_w_expert_in[None],
        grad_w_expert_out[None],
    )


def solution(mesh):
    rows = P(BOTH, None)
    vector = P(BOTH)
    experts = P(BOTH, None, None)
    return jax.shard_map(
        shards,
        mesh=mesh,
        in_specs=(
            rows,
            P("dp"),
            rows,
            rows,
            rows,
            vector,
            rows,
            rows,
            vector,
            rows,
            rows,
            vector,
            rows,
            rows,
            experts,
            experts,
        ),
        out_specs=(
            rows,
            rows,
            vector,
            rows,
            rows,
            vector,
            rows,
            rows,
            vector,
            rows,
            rows,
            experts,
            experts,
        ),
        check_vma=False,
    )
```

```python
import math

import jax
import jax.numpy as jnp
from jax import lax
from jax.experimental import pallas as pl
from jax.experimental.pallas import tpu as pltpu
from jax.sharding import PartitionSpec as P

D = 2048
HEADS = 16
NOPE = 128
ROPE = 64
VDIM = 128
LATENT = 512
EXPERT_FF = 1408
SHARED_FF = 2816
TOP = 6

BOTH = ("dp", "ctx")
epsilon = 1e-06
f32 = jnp.float32
bf16 = jnp.bfloat16


def matmul(left, right):
    return jnp.dot(left, right, preferred_element_type=f32)


def matmul_left_t(left, right):
    return lax.dot_general(left, right, (((0,), (0,)), ((), ())), preferred_element_type=f32)


def matmul_right_t(left, right):
    return lax.dot_general(left, right, (((1,), (1,)), ((), ())), preferred_element_type=f32)


def rope_tables(positions, rope_width):
    half_width = rope_width // 2
    frequency = jnp.exp(
        -math.log(10000.0) * jnp.arange(half_width).astype(f32) / half_width
    )
    angles = positions.astype(f32)[:, None] * frequency[None, :]
    return (jnp.cos(angles), jnp.sin(angles))


def rotate(operand, cosine, sine_part):
    half_width = operand.shape[-1] // 2
    first_half = operand[..., :half_width]
    second_half = operand[..., half_width:]
    return jnp.concatenate(
        [
            first_half * cosine - second_half * sine_part,
            second_half * cosine + first_half * sine_part,
        ],
        axis=-1,
    )


def unrotate(operand, cosine, sine_part):
    return rotate(operand, cosine, -sine_part)


def swish(operand):
    return operand * jax.nn.sigmoid(operand)


def swish_slope(operand):
    sigma = jax.nn.sigmoid(operand)
    return sigma * (1.0 + operand * (1.0 - sigma))


def rms_inverse(operand):
    return lax.rsqrt(jnp.mean(operand * operand, axis=-1, keepdims=True) + epsilon)


def rms_backward(operand, inverse, gain_vec, grad_out):
    scaled = grad_out * gain_vec
    grad_gain = jnp.sum(grad_out * operand * inverse, axis=0)
    grad_operand = inverse * scaled - operand * inverse * inverse * inverse * jnp.mean(
        scaled * operand, axis=-1, keepdims=True
    )
    return (grad_operand, grad_gain)


class Links:
    def __init__(self):
        self.dp = lax.axis_size("dp")
        self.ctx = lax.axis_size("ctx")
        self.size = {"z": self.dp // 2, "c": 2, "w": self.ctx // 4, "y": 2, "x": 2}
        dp = lax.axis_index("dp").astype(jnp.uint32)
        self.place = ctx = lax.axis_index("ctx").astype(jnp.uint32)
        self.own = {
            "z": dp >> 1,
            "c": dp & 1,
            "w": ctx >> 2,
            "y": (ctx >> 1) & 1,
            "x": ctx & 1,
        }

    def minus(self, axis, steps):
        return (self.own[axis] - steps) & (self.size[axis] - 1)

    def ctx_at(self, k):
        return self.minus("w", jnp.uint32(k // 4)) * 4 + ((self.place ^ jnp.uint32(k)) & 3)

    def shift(self, value, axis, by=1):
        name, count = ("dp", self.dp) if axis in "zc" else ("ctx", self.ctx)
        if axis == "z":
            pairs = [(i, (i + 2 * by) % count) for i in range(count)]
        elif axis == "w":
            pairs = [(i, (i + 4 * by) % count) for i in range(count)]
        else:
            pairs = [(i, i ^ (2 if axis == "y" else 1)) for i in range(count)]
        return lax.ppermute(value, name, pairs)

    def shift_ctx(self, value, k):
        pairs = [
            (i, (i // 4 - k // 4) % self.size["w"] * 4 + (i ^ k) % 4) for i in range(self.ctx)
        ]
        return lax.ppermute(value, "ctx", pairs)

    def ring(self, block, axis):
        held = [block]
        for _ in range(self.size[axis] - 1):
            held.append(self.shift(held[-1], axis))
        return held

    def gather(self, block, order):
        for axis in order:
            block = joined_rows(self.ring(block, axis))
        return block

    def reduce(self, parts, axis):
        total = parts[-1]
        for part in parts[-2::-1]:
            total = plus(self.shift(total, axis, -1), part)
        return total

    def scatter_sum(self, block, order):
        for axis in order[::-1]:
            block = self.reduce(jnp.split(block, self.size[axis]), axis)
        return block

    def device_of(self, order):
        place = dict(self.own)
        depth = len(order)
        for i, axis in enumerate(order):
            shape = [1] * depth
            shape[depth - 1 - i] = self.size[axis]
            place[axis] = self.minus(
                axis, jnp.arange(self.size[axis], dtype=jnp.uint32).reshape(shape)
            )
        number = (place["z"] * 2 + place["c"]) * self.ctx
        number = number + place["w"] * 4 + place["y"] * 2 + place["x"]
        return number.reshape(-1)

    def place_of(self, order):
        number = jnp.arange(self.dp * self.ctx, dtype=jnp.uint32)
        coordinate = {
            "x": number & 1,
            "y": (number >> 1) & 1,
            "w": (number >> 2) & (self.size["w"] - 1),
            "c": (number // self.ctx) & 1,
            "z": number // (2 * self.ctx),
        }
        place = jnp.zeros_like(number)
        for axis in order[::-1]:
            place = place * self.size[axis] + self.minus(axis, coordinate[axis])
        return place

    def ctx_place(self):
        number = jnp.arange(self.ctx, dtype=jnp.uint32)
        return self.minus("w", number >> 2) * 4 + ((self.place ^ number) & 3)

    def ctx_exchange(self, pieces):
        result = [pieces[0]] + [None] * (self.ctx - 1)
        for k in range(1, self.ctx):
            back = (-(k // 4)) % self.size["w"] * 4 + k % 4
            result[back] = self.shift_ctx(pieces[k], k)
        return result


def joined_rows(parts):
    return parts[0] if len(parts) == 1 else jnp.concatenate(parts, axis=0)


def plus(left, right):
    return (left.astype(f32) + right.astype(f32)).astype(bf16)


def tie(*values):
    return lax.optimization_barrier(values)


def after(value, *others):
    return lax.optimization_barrier((value,) + others)[0]


GROUP = 4


def ffn_kernel(half_ff, parts, part_steps, sources, x_ref, *refs):
    g_refs, (m_ref, w_in, w_out) = refs[:GROUP], refs[GROUP : GROUP + 3]
    refs = refs[GROUP + 3 :]
    if parts:
        moved, refs = refs[0], refs[1:]
    outs = refs[-max(2 * parts, 1) :]
    x_all, g_all, act, grad_pre = refs[-len(outs) - 4 : -len(outs)]
    half_all = act.shape[1]
    count = x_ref.shape[0] // GROUP
    x_all[...] = x_ref[...]
    for i, g_ref in enumerate(g_refs):
        g_all[i * count : (i + 1) * count] = g_ref[0]
    pre = matmul(x_ref[...], w_in[...])
    gate, up = pre[:, :half_all], pre[:, half_all:]
    column = lax.broadcasted_iota(jnp.int32, (1, half_all), 1)
    weight = jnp.where(column < half_ff, m_ref[...], 1.0)
    sigma = jax.nn.sigmoid(gate)
    swished = gate * sigma
    act[...] = (swished * up * weight).astype(bf16)
    grad_act = matmul_right_t(g_all[...], w_out[...]) * weight
    slope = sigma * (1.0 + gate * (1.0 - sigma))
    grad_pre[:, :half_all] = (grad_act * up * slope).astype(bf16)
    grad_pre[:, half_all:] = (grad_act * swished).astype(bf16)
    out_part = matmul(act[...], w_out[...])
    grad_part = matmul_right_t(grad_pre[...], w_in[...])
    if not parts:
        outs[0][:, :D] = out_part.astype(bf16)
        outs[0][:, D:] = grad_part.astype(bf16)
        return
    out_part = (out_part + moved[:, :D].astype(f32)).astype(bf16)
    grad_part = (grad_part + moved[:, D:].astype(f32)).astype(bf16)
    for k in range(parts):

        @pl.when(pl.program_id(0) // part_steps == k)
        def _():
            outs[2 * k][...] = out_part
            outs[2 * k + 1][...] = grad_part


def ffn_chunk(x, g_blocks, m, w_in, w_out, half_ff, sources, group, far, side, kept, moved, lean):
    half_all = w_out.shape[0]
    tokens = m.shape[0]
    count = tokens // sources.shape[0]
    tile = GROUP * count
    steps = x.shape[0] // tile
    parts = 4 if far == 2 else 2
    half = steps // parts
    per_slice = 4 * half
    base = 2 * group * per_slice + (2 * side + far % 2) * half

    def second(i):
        return (i // half) % 2

    def place(i):
        return base + i % half + second(i) * per_slice + i // (2 * half) * half

    def rows(width):
        return pl.BlockSpec((tile, width), lambda i, _: (i, 0))

    def kept_rows(width):
        return pl.BlockSpec((tile, width), lambda i, _: (i if lean else place(i), 0))

    def whole(value):
        return pl.BlockSpec(value.shape, lambda i, _: (0, 0), pipeline_mode=pl.Buffered(1))

    def g_spec(j):
        def index(i, s):
            return (s[GROUP * place(i) + j], 2 * group + second(i), 0)

        return pl.BlockSpec((1, count, D), index)

    operands = [sources, x] + [g_blocks] * GROUP + [m, w_in, w_out]
    in_specs = [rows(D)] + [g_spec(j) for j in range(GROUP)]
    in_specs += [pl.BlockSpec((tile, 1), lambda i, _: (place(i), 0)), whole(w_in), whole(w_out)]
    out_specs = [rows(2 * D)]
    out_shape = [jax.ShapeDtypeStruct((x.shape[0], 2 * D), bf16)]
    if moved is not None:
        operands.append(moved)
        in_specs.append(rows(2 * D))

        def part_spec(k):
            return pl.BlockSpec(
                (tile, D), lambda i, _: (jnp.clip(i - k * half, 0, half - 1), 0)
            )

        out_specs = [part_spec(k // 2) for k in range(2 * parts)]
        out_shape = [jax.ShapeDtypeStruct((half * tile, D), bf16)] * (2 * parts)
    aliases = {}
    if kept is not None:
        aliases = {len(operands) + i: i for i in range(4)}
        operands += kept
        in_specs += [pl.BlockSpec(memory_space=pl.ANY)] * 4
    widths = (D, D, half_all, 2 * half_all)
    kept_count = x.shape[0] if lean else tokens
    flops = 2 * x.shape[0] * D * 6 * half_all
    result = pl.pallas_call(
        lambda *refs: ffn_kernel(half_ff, 0 if moved is None else parts, half, *refs),
        grid_spec=pltpu.PrefetchScalarGridSpec(
            num_scalar_prefetch=1,
            grid=(steps,),
            in_specs=in_specs,
            out_specs=[kept_rows(w) for w in widths] + out_specs,
        ),
        out_shape=[jax.ShapeDtypeStruct((kept_count, w), bf16) for w in widths] + out_shape,
        input_output_aliases=aliases,
        compiler_params=pltpu.CompilerParams(vmem_limit_bytes=60 * 2**20),
        cost_estimate=pl.CostEstimate(
            flops=flops, bytes_accessed=x.shape[0] * D * 16, transcendentals=0
        ),
        name="ffn_chunk",
    )(*operands)
    return list(result[:4]), list(result[4:])


def shards(
    hidden_in,
    segments,
    routes,
    gates,
    cotangent,
    norm_attn,
    w_query,
    w_kv_down,
    norm_latent,
    w_kv_up,
    w_out,
    norm_ffn,
    w_shared_in,
    w_shared_out,
    w_expert_in,
    w_expert_out,
):
    links = Links()
    tok = hidden_in.shape[0]
    row = segments.shape[0]
    ctx = links.ctx
    devices = links.dp * ctx
    half_ff = EXPERT_FF // 2
    half_sh = w_shared_out.shape[0]
    half_all = -(-(half_ff + half_sh) // 128) * 128
    heads = HEADS // ctx
    q_cols = heads * (NOPE + ROPE)
    v_cols = heads * VDIM
    kv_cols = heads * (NOPE + VDIM)
    dn_cols = (LATENT + ROPE) // ctx
    rows_d = w_query.shape[0]
    rows_l = w_kv_up.shape[0]
    up_fold = rows_l * kv_cols // rows_d
    up_parts = rows_d // rows_l
    scale = 1.0 / math.sqrt(NOPE + ROPE)
    rel_ctx = [links.ctx_at(k) for k in range(ctx)]
    ctx_place = links.ctx_place()

    def columns(value, k, width):
        return lax.dynamic_slice_in_dim(value, rel_ctx[k] * width, width, 1)

    latent_gain = jnp.zeros((rows_d,), bf16).at[:rows_l].set(norm_latent)
    small = jnp.concatenate(
        [w_kv_down, norm_attn[:, None], norm_ffn[:, None], latent_gain[:, None]], axis=1
    )
    small = jnp.pad(small, ((0, 0), (0, -small.shape[1] % 128)))
    small_cols = small.shape[1]
    small = jnp.concatenate([small, w_out], axis=1)
    pieces = []
    for k in range(ctx):
        folded = columns(w_kv_up, k, kv_cols).reshape(rows_l, up_parts, up_fold)
        folded = folded.transpose(1, 0, 2).reshape(rows_d, up_fold)
        pieces.append(jnp.concatenate([columns(w_query, k, q_cols), folded], axis=1))
    hidden_parts = links.ctx_exchange([hidden_in] * ctx)
    step, *received = tie(links.shift(small, "z"), *links.ctx_exchange(pieces))
    heads_w = joined_rows(received)
    small_parts, heads_parts = [small, step], [heads_w]
    for i in range(links.size["z"] - 1):
        pair = [links.shift(heads_parts[-1], "z")]
        if i < links.size["z"] - 2:
            pair.append(links.shift(small_parts[-1], "z"))
        else:
            small_all = links.gather(joined_rows(small_parts), ("w",))
            small_all = small_all.reshape(-1, 2, rows_d // 2, small.shape[1])
            small_a = small_all[:, 0].reshape(-1, small.shape[1])
            small_b = small_all[:, 1].reshape(-1, small.shape[1])
            pair += [links.shift(small_a, "x"), links.shift(small_b, "y")]
        pair = list(tie(*pair))
        if i < links.size["z"] - 2:
            small_parts.append(pair[1])
        if i == 0:
            w_shared_in, _ = tie(w_shared_in, pair[0])
        if i == links.size["z"] - 3:
            pair[0], *hidden_parts = tie(pair[0], *hidden_parts)
            hidden_row = joined_rows(hidden_parts)
        heads_parts.append(pair[0])
    small_a, small_b = joined_rows([small_a, pair[1]]), joined_rows([small_b, pair[2]])
    heads_w = joined_rows(heads_parts)
    heads_c = links.shift(heads_w, "c")
    last_a, last_b = small_a[:, small_cols:], small_b[:, small_cols:]
    small_a, small_b = small_a[:, :small_cols], small_b[:, :small_cols]
    shared_pieces = jnp.concatenate(
        [
            w_shared_in[:, :SHARED_FF].reshape(rows_d, devices, half_sh),
            w_shared_in[:, SHARED_FF:].reshape(rows_d, devices, half_sh),
        ],
        axis=2,
    ).transpose(1, 0, 2)
    shared_w = lax.all_to_all(shared_pieces, BOTH, split_axis=0, concat_axis=0, tiled=True)
    far_a, far_b, shared_w = tie(links.shift(small_a, "y"), links.shift(small_b, "x"), shared_w)
    small_all = joined_rows([small_a, far_a, small_b, far_b])
    small_all = joined_rows([small_all, links.shift(small_all, "c")])
    heads_w = joined_rows([heads_w, heads_c]).reshape(devices, rows_d, q_cols + up_fold)
    blocks = devices // 2
    place_a = links.place_of(("z", "w", "x", "y", "c"))
    place_b = links.place_of(("z", "w", "y", "x", "c"))
    take_a = (place_a // blocks) * 2 * blocks + place_a % blocks
    take_b = (place_b // blocks) * 2 * blocks + blocks + place_b % blocks
    take = jnp.stack([take_a, take_b], axis=1).reshape(-1)
    small_all = small_all.reshape(2 * devices, rows_d // 2, small_cols)[take]
    small_all = small_all.reshape(devices, rows_d, small_cols)
    down_w = small_all[:, :, : LATENT + ROPE].reshape(D, LATENT + ROPE)
    gain_attn = small_all[:, :, LATENT + ROPE].reshape(D).astype(f32)
    gain_ffn = small_all[:, :, LATENT + ROPE + 1].reshape(D).astype(f32)
    gain_latent = small_all[:, :rows_l, LATENT + ROPE + 2].reshape(LATENT).astype(f32)

    heads_place = links.place_of(("x", "y", "w", "z", "c"))
    heads_w = heads_w[heads_place]
    query_w = heads_w[:, :, :q_cols].reshape(D, q_cols)
    up_w = heads_w[:, :, q_cols:].reshape(devices, up_parts, rows_l, up_fold)
    up_w = up_w.transpose(0, 2, 1, 3).reshape(LATENT, kv_cols)

    orders = (
        ("z", "w", "x", "y"),
        ("z", "w", "y", "x"),
        ("y", "z", "w", "x"),
        ("x", "z", "w", "y"),
    )
    slices = len(orders)
    count = tok // slices
    tokens = devices * tok
    source_list = [links.device_of(order + ("c",)) for order in orders]
    sources = jnp.concatenate(source_list).astype(jnp.int32)
    m_place = jnp.concatenate([d * slices + i for i, d in enumerate(source_list)])
    g_all = lax.all_gather(after(cotangent, far_a), BOTH, axis=0, tiled=True)
    g_blocks = g_all.reshape(devices, tok, D)

    inputs_row = hidden_row.astype(f32)
    inverse_row = rms_inverse(inputs_row)
    normed_row = (inputs_row * inverse_row * gain_attn).astype(bf16)
    rel_numbers = jnp.stack(rel_ctx)
    positions = rel_numbers.astype(jnp.int32)[:, None] * tok
    positions = (positions + jnp.arange(tok, dtype=jnp.int32)[None, :]).reshape(-1)
    row_segments = segments.reshape(ctx, tok)[rel_numbers].reshape(-1)
    allowed = (positions[None, :] <= positions[:, None]) & (
        row_segments[None, :] == row_segments[:, None]
    )
    cosine, sine_part = rope_tables(positions, ROPE)
    query_raw = matmul(normed_row, query_w).reshape(row, heads, NOPE + ROPE)
    query = jnp.concatenate(
        [
            query_raw[..., :NOPE],
            rotate(query_raw[..., NOPE:], cosine[:, None, :], sine_part[:, None, :]),
        ],
        axis=-1,
    ).astype(bf16)
    query = query.transpose(1, 0, 2)
    compressed = matmul(normed_row, down_w)
    raw_latent = compressed[:, :LATENT]
    inverse_latent = rms_inverse(raw_latent)
    latent = (raw_latent * inverse_latent * gain_latent).astype(bf16)
    key_rope = rotate(compressed[:, LATENT:], cosine, sine_part).astype(bf16)
    keyval = matmul(latent, up_w).astype(bf16).reshape(row, heads, NOPE + VDIM)
    last_a, last_b = tie(last_a, last_b, far_a)[:2]
    last_y, last_x, keyval = tie(links.shift(last_a, "y"), links.shift(last_b, "x"), keyval)
    out_w = joined_rows([last_a, last_y, last_b, last_x])
    out_w = joined_rows([out_w, links.shift(out_w, "c")])
    out_w = out_w.reshape(2 * devices, rows_d // 2, D)[take].reshape(D, D)
    keyval = keyval.transpose(1, 0, 2)
    key = jnp.concatenate(
        [keyval[..., :NOPE], jnp.broadcast_to(key_rope[None], (heads, row, ROPE))], axis=-1
    )
    value = keyval[..., NOPE:]

    def masked_scores():
        raw = jnp.einsum("hqd,hkd->hqk", query, key, preferred_element_type=f32)
        return jnp.where(allowed[None], raw * scale, -1e30)

    scores = masked_scores()
    row_max = jnp.max(scores, axis=-1, keepdims=True)
    exponent = jnp.exp(scores - row_max)
    row_total = jnp.sum(exponent, axis=-1, keepdims=True)
    log_total = row_max + jnp.log(row_total)
    probs = (exponent / row_total).astype(bf16)
    heads_part = jnp.einsum("hqk,hkd->qhd", probs, value, preferred_element_type=f32)
    heads_part = heads_part.astype(bf16).reshape(ctx, tok, v_cols)
    returned = jnp.stack(links.ctx_exchange([heads_part[k] for k in range(ctx)]))
    heads_out = returned[ctx_place].transpose(1, 0, 2).reshape(tok, HEADS * VDIM)
    inputs = hidden_in.astype(f32)
    middle = inputs + matmul(heads_out, out_w)
    inverse_ffn = rms_inverse(middle)
    ffn_in = (middle * inverse_ffn * gain_ffn).astype(bf16)

    cut = [ffn_in[i * count : (i + 1) * count] for i in range(slices)]

    def halved(parts):
        both = [jnp.split(part, 2) for part in parts]
        return [joined_rows([pair[i] for pair in both]) for i in range(2)]

    held = joined_rows(cut[:2])
    heads_half = [heads_out[: tok // 2], heads_out[tok // 2 :]]
    near_y, near_x, first, shared_w, w_expert_in, routes, gates = tie(
        links.shift(cut[2], "y"),
        links.shift(cut[3], "x"),
        links.shift(held, "z"),
        shared_w,
        w_expert_in,
        routes,
        gates,
    )
    experts = devices // 2
    expert_number = jnp.arange(experts, dtype=jnp.int32)[:, None, None]
    gate_matrix = jnp.sum(
        jnp.where(routes.T[None] == expert_number, gates.T[None], 0.0), axis=1
    )
    m_all = lax.all_to_all(
        jnp.repeat(gate_matrix, 2, axis=0), BOTH, split_axis=0, concat_axis=0, tiled=True
    )
    shared_w = shared_w.reshape(D, 2 * half_sh)
    pad = half_all - half_ff - half_sh
    w_in = jnp.concatenate(
        [
            w_expert_in[0][:, :half_ff],
            jnp.pad(shared_w[:, :half_sh], ((0, 0), (0, pad))),
            w_expert_in[0][:, half_ff:],
            jnp.pad(shared_w[:, half_sh:], ((0, 0), (0, pad))),
        ],
        axis=1,
    )
    w_back = jnp.concatenate(
        [w_expert_out[0], jnp.pad(w_shared_out, ((0, pad), (0, 0)))], axis=0
    )
    m = m_all.reshape(devices * slices, count)[m_place].reshape(tokens, 1)
    ring_a = [held, first]
    heads_far = [links.shift(heads_half[0], "x"), links.shift(heads_half[1], "y")]
    while len(ring_a) < links.size["z"]:
        step, *heads_far = tie(links.shift(ring_a[-1], "z"), *heads_far)
        if len(ring_a) == 2:
            heads_half = [joined_rows(p) for p in zip(heads_half, heads_far)]
            heads_far = [links.shift(heads_half[0], "y"), links.shift(heads_half[1], "x")]
        ring_a.append(step)
    held = links.gather(joined_rows(ring_a), ("w",)) if links.size["w"] > 1 else None
    slice_0, slice_1 = halved(jnp.split(held, ctx // 4 * links.size["z"]) if held is not None else ring_a)
    held = joined_rows([cut[2], near_y, cut[3], near_x])
    held, slice_0, slice_1, w_in, w_back, m = tie(held, slice_0, slice_1, w_in, w_back, m)
    ring_b = [held]
    moved_0, moved_1, step = tie(
        links.shift(slice_0, "x"), links.shift(slice_1, "y"), links.shift(held, "z")
    )
    ring_b.append(step)
    near_a = [joined_rows([slice_0, moved_0]), joined_rows([slice_1, moved_1])]
    far_a = [links.shift(near_a[0], "y"), links.shift(near_a[1], "x")]
    near_a_rows = joined_rows(near_a)
    near_a_sib = links.shift(near_a_rows, "c")

    lean = devices > 32
    kept = None
    done, moved = {}, {}

    def ffn(rows, name, side):
        kept_now, parts = ffn_chunk(
            rows,
            g_blocks,
            m,
            w_in,
            w_back,
            half_ff,
            sources,
            "ab".index(name[0]),
            ("n", "f", "").index(name[1:]),
            side,
            None if lean else kept,
            moved.get(name) if side == 0 else None,
            lean,
        )
        if side == 1:
            moved[name] = links.shift(parts[0], "c", -1)
        done[name, side] = parts
        if lean:
            sums = [
                matmul_left_t(kept_now[0], kept_now[3]),
                matmul_left_t(kept_now[2], kept_now[1]),
            ]
            return sums if kept is None else [a + b for a, b in zip(kept, sums)]
        return kept_now

    near_a_sib, step = tie(near_a_sib, links.shift(ring_b[-1], "z"))
    ring_b.append(step)
    step = links.shift(ring_b[-1], "z")
    kept = ffn(near_a_sib, "an", 1)
    step, *far_a = tie(step, *far_a, done["an", 1][0])[:3]
    far_a_rows = joined_rows(far_a)
    far_a_sib = links.shift(far_a_rows, "c")
    ring_b.append(step)
    far_a_sib, ring_b[-1] = tie(far_a_sib, ring_b[-1])
    while len(ring_b) < links.size["z"]:
        ring_b.append(links.shift(ring_b[-1], "z"))
    held = links.gather(joined_rows(ring_b), ("w",)) if links.size["w"] > 1 else None
    near_b = halved(jnp.split(held, ctx // 4 * links.size["z"]) if held is not None else ring_b)
    far_b = [links.shift(near_b[0], "x"), links.shift(near_b[1], "y")]
    kept = ffn(far_a_sib, "af", 1)
    kept = ffn(far_a_rows, "af", 0)
    near_a_rows, *far_b = tie(near_a_rows, *far_b, done["af", 0][0])[:3]
    rows_b = joined_rows([*near_b, *far_b])
    sib_b = links.shift(rows_b, "c")

    def add_far(moved_rows, near):
        return [plus(m_rows, n_rows) for m_rows, n_rows in zip(moved_rows, near)]

    def split_far(rows):
        pairs = [jnp.split(r, 2) for r in rows]
        return [p[0] for p in pairs], [p[1] for p in pairs]

    def z_parts(rows):
        if links.size["w"] > 1:
            rows = [links.scatter_sum(r, ("w",)) for r in rows]
        return [joined_rows(p) for p in zip(*[jnp.split(r, links.size["z"]) for r in rows])]

    def last_b(total):
        n0, f0, n1, f1 = jnp.split(total, 4)
        return plus(links.shift(f0, "y", -1), n0), plus(links.shift(f1, "x", -1), n1)

    far = done["af", 0][1::2]
    a_far = [links.shift(far[0], "y", -1), links.shift(far[1], "x", -1)]
    kept = ffn(near_a_rows, "an", 0)
    a_far = tie(*a_far, done["an", 0][0])[:2]
    a_near = add_far(a_far, done["an", 0][1::2])
    sib_b, *a_near = tie(sib_b, *a_near)
    a_near, far = split_far(a_near)
    a_far = [links.shift(far[0], "x", -1), links.shift(far[1], "y", -1)]
    query_w_all = lax.all_gather(after(w_query, sib_b), BOTH, axis=0, tiled=True)
    kept = ffn(sib_b, "b", 1)
    kept = ffn(rows_b, "b", 0)
    a_far = tie(*a_far, done["b", 0][0])[:2]
    a_parts = z_parts(add_far(a_far, a_near))
    a_sum = links.shift(a_parts[-1], "z", -1)
    done["bn", 0], done["bf", 0] = done["b", 0][:4], done["b", 0][4:]
    far = done["bf", 0][1::2]
    b_far = [links.shift(far[0], "x", -1), links.shift(far[1], "y", -1)]
    out_far = [done["af", 0][0], done["af", 0][2]]
    out_far_b = [done["bf", 0][0], done["bf", 0][2]]

    def send_outputs(far_rows, far_rows_b):
        near_rows, far_rows = split_far(add_far(far_rows, [done["an", 0][0], done["an", 0][2]]))
        return near_rows, [
            links.shift(joined_rows(pair), axis, -1)
            for pair, axis in zip(zip(far_rows, far_rows_b), "xy")
        ]

    if lean:
        grad_w_in, grad_w_back = kept
        a_sum = plus(a_sum, a_parts[-2])
        for part in a_parts[-3::-1]:
            a_sum = plus(links.shift(a_sum, "z", -1), part)
        out_far = [links.shift(p, axis, -1) for p, axis in zip(out_far, "yx")]
        out_near, out_sent = send_outputs(out_far, out_far_b)
        b_parts = z_parts(add_far(b_far, done["bn", 0][1::2]))
        b_sum = b_parts[-1]
        for part in b_parts[-2:0:-1]:
            b_sum = plus(links.shift(b_sum, "z", -1), part)
    else:
        x_all, g_kept, act_all, grad_pre_all = kept
        grad_w_top = matmul_left_t(x_all[:, : D // 2], grad_pre_all)
        *b_far, a_sum, _ = tie(*b_far, a_sum, grad_w_top)
        b_parts = z_parts(add_far(b_far, done["bn", 0][1::2]))
        a_sum = plus(a_sum, a_parts[-2])
        x_all, a_sum, out_far[0], out_far[1], *b_parts = tie(x_all, a_sum, *out_far, *b_parts)
        out_far = [links.shift(p, axis, -1) for p, axis in zip(out_far, "yx")]
        a_next = links.shift(a_sum, "z", -1)
        b_next = links.shift(b_parts[-1], "z", -1)
        grad_w_end = matmul_left_t(x_all[:, D // 2 :], grad_pre_all)
        a_next, b_next, _ = tie(a_next, b_next, grad_w_end)
        a_sum = plus(a_next, a_parts[-3])
        b_sum = plus(b_next, b_parts[-2])
        act_all, a_sum, b_sum, *out_all = tie(act_all, a_sum, b_sum, *out_far, *out_far_b)
        out_near, out_sent = send_outputs(out_all[:2], out_all[2:])
        b_next = links.shift(b_sum, "z", -1)
        a_next = links.shift(a_sum, "z", -1)
        grad_w_back = matmul_left_t(act_all, g_kept)
        a_next, b_next, _ = tie(a_next, b_next, grad_w_back)
        a_sum = plus(a_next, a_parts[-4])
        b_sum = plus(b_next, b_parts[-3])
        for part in b_parts[-4:0:-1]:
            b_sum = plus(links.shift(b_sum, "z", -1), part)
        grad_w_top, grad_w_end, grad_w_back, b_sum = tie(
            grad_w_top, grad_w_end, grad_w_back, b_sum
        )
    b_sum = plus(links.shift(b_sum, "z", -1), b_parts[0])
    grad_ffn = joined_rows([a_sum, *last_b(b_sum)])
    out_sent[0], out_sent[1], grad_ffn = tie(*out_sent, grad_ffn)
    out_split = out_near[0].shape[0]
    out_far = [p[:out_split] for p in out_sent]
    out_near_b = add_far(
        [p[out_split:] for p in out_sent], [done["bn", 0][0], done["bn", 0][2]]
    )
    grad_ffn = grad_ffn.astype(f32)

    def output_steps():
        parts = [
            joined_rows(p)
            for p in zip(z_parts(add_far(out_far, out_near)), z_parts(out_near_b))
        ]
        total = parts[-1]
        for part in parts[-2::-1]:
            moved_total = links.shift(total, "z", -1)
            yield [moved_total]
            total = plus(moved_total, part)
        rows = total.shape[0] // 3
        yield [joined_rows([total[:rows], *last_b(total[rows:])])]

    out_steps = output_steps()
    out_now = next(out_steps)
    def pick(value, start, count):
        return jnp.concatenate(
            [value[:, start : start + count], value[:, half_all + start : half_all + start + count]],
            axis=1,
        )

    blocks_in = [grad_w_in] if lean else [grad_w_top, grad_w_end]
    grad_w_expert_in = joined_rows([pick(v, 0, half_ff) for v in blocks_in])
    grad_w_expert_out = grad_w_back[:half_ff]
    grad_w_shared_out = grad_w_back[half_ff : half_ff + half_sh]
    grad_shared = joined_rows([pick(v, half_ff, half_sh) for v in blocks_in])
    grad_shared = grad_shared.reshape(devices, rows_d, 2 * half_sh)
    def owner_steps(value, direct):
        count, size = value.shape[1], links.size["z"]
        value = value.reshape(size, 2, ctx * count, -1)

        def core(c):
            return lax.dynamic_index_in_dim(value, c, 1, keepdims=False)

        moved_core = links.shift(core(links.own["c"] ^ 1), "c")
        (moved_core,) = yield [moved_core]
        total = plus(moved_core, core(links.own["c"]))
        parts = [
            lax.dynamic_index_in_dim(total, links.minus("z", jnp.uint32(k)), 0, keepdims=False)
            for k in range(size)
        ]
        if direct:
            back = [links.shift(parts[k], "z", -k) for k in range(1, size)]
            back = yield back
            summed = sum([p.astype(f32) for p in back], parts[0].astype(f32)).astype(bf16)
        else:
            summed = parts[-1]
            for part in parts[-2::-1]:
                moved_sum = links.shift(summed, "z", -1)
                (moved_sum,) = yield [moved_sum]
                summed = plus(moved_sum, part)
        summed = summed.reshape(ctx, count, -1)
        pieces = [
            lax.dynamic_index_in_dim(summed, rel_ctx[k], 0, keepdims=False) for k in range(ctx)
        ]
        pieces = links.ctx_exchange(pieces)
        received = yield pieces[1:]
        yield jnp.stack([pieces[0], *received])[ctx_place].astype(f32)

    grad_out = cotangent.astype(f32)
    grad_middle_part, grad_norm_ffn = rms_backward(middle, inverse_ffn, gain_ffn, grad_ffn)
    grad_middle = grad_out + grad_middle_part
    grad_attended = grad_middle.astype(bf16)
    grad_heads_all = matmul_right_t(grad_attended, out_w).astype(bf16)
    pieces = [
        jnp.concatenate(
            [columns(grad_heads_all, k, v_cols), columns(grad_attended, k, D // ctx)], axis=1
        )
        for k in range(ctx)
    ]
    arrived = jnp.concatenate(links.ctx_exchange(pieces), axis=0)
    arrived, grad_shared, *out_now = tie(arrived, grad_shared, *out_now)
    grad_shared = lax.all_to_all(grad_shared, BOTH, split_axis=0, concat_axis=0, tiled=True)
    grad_shared = grad_shared.transpose(1, 0, 2)
    grad_w_shared_in = jnp.concatenate(
        [
            grad_shared[:, :, :half_sh].reshape(rows_d, SHARED_FF),
            grad_shared[:, :, half_sh:].reshape(rows_d, SHARED_FF),
        ],
        axis=1,
    )
    out_now = next(out_steps)
    grad_heads = arrived[:, :v_cols].reshape(row, heads, VDIM).transpose(1, 0, 2)
    grad_attended_cols = arrived[:, v_cols:]
    quarter = tok // 2
    parts = [heads_half[0][:quarter], heads_half[1][:quarter]]
    parts += [heads_half[0][quarter:], heads_far[1][:quarter]]
    parts += [heads_far[0][:quarter], heads_half[1][quarter:]]
    parts += [heads_far[0][quarter:], heads_far[1][quarter:]]
    heads_out_row = joined_rows(parts)
    if links.size["w"] > 1:
        heads_out_row = links.gather(heads_out_row, ("w",))

    soft = jnp.exp(masked_scores() - log_total)
    grad_values = jnp.einsum(
        "hqk,hqd->hkd", soft.astype(bf16), grad_heads, preferred_element_type=f32
    )
    grad_probs = jnp.einsum("hqd,hkd->hqk", grad_heads, value, preferred_element_type=f32)
    row_delta = jnp.sum(soft * grad_probs, axis=-1, keepdims=True)
    grad_raw = (soft * (grad_probs - row_delta) * scale).astype(bf16)
    grad_raw, grad_values, *out_now = tie(grad_raw, grad_values, *out_now)
    out_now = next(out_steps)
    grad_query = jnp.einsum("hqk,hkd->qhd", grad_raw, key, preferred_element_type=f32)
    grad_key = jnp.einsum("hqk,hqd->khd", grad_raw, query, preferred_element_type=f32)
    grad_key_rope = jnp.sum(grad_key[..., NOPE:], axis=1)
    grad_keyval = jnp.concatenate(
        [grad_key[..., :NOPE], grad_values.transpose(1, 0, 2)], axis=-1
    )
    grad_keyval = grad_keyval.astype(bf16).reshape(row, kv_cols)
    grad_w_up = matmul_left_t(latent, grad_keyval)
    grad_latent = matmul_right_t(grad_keyval, up_w)
    grad_low = jnp.concatenate([grad_latent, grad_key_rope], axis=1).astype(bf16)
    grad_query_raw = jnp.concatenate(
        [
            grad_query[..., :NOPE],
            unrotate(grad_query[..., NOPE:], cosine[:, None, :], sine_part[:, None, :]),
        ],
        axis=-1,
    )
    grad_query_raw = grad_query_raw.astype(bf16).reshape(ctx, tok, q_cols)
    query_back = links.ctx_exchange([grad_query_raw[k] for k in range(ctx)])
    grad_low, *query_back = tie(grad_low, *query_back)
    query_back = jnp.stack(query_back)
    grad_out_cols = matmul_left_t(heads_out_row, grad_attended_cols)
    grad_w_q = matmul_left_t(normed_row, grad_query_raw.reshape(row, q_cols))
    grad_w_up = grad_w_up.astype(bf16).reshape(devices, rows_l, up_parts, up_fold)
    grad_w_up = grad_w_up.transpose(0, 2, 1, 3).reshape(devices, rows_d, up_fold)
    heads_owned = owner_steps(
        jnp.concatenate(
            [
                grad_w_q.astype(bf16).reshape(devices, rows_d, q_cols),
                grad_w_up,
                grad_out_cols.astype(bf16).reshape(devices, rows_d, D // ctx),
            ],
            axis=2,
        ),
        False,
    )
    heads_moved = next(heads_owned)
    low_parts = links.ctx_exchange(list(grad_low.reshape(ctx, tok, -1)))
    *low_parts, out_now[0], heads_moved[0] = tie(*low_parts, *out_now, *heads_moved)
    heads_moved = heads_owned.send(heads_moved)
    grad_low = sum(p.astype(f32) for p in low_parts)
    mixed = (middle + list(out_steps)[-1][0].astype(f32)).astype(bf16)
    query_back = query_back[ctx_place].transpose(1, 0, 2).reshape(tok, ctx * q_cols)
    grad_compressed_latent, grad_norm_latent = rms_backward(
        raw_latent[:tok], inverse_latent[:tok], gain_latent, grad_low[:, :LATENT]
    )
    grad_compressed = jnp.concatenate(
        [
            grad_compressed_latent,
            unrotate(grad_low[:, LATENT:], cosine[:tok], sine_part[:tok]),
        ],
        axis=1,
    ).astype(bf16)
    grad_normed = matmul_right_t(grad_compressed, down_w) + matmul_right_t(
        query_back, query_w_all
    )
    grad_normed, heads_moved[0] = tie(grad_normed, *heads_moved)
    heads_moved = heads_owned.send(heads_moved)
    grad_input_part, grad_norm_attn = rms_backward(
        inputs, inverse_row[:tok], gain_attn, grad_normed
    )
    grad_in = grad_middle + grad_input_part

    def joined(value):
        return value.transpose(1, 0, 2).reshape(value.shape[1], -1)

    compressed_cols = jnp.concatenate(
        links.ctx_exchange([columns(grad_compressed, k, dn_cols) for k in range(ctx)]), axis=0
    )
    grad_w_down = matmul_left_t(normed_row, compressed_cols).astype(bf16)
    vectors = jnp.stack(
        [
            jnp.pad(v.reshape(devices, -1), ((0, 0), (0, dn_cols - v.size // devices)))
            for v in (grad_norm_attn, grad_norm_ffn, grad_norm_latent)
        ],
        axis=1,
    )
    vectors = jnp.pad(vectors, ((0, 0), (0, 13), (0, 0))).astype(bf16)
    last_owned = owner_steps(
        jnp.concatenate([grad_w_down.reshape(devices, rows_d, dn_cols), vectors], axis=1), True
    )
    last_moved = next(last_owned)
    last_moved[0], heads_moved[0] = tie(*last_moved, *heads_moved)
    heads_moved = heads_owned.send(heads_moved)
    last_moved = last_owned.send(last_moved)

    def finish(steps, received):
        for received in iter(lambda: steps.send(received), None):
            if not isinstance(received, list):
                return received

    heads_grads = finish(heads_owned, heads_moved)
    last_grads = finish(last_owned, last_moved)
    grad_w_query = joined(heads_grads[:, :, :q_cols])
    grad_w_out = joined(heads_grads[:, :, q_cols + up_fold :])
    grad_w_kv_up = heads_grads[:, :, q_cols : q_cols + up_fold]
    grad_w_kv_up = grad_w_kv_up.reshape(ctx, up_parts, rows_l, up_fold)
    grad_w_kv_up = grad_w_kv_up.transpose(2, 0, 1, 3).reshape(rows_l, ctx * kv_cols)
    grad_w_kv_down = joined(last_grads[:, :rows_d])
    vector_sums = jnp.sum(last_grads[:, rows_d : rows_d + 3], axis=0)
    return (
        mixed,
        grad_in,
        vector_sums[0, :rows_d],
        grad_w_query,
        grad_w_kv_down,
        vector_sums[2, :rows_l],
        grad_w_kv_up,
        grad_w_out,
        vector_sums[1, :rows_d],
        grad_w_shared_in,
        grad_w_shared_out,
        grad_w_expert_in[None],
        grad_w_expert_out[None],
    )


def solution(mesh):
    rows = P(BOTH, None)
    vector = P(BOTH)
    experts = P(BOTH, None, None)
    return jax.shard_map(
        shards,
        mesh=mesh,
        in_specs=(
            rows,
            P("dp"),
            rows,
            rows,
            rows,
            vector,
            rows,
            rows,
            vector,
            rows,
            rows,
            vector,
            rows,
            rows,
            experts,
            experts,
        ),
        out_specs=(
            rows,
            rows,
            vector,
            rows,
            rows,
            vector,
            rows,
            rows,
            vector,
            rows,
            rows,
            experts,
            experts,
        ),
        check_vma=False,
    )
```
